32 devices in a mesh: copies: 2 (over x), rollout: 2 (over core), tensor: 8 (over z, y).
Axes of the slice: x: 2, y: 2, z: 4, core: 2. Of those that a mesh axis runs over, the one named last changes fastest.
Arguments:
- owners: int32 [4, 3], P('copies'), parts along dimension 0, may hold values from 0 to 1
- base_query: bfloat16 [4, 5120, 5120], P('copies', 'tensor'), parts along dimension 0, may hold values from -6 to 6
- base_key: bfloat16 [4, 1024, 5120], P('copies', 'tensor'), parts along dimension 0, may hold values from -6 to 6
- base_value: bfloat16 [4, 1024, 5120], P('copies', 'tensor'), parts along dimension 0, may hold values from -6 to 6
- left_shared_matrix: bfloat16 [2, 4, 3, 64, 5120], P('rollout', 'copies', None, None, 'tensor'), parts along dimension 1, may hold values from -6 to 6
- right_queries_matrix: bfloat16 [2, 4, 5120, 64], P('rollout', 'copies', 'tensor'), parts along dimension 1, may hold values from -6 to 6
- right_keys_matrix: bfloat16 [2, 4, 1024, 64], P('rollout', 'copies', 'tensor'), parts along dimension 1, may hold values from -6 to 6
- right_values_matrix: bfloat16 [2, 4, 1024, 64], P('rollout', 'copies', 'tensor'), parts along dimension 1, may hold values from -6 to 6
Outputs:
- merged_query: bfloat16 [4, 5120, 5120], P('copies', 'tensor'), parts along dimension 0
- merged_key: bfloat16 [4, 1024, 5120], P('copies', 'tensor'), parts along dimension 0
- merged_value: bfloat16 [4, 1024, 5120], P('copies', 'tensor'), parts along dimension 0
The draws below stay inside these ranges and needn't reach their ends.
There are 2 independent parts, one for each index of `copies`. The reference program is written for one: setup_inputs(seed, part) draws one part's arguments, and reference() takes and returns one part's arrays. A program takes and returns all parts, laid end to end along the dimension named above; each array names one. Nothing has to cross between parts.
All inputs are finite; a program needn't handle non-finite values.
Results may differ from the reference program's by a relative error of at most 0.001.
Values may be sent and summed in bfloat16 or wider, within the bound.
No kernel may reach another device: no remote copies, remote signals or barrier semaphores. Data moves between devices by JAX's collectives and lax.ppermute only.
A program may use at most 128 MiB of HBM per device.

```python
import jax
import jax.numpy as jnp

HIDDEN_WIDTH = 5120
QUESTION_DIMS = 5120
KEYVAL_HEADDIMS = 1024
INNER_DIMENSION = 64
BLOCK_TOTAL = 2
ATTN_MAPS = 3
SAMPLER_TEAMS = 2


def place_ends(array, key, smallest, high):
    place = [jax.random.randint(jax.random.fold_in(key, axis), (), 0, length) for axis, length in enumerate(array.shape)]
    main_axis = array.shape.index(max(array.shape))
    neighbour = place[:main_axis] + [(place[main_axis] + 1) % array.shape[main_axis]] + place[main_axis + 1:]
    return array.at[tuple(place)].set(smallest).at[tuple(neighbour)].set(high)


def block_levels(key, dims, shards, least, high):
    loudness = 1.0
    for axis_at, blocks in shards:
        steps = jax.random.uniform(jax.random.fold_in(jax.random.fold_in(key, 6), axis_at), (blocks,), jnp.float32, least / len(shards), high / len(shards))
        loudness = loudness * jnp.repeat(jnp.exp(steps), dims[axis_at] // blocks).reshape((-1,) + (1,) * (len(dims) - 1 - axis_at))
    return loudness


def gaussian(stream_key, shape, scale, most, pieces=(), held_as=jnp.bfloat16):
    entries = jax.random.normal(stream_key, shape, jnp.float32) * scale
    if len(pieces) > 0:
        entries = block_levels(stream_key, shape, pieces, -0.22, 0.18) * entries
    return jnp.clip(entries, min=-most, max=most).astype(held_as)


def setup_inputs(seed: int = 0, part: int = 0) -> dict:
    splits = jax.random.split(jax.random.key(seed), 9)
    part_keys = jax.random.split(jax.random.fold_in(splits[8], part), 9)
    owners = place_ends(jax.random.randint(part_keys[0], (BLOCK_TOTAL, ATTN_MAPS), 0, SAMPLER_TEAMS), jax.random.fold_in(part_keys[0], 1), 0, SAMPLER_TEAMS - 1).astype(jnp.int32)
    base_query = gaussian(part_keys[1], (BLOCK_TOTAL, QUESTION_DIMS, HIDDEN_WIDTH), 1.0, 6.0, ((1, 8),))
    base_key = gaussian(part_keys[2], (BLOCK_TOTAL, KEYVAL_HEADDIMS, HIDDEN_WIDTH), 1.0, 6.0, ((1, 8),))
    base_value = gaussian(part_keys[3], (BLOCK_TOTAL, KEYVAL_HEADDIMS, HIDDEN_WIDTH), 1.0, 6.0, ((1, 8),))
    left_shared_matrix = gaussian(part_keys[4], (SAMPLER_TEAMS, BLOCK_TOTAL, ATTN_MAPS, INNER_DIMENSION, HIDDEN_WIDTH), 1.0, 6.0, ((0, 2), (4, 8)))
    right_queries_matrix = gaussian(part_keys[5], (SAMPLER_TEAMS, BLOCK_TOTAL, QUESTION_DIMS, INNER_DIMENSION), 1.0, 6.0, ((0, 2), (2, 8)))
    right_keys_matrix = gaussian(part_keys[6], (SAMPLER_TEAMS, BLOCK_TOTAL, KEYVAL_HEADDIMS, INNER_DIMENSION), 1.0, 6.0, ((0, 2), (2, 8)))
    right_values_matrix = gaussian(part_keys[7], (SAMPLER_TEAMS, BLOCK_TOTAL, KEYVAL_HEADDIMS, INNER_DIMENSION), 1.0, 6.0, ((0, 2), (2, 8)))
    return {"owners": owners, "base_query": base_query, "base_key": base_key, "base_value": base_value, "left_shared_matrix": left_shared_matrix, "right_queries_matrix": right_queries_matrix, "right_keys_matrix": right_keys_matrix, "right_values_matrix": right_values_matrix}


numerator_gain = 16.0


def reference(owners, base_query, base_key, base_value, left_shared_matrix, right_queries_matrix, right_keys_matrix, right_values_matrix):
    update_multiplier = numerator_gain / INNER_DIMENSION
    bases = (base_query, base_key, base_value)
    outside = (right_queries_matrix, right_keys_matrix, right_values_matrix)
    merged_outputs = []
    for proj in range(ATTN_MAPS):
        layers_out = []
        for layer in range(BLOCK_TOTAL):
            owner = owners[layer, proj]
            inside = left_shared_matrix[owner, layer, proj]
            rows_b = outside[proj][owner, layer]
            delta = jnp.dot(rows_b, inside, preferred_element_type=jnp.float32)
            merged = bases[proj][layer].astype(jnp.float32) + update_multiplier * delta
            layers_out.append(merged.astype(jnp.bfloat16))
        merged_outputs.append(jnp.stack(layers_out, axis=0))
    return (merged_outputs[0], merged_outputs[1], merged_outputs[2])
```

```python
import functools

import jax
import jax.numpy as jnp
from jax import lax
from jax.experimental import pallas as pl
from jax.experimental.pallas import tpu as pltpu
from jax.sharding import PartitionSpec as P

numerator_gain = 16.0
LANES = 128


def ring_order(n):
    return list(range(0, n, 2)) + list(range(n - 1, 0, -2))


def ring_perm(n):
    order = ring_order(n)
    pairs = []
    for k in range(n):
        pairs.append((order[k], order[(k + 1) % n]))
        pairs.append((n + order[k], n + order[(k - 1) % n]))
    return pairs


def ring_pass(array, n):
    return lax.ppermute(array, ("rollout", "tensor"), ring_perm(n))


def swap_cores(array):
    return lax.ppermute(array, "rollout", [(0, 1), (1, 0)])


def chunk_places(n, core, tensor):
    position = jnp.where(tensor % 2 == 0, tensor // 2, n - 1 - tensor // 2)
    slot = jnp.arange(n, dtype=jnp.int32)
    step = (slot + 1) // 2
    backward = (slot + core) % 2 == 1
    k = jnp.where(slot == 0, position, position + jnp.where(backward, -step, step))
    k = (k + n) % n
    return jnp.where(k < n // 2, 2 * k, 2 * n - 1 - 2 * k).astype(jnp.int32)


def merge_kernel(pieces, scale, cols, n_a, fresh, places, *refs):
    b_refs = refs[:3]
    a_refs = refs[3 : 3 + n_a]
    bases = refs[3 + n_a : 6 + n_a]
    at = 6 + n_a + (0 if fresh else 3)
    outs = refs[at : at + 3]
    buf, load_sem, store_sem = refs[at + 3 : at + 6]
    core = places[places.shape[0] - 1]
    tasks = []
    for slot, a_index, a_layer, layer in pieces:
        out_layer = layer if isinstance(layer, int) else layer[0] + (1 - 2 * layer[0]) * core
        columns = pl.ds(pl.multiple_of(places[slot] * cols, LANES), cols)
        for proj in range(3):
            rows = bases[proj].shape[1]
            for row in range(0, rows, min(rows, LANES)):
                tasks.append((proj, out_layer, row, min(rows, LANES), columns, a_index, a_layer))

    def load(j):
        proj, layer, row, size, columns, _, _ = tasks[j]
        return pltpu.make_async_copy(
            bases[proj].at[layer, pl.ds(row, size), columns], buf.at[j, pl.ds(0, size)], load_sem.at[j]
        )

    def store(j):
        proj, layer, row, size, columns, _, _ = tasks[j]
        return pltpu.make_async_copy(
            buf.at[j, pl.ds(0, size)], outs[proj].at[layer, pl.ds(row, size), columns], store_sem.at[j]
        )

    for j in range(len(tasks)):
        load(j).start()
    for j in range(len(tasks)):
        proj, layer, row, size, _, a_index, a_layer = tasks[j]
        load(j).wait()
        delta = lax.dot_general(
            b_refs[proj][layer, :, row : row + size],
            a_refs[a_index][a_layer, proj],
            (((0,), (0,)), ((), ())),
            preferred_element_type=jnp.float32,
        )
        merged = buf[j, :size].astype(jnp.float32) + scale * delta
        buf[j, :size] = merged.astype(jnp.bfloat16)
        store(j).start()
    for j in range(len(tasks)):
        store(j).wait()


def merge(places, b, a_list, bases, outs, pieces, scale, cols):
    fresh = outs is None
    n_a = len(a_list)
    tasks = len(pieces) * sum(-(-base.shape[1] // LANES) for base in bases)
    vmem = pl.BlockSpec(memory_space=pltpu.VMEM)
    hbm = pl.BlockSpec(memory_space=pl.ANY)
    operands = [places, *b, *a_list, *bases] + ([] if fresh else list(outs))
    rows = sum(base.shape[1] for base in bases)
    rank = a_list[0].shape[2]
    return pl.pallas_call(
        functools.partial(merge_kernel, pieces, scale, cols, n_a, fresh),
        in_specs=[pl.BlockSpec(memory_space=pltpu.SMEM)] + [vmem] * (3 + n_a) + [hbm] * (3 if fresh else 6),
        out_specs=[hbm] * 3,
        out_shape=[jax.ShapeDtypeStruct(base.shape, base.dtype) for base in bases],
        scratch_shapes=[
            pltpu.VMEM((tasks, min(LANES, max(base.shape[1] for base in bases)), cols), jnp.bfloat16),
            pltpu.SemaphoreType.DMA((tasks,)),
            pltpu.SemaphoreType.DMA((tasks,)),
        ],
        input_output_aliases={} if fresh else {7 + n_a + i: i for i in range(3)},
        compiler_params=pltpu.CompilerParams(vmem_limit_bytes=16 * 1024 * 1024),
        cost_estimate=pl.CostEstimate(
            flops=2 * len(pieces) * rows * cols * rank,
            bytes_accessed=4 * len(pieces) * rows * cols,
            transcendentals=0,
        ),
    )(*operands)


def per_device(
    n,
    owners,
    base_query,
    base_key,
    base_value,
    left_shared_matrix,
    right_queries_matrix,
    right_keys_matrix,
    right_values_matrix,
):
    layers, projs, rank, cols = left_shared_matrix.shape[1:]
    scale = numerator_gain / rank
    bases = (base_query, base_key, base_value)
    core = lax.axis_index("rollout")
    tensor = lax.axis_index("tensor")
    mine = owners == core

    own_a = left_shared_matrix[0]
    a = jnp.where(mine[:, :, None, None], own_a, swap_cores(own_a))
    b = []
    for proj, right in enumerate((right_queries_matrix, right_keys_matrix, right_values_matrix)):
        own_b = jnp.swapaxes(right[0], 1, 2)
        b.append(jnp.where(mine[:, proj, None, None], own_b, swap_cores(own_b)))

    half = layers // 2
    arrived = [(a,)]
    held = a
    for step in range(1, n // 2):
        held = ring_pass(held, n)
        arrived.append((held, swap_cores(held)))
    last = lax.dynamic_slice_in_dim(held, core * half, half, 0)
    last = ring_pass(last, n)
    arrived.append((last, swap_cores(last)))

    places = jnp.concatenate([chunk_places(n, core, tensor), core[None].astype(jnp.int32)])

    if cols % LANES == 0 and half == 1:
        outs = None
        for step, chunks in enumerate(arrived):
            if step == 0:
                pieces = [(0, 0, layer, layer) for layer in range(layers)]
            elif step < n // 2:
                pieces = [(2 * step - 1 + i, i, layer, layer) for i in range(2) for layer in range(layers)]
            else:
                pieces = [(n - 1, 0, 0, (0,)), (n - 1, 1, 0, (1,))]
            outs = merge(places, b, chunks, bases, outs, pieces, scale, cols)
        return tuple(outs)

    full = jnp.zeros((layers, projs, rank, n * cols), own_a.dtype)
    for step, chunks in enumerate(arrived[:-1]):
        for i, chunk in enumerate(chunks):
            start = places[max(0, 2 * step - 1) + i] * cols
            full = lax.dynamic_update_slice(full, chunk, (0, 0, 0, start))
    for i, chunk in enumerate(arrived[-1]):
        layer = half * jnp.where(core == i, 0, 1)
        full = lax.dynamic_update_slice(full, chunk, (layer, 0, 0, places[n - 1] * cols))
    merged = []
    for proj in range(projs):
        delta = jnp.einsum("lkr,lkc->lrc", b[proj], full[:, proj], preferred_element_type=jnp.float32)
        merged.append((bases[proj].astype(jnp.float32) + scale * delta).astype(jnp.bfloat16))
    return tuple(merged)


def solution(mesh):
    return jax.shard_map(
        functools.partial(per_device, mesh.shape["tensor"]),
        mesh=mesh,
        in_specs=(
            P("copies", None),
            P("copies", "tensor", None),
            P("copies", "tensor", None),
            P("copies", "tensor", None),
            P("rollout", "copies", None, None, "tensor"),
            P("rollout", "copies", "tensor", None),
            P("rollout", "copies", "tensor", None),
            P("rollout", "copies", "tensor", None),
        ),
        out_specs=(
            P("copies", "tensor", None),
            P("copies", "tensor", None),
            P("copies", "tensor", None),
        ),
        check_vma=False,
    )
```

```python
import functools

import jax
import jax.numpy as jnp
from jax import lax
from jax.experimental import pallas as pl
from jax.experimental.pallas import tpu as pltpu
from jax.sharding import PartitionSpec as P

numerator_gain = 16.0
LANES = 128


def ring_order(n):
    return list(range(0, n, 2)) + list(range(n - 1, 0, -2))


def ring_pass(array, n):
    order = ring_order(n)
    pairs = []
    for k in range(n):
        pairs.append((order[k], order[(k + 1) % n]))
        pairs.append((n + order[k], n + order[(k - 1) % n]))
    return lax.ppermute(array, ("rollout", "tensor"), pairs)


def swap_cores(array):
    return lax.ppermute(array, "rollout", [(0, 1), (1, 0)])


def chunk_places(n, core, tensor):
    position = jnp.where(tensor % 2 == 0, tensor // 2, n - 1 - tensor // 2)
    slot = jnp.arange(n, dtype=jnp.int32)
    step = (slot + 1) // 2
    backward = (slot + core) % 2 == 1
    k = jnp.where(slot == 0, position, position + jnp.where(backward, -step, step))
    k = (k + n) % n
    return jnp.where(k < n // 2, 2 * k, 2 * n - 1 - 2 * k).astype(jnp.int32)


def start_chosen(mine, own, other, target, sem):
    copy = pltpu.make_async_copy(own, target, sem)
    pl.when(mine)(copy.start)
    pl.when(jnp.logical_not(mine))(pltpu.make_async_copy(other, target, sem).start)
    return copy


def choose_a_kernel(n, places, own, other, first, second, sems):
    core = places[n]
    projs = own.shape[1]
    copies = []
    for i, (out, layer) in enumerate(((first, core), (second, 1 - core))):
        for proj in range(projs):
            mine = places[n + 1 + layer * 3 + proj] == core
            target = out.at[proj]
            copies.append(
                start_chosen(mine, own.at[layer, proj], other.at[layer, proj], target, sems.at[i * projs + proj])
            )
    for copy in copies:
        copy.wait()


def choose_a(places, n, own, other):
    smem = pl.BlockSpec(memory_space=pltpu.SMEM)
    vmem = pl.BlockSpec(memory_space=pltpu.VMEM)
    anywhere = pl.BlockSpec(memory_space=pl.ANY)
    piece = jax.ShapeDtypeStruct(own.shape[1:], own.dtype)
    return pl.pallas_call(
        functools.partial(choose_a_kernel, n),
        in_specs=[smem, anywhere, anywhere],
        out_specs=[vmem, vmem],
        out_shape=[piece, piece],
        scratch_shapes=[pltpu.SemaphoreType.DMA((own.shape[0] * own.shape[1],))],
    )(places, pltpu.with_memory_space_constraint(own, pltpu.HBM), other)


def choose_b_kernel(n, places, *refs):
    core = places[n]
    sems = refs[12]
    copies = []
    for proj in range(3):
        own, other, held = refs[proj], refs[3 + proj], refs[9 + proj]
        for layer in range(own.shape[0]):
            mine = places[n + 1 + layer * 3 + proj] == core
            copies.append(
                start_chosen(mine, own.at[layer], other.at[layer], held.at[layer], sems.at[layer * 3 + proj])
            )
    for proj in range(3):
        out, held = refs[6 + proj], refs[9 + proj]
        for layer in range(held.shape[0]):
            copies.pop(0).wait()
            out[layer] = held[layer].T


def choose_b(places, n, own, other):
    smem = pl.BlockSpec(memory_space=pltpu.SMEM)
    vmem = pl.BlockSpec(memory_space=pltpu.VMEM)
    anywhere = pl.BlockSpec(memory_space=pl.ANY)
    shapes = [jax.ShapeDtypeStruct((x.shape[0], x.shape[2], x.shape[1]), x.dtype) for x in own]
    return pl.pallas_call(
        functools.partial(choose_b_kernel, n),
        in_specs=[smem] + [anywhere] * 6,
        out_specs=[vmem] * 3,
        out_shape=shapes,
        scratch_shapes=[pltpu.VMEM(x.shape, x.dtype) for x in own] + [pltpu.SemaphoreType.DMA((3 * own[0].shape[0],))],
    )(places, *[pltpu.with_memory_space_constraint(x, pltpu.HBM) for x in own], *other)


def merge_kernel(n, pieces, scale, cols, n_a, fresh, places, *refs):
    b_refs = refs[:3]
    a_refs = refs[3 : 3 + n_a]
    bases = refs[3 + n_a : 6 + n_a]
    at = 6 + n_a + (0 if fresh else 3)
    outs = refs[at : at + 3]
    bufs = refs[at + 3 : at + 6]
    load_sem, store_sem = refs[at + 6 : at + 8]
    core = places[n]
    tasks = []
    for i, (slot, a_index, own) in enumerate(pieces):
        layer = core if own else 1 - core
        columns = pl.ds(pl.multiple_of(places[slot] * cols, LANES), cols)
        for proj in range(3):
            tasks.append((i, proj, layer, columns, a_index))

    def load(j):
        i, proj, layer, columns, _ = tasks[j]
        return pltpu.make_async_copy(bases[proj].at[layer, :, columns], bufs[proj].at[i], load_sem.at[j])

    def store(j):
        i, proj, layer, columns, _ = tasks[j]
        return pltpu.make_async_copy(bufs[proj].at[i], outs[proj].at[layer, :, columns], store_sem.at[j])

    for j in range(len(tasks)):
        load(j).start()
    for j in range(len(tasks)):
        i, proj, layer, _, a_index = tasks[j]
        load(j).wait()
        delta = jnp.dot(b_refs[proj][layer], a_refs[a_index][proj], preferred_element_type=jnp.float32)
        merged = bufs[proj][i].astype(jnp.float32) + scale * delta
        bufs[proj][i] = merged.astype(jnp.bfloat16)
        store(j).start()
    for j in range(len(tasks)):
        store(j).wait()


def merge(n, places, b, a_list, bases, outs, pieces, scale, cols):
    fresh = outs is None
    n_a = len(a_list)
    tasks = 3 * len(pieces)
    vmem = pl.BlockSpec(memory_space=pltpu.VMEM)
    hbm = pl.BlockSpec(memory_space=pltpu.HBM)
    held = [pltpu.with_memory_space_constraint(base, pltpu.HBM) for base in bases]
    operands = [places, *b, *a_list, *held] + ([] if fresh else list(outs))
    rows = sum(base.shape[1] for base in bases)
    rank = a_list[0].shape[1]
    return pl.pallas_call(
        functools.partial(merge_kernel, n, pieces, scale, cols, n_a, fresh),
        in_specs=[pl.BlockSpec(memory_space=pltpu.SMEM)] + [vmem] * (3 + n_a) + [hbm] * (3 if fresh else 6),
        out_specs=[hbm] * 3,
        out_shape=[jax.ShapeDtypeStruct(base.shape, base.dtype) for base in bases],
        scratch_shapes=[pltpu.VMEM((len(pieces), base.shape[1], cols), base.dtype) for base in bases]
        + [pltpu.SemaphoreType.DMA((tasks,)), pltpu.SemaphoreType.DMA((tasks,))],
        input_output_aliases={} if fresh else {7 + n_a + i: i for i in range(3)},
        compiler_params=pltpu.CompilerParams(vmem_limit_bytes=16 * 1024 * 1024),
        cost_estimate=pl.CostEstimate(
            flops=2 * len(pieces) * rows * cols * rank,
            bytes_accessed=4 * len(pieces) * rows * cols,
            transcendentals=0,
        ),
    )(*operands)


def after(array, outs):
    array, outs = lax.optimization_barrier((array, outs))
    return array, outs


def per_device(
    n,
    owners,
    base_query,
    base_key,
    base_value,
    left_shared_matrix,
    right_queries_matrix,
    right_keys_matrix,
    right_values_matrix,
):
    layers, projs, rank, cols = left_shared_matrix.shape[1:]
    scale = numerator_gain / rank
    bases = (base_query, base_key, base_value)
    core = lax.axis_index("rollout")
    tensor = lax.axis_index("tensor")
    places = jnp.concatenate([chunk_places(n, core, tensor), core[None].astype(jnp.int32), owners.reshape(-1)])

    own_a = left_shared_matrix[0]
    first, second = choose_a(places, n, own_a, swap_cores(own_a))
    own_b = [jnp.swapaxes(right[0], 1, 2) for right in (right_queries_matrix, right_keys_matrix, right_values_matrix)]
    b = choose_b(places, n, own_b, [swap_cores(x) for x in own_b])

    if cols % LANES == 0:
        held = [first, second]
        last = n // 2
        ready = []
        first = ring_pass(first, n)
        second = ring_pass(second, n)
        first, b = lax.optimization_barrier((first, b))
        go = functools.partial(merge, n, places, b, bases=bases, scale=scale, cols=cols)
        outs = go(held, outs=None, pieces=[(0, 0, True), (0, 1, False)])
        for step in range(1, last + 1):
            slot = 2 * step - 1
            if step > 1:
                chunks, pieces = ready.pop(0)
                outs = go(chunks, outs=outs, pieces=pieces)
            ready.append(([first, swap_cores(first)], [(slot, 0, True), (min(slot + 1, n - 1), 1, False)]))
            if step < last:
                first = ring_pass(first, n)
                second, outs = after(second, outs)
                ready.append(([second, swap_cores(second)], [(slot, 0, False), (slot + 1, 1, True)]))
                chunks, pieces = ready.pop(0)
                outs = go(chunks, outs=outs, pieces=pieces)
                first, outs = after(first, outs)
                if step < last - 1:
                    second = ring_pass(second, n)
        for chunks, pieces in ready:
            outs = go(chunks, outs=outs, pieces=pieces)
        return tuple(outs)

    full = jnp.zeros((layers, projs, rank, n * cols), own_a.dtype)

    def put(full, piece, layer, slot):
        return lax.dynamic_update_slice(full, piece[None], (layer, 0, 0, places[slot] * cols))

    full = put(full, first, core, 0)
    full = put(full, second, 1 - core, 0)
    for step in range(1, n // 2 + 1):
        slot = 2 * step - 1
        first = ring_pass(first, n)
        full = put(full, first, core, slot)
        full = put(full, swap_cores(first), 1 - core, min(slot + 1, n - 1))
        if step < n // 2:
            second = ring_pass(second, n)
            full = put(full, second, 1 - core, slot)
            full = put(full, swap_cores(second), core, slot + 1)
    merged = []
    for proj in range(projs):
        delta = jnp.einsum("lrk,lkc->lrc", b[proj], full[:, proj], preferred_element_type=jnp.float32)
        merged.append((bases[proj].astype(jnp.float32) + scale * delta).astype(jnp.bfloat16))
    return tuple(merged)


def solution(mesh):
    return jax.shard_map(
        functools.partial(per_device, mesh.shape["tensor"]),
        mesh=mesh,
        in_specs=(
            P("copies", None),
            P("copies", "tensor", None),
            P("copies", "tensor", None),
            P("copies", "tensor", None),
            P("rollout", "copies", None, None, "tensor"),
            P("rollout", "copies", "tensor", None),
            P("rollout", "copies", "tensor", None),
            P("rollout", "copies", "tensor", None),
        ),
        out_specs=(
            P("copies", "tensor", None),
            P("copies", "tensor", None),
            P("copies", "tensor", None),
        ),
        check_vma=False,
    )
```

```python
import functools

import jax
import jax.numpy as jnp
from jax import lax
from jax.experimental import pallas as pl
from jax.experimental.pallas import tpu as pltpu
from jax.sharding import PartitionSpec as P

numerator_gain = 16.0
LANES = 128
MIB = 1024 * 1024
SMEM = pl.BlockSpec(memory_space=pltpu.SMEM)
VMEM = pl.BlockSpec(memory_space=pltpu.VMEM)
HBM = pl.BlockSpec(memory_space=pltpu.HBM)
ANY = pl.BlockSpec(memory_space=pl.ANY)


def in_hbm(array):
    return pltpu.with_memory_space_constraint(array, pltpu.HBM)


def ring_order(n):
    return list(range(0, n, 2)) + list(range(n - 1, 0, -2))


def ring_pass(array, n):
    order = ring_order(n)
    pairs = []
    for k in range(n):
        pairs.append((order[k], order[(k + 1) % n]))
        pairs.append((n + order[k], n + order[(k - 1) % n]))
    return lax.ppermute(array, ("rollout", "tensor"), pairs)


def swap_cores(array):
    return lax.ppermute(array, "rollout", [(0, 1), (1, 0)])


def place_of(n, step, from_core, tensor):
    position = jnp.where(tensor % 2 == 0, tensor // 2, n - 1 - tensor // 2)
    k = position + jnp.where(from_core == 0, -step, step)
    k = jnp.where(k < 0, k + n, jnp.where(k >= n, k - n, k))
    return jnp.where(k < n // 2, 2 * k, 2 * n - 1 - 2 * k)


def base_copies(n, pieces, bases, targets, sems):
    core = lax.axis_index("rollout")
    tensor = lax.axis_index("tensor")
    cols = targets[0].shape[2]
    copies = []
    for i, (step, own_ring, own_layer) in enumerate(pieces):
        layer = core if own_layer else 1 - core
        place = place_of(n, step, core if own_ring else 1 - core, tensor)
        columns = pl.ds(pl.multiple_of(place * cols, LANES), cols)
        for proj in range(3):
            block = bases[proj].at[layer, :, columns]
            copies.append((block, targets[proj].at[i], sems.at[3 * i + proj]))
    return copies


def start_loads(n, pieces, bases, targets, sems):
    loads = [pltpu.make_async_copy(*copy) for copy in base_copies(n, pieces, bases, targets, sems)]
    for load in loads:
        load.start()
    return loads


def start_chosen(mine, own, other, target, sem):
    copy = pltpu.make_async_copy(own, target, sem)
    pl.when(mine)(copy.start)
    pl.when(jnp.logical_not(mine))(pltpu.make_async_copy(other, target, sem).start)
    return copy


def choose_a_kernel(owners, own, other, first, second, sems):
    core = lax.axis_index("rollout")
    projs = own.shape[1]
    copies = []
    for i, (out, layer) in enumerate(((first, core), (second, 1 - core))):
        for proj in range(projs):
            mine = owners[layer, proj] == core
            copies.append(
                start_chosen(
                    mine, own.at[layer, proj], other.at[layer, proj], out.at[proj], sems.at[i * projs + proj]
                )
            )
    for copy in copies:
        copy.wait()


def choose_a(owners, own, other):
    piece = jax.ShapeDtypeStruct(own.shape[1:], own.dtype)
    return pl.pallas_call(
        choose_a_kernel,
        in_specs=[SMEM, ANY, ANY],
        out_specs=[VMEM, VMEM],
        out_shape=[piece, piece],
        scratch_shapes=[pltpu.SemaphoreType.DMA((own.shape[0] * own.shape[1],))],
        compiler_params=pltpu.CompilerParams(vmem_limit_bytes=4 * MIB),
    )(owners, in_hbm(own), other)


def choose_b_kernel(n, pieces, owners, *refs):
    core = lax.axis_index("rollout")
    own, other, bases = refs[0:3], refs[3:6], refs[6:9]
    outs, nexts, held = refs[9:12], refs[12:15], refs[15:18]
    sems, load_sems = refs[18:20]
    copies = []
    for proj in range(3):
        for layer in range(own[proj].shape[0]):
            mine = owners[layer, proj] == core
            copies.append(
                start_chosen(
                    mine,
                    own[proj].at[layer],
                    other[proj].at[layer],
                    held[proj].at[layer],
                    sems.at[layer * 3 + proj],
                )
            )
    loads = start_loads(n, pieces, bases, nexts, load_sems)
    for proj in range(3):
        for layer in range(held[proj].shape[0]):
            copies.pop(0).wait()
            outs[proj][layer] = held[proj][layer].T
    for load in loads:
        load.wait()


def block_shapes(bases, pieces, cols):
    return [jax.ShapeDtypeStruct((len(pieces), base.shape[1], cols), base.dtype) for base in bases]


def choose_b(n, cols, owners, own, other, bases, pieces):
    shapes = [jax.ShapeDtypeStruct((x.shape[0], x.shape[2], x.shape[1]), x.dtype) for x in own]
    out = pl.pallas_call(
        functools.partial(choose_b_kernel, n, pieces),
        in_specs=[SMEM] + [ANY] * 6 + [HBM] * 3,
        out_specs=[VMEM] * 6,
        out_shape=shapes + block_shapes(bases, pieces, cols),
        scratch_shapes=[pltpu.VMEM(x.shape, x.dtype) for x in own]
        + [pltpu.SemaphoreType.DMA((3 * own[0].shape[0],)), pltpu.SemaphoreType.DMA((3 * len(pieces),))],
        compiler_params=pltpu.CompilerParams(vmem_limit_bytes=16 * MIB),
    )(owners, *[in_hbm(x) for x in own], *other, *[in_hbm(x) for x in bases])
    return out[:3], out[3:]


def merge_kernel(n, pieces, next_pieces, scale, fresh, *refs):
    b_refs, a_refs, blocks, bases = refs[0:3], refs[3:5], refs[5:8], refs[8:11]
    at = 11 if fresh else 14
    outs, at = refs[at : at + 3], at + 3
    nexts, at = (refs[at : at + 3], at + 3) if next_pieces else (None, at)
    bufs, load_sems, store_sems = refs[at : at + 3], refs[at + 3], refs[at + 4]
    core = lax.axis_index("rollout")
    loads = start_loads(n, next_pieces, bases, nexts, load_sems) if next_pieces else []
    stores = [
        pltpu.make_async_copy(buf, out, sem) for out, buf, sem in base_copies(n, pieces, outs, bufs, store_sems)
    ]
    for i, (_, _, own_layer) in enumerate(pieces):
        layer = core if own_layer else 1 - core
        for proj in range(3):
            delta = jnp.dot(b_refs[proj][layer], a_refs[i][proj], preferred_element_type=jnp.float32)
            merged = blocks[proj][i].astype(jnp.float32) + scale * delta
            bufs[proj][i] = merged.astype(jnp.bfloat16)
            stores[3 * i + proj].start()
    for copy in loads + stores:
        copy.wait()


def merge(n, scale, cols, b, a_list, blocks, bases, outs, pieces, next_pieces):
    fresh = outs is None
    rows = sum(base.shape[1] for base in bases)
    nexts = block_shapes(bases, next_pieces, cols) if next_pieces else []
    out = pl.pallas_call(
        functools.partial(merge_kernel, n, pieces, next_pieces, scale, fresh),
        in_specs=[VMEM] * (3 + len(a_list) + 3) + [HBM] * (3 if fresh else 6),
        out_specs=[HBM] * 3 + [VMEM] * len(nexts),
        out_shape=[jax.ShapeDtypeStruct(base.shape, base.dtype) for base in bases] + nexts,
        scratch_shapes=[pltpu.VMEM(x.shape, x.dtype) for x in block_shapes(bases, pieces, cols)]
        + [pltpu.SemaphoreType.DMA((3 * len(pieces),)), pltpu.SemaphoreType.DMA((3 * len(pieces),))],
        input_output_aliases={} if fresh else {9 + len(a_list) + i: i for i in range(3)},
        compiler_params=pltpu.CompilerParams(vmem_limit_bytes=16 * MIB),
        cost_estimate=pl.CostEstimate(
            flops=2 * len(pieces) * rows * cols * a_list[0].shape[1],
            bytes_accessed=4 * len(pieces) * rows * cols,
            transcendentals=0,
        ),
    )(*b, *a_list, *blocks, *[in_hbm(base) for base in bases], *([] if fresh else outs))
    return out[:3], out[3:]


def per_device(
    n,
    owners,
    base_query,
    base_key,
    base_value,
    left_shared_matrix,
    right_queries_matrix,
    right_keys_matrix,
    right_values_matrix,
):
    layers, projs, rank, cols = left_shared_matrix.shape[1:]
    scale = numerator_gain / rank
    bases = (base_query, base_key, base_value)
    rights = (right_queries_matrix, right_keys_matrix, right_values_matrix)
    last = n // 2

    own_a = left_shared_matrix[0]
    own_b = [jnp.swapaxes(right[0], 1, 2) for right in rights]

    if cols % LANES == 0:
        plan = [[(0, True, True), (0, True, False)]]
        for step in range(1, last + 1):
            plan.append([(step, True, True), (step, False, False)])
            if step < last:
                plan.append([(step, True, False), (step, False, True)])
        plan.append(None)

        first, second = choose_a(owners, own_a, swap_cores(own_a))
        held = [first, second]
        first = ring_pass(first, n)
        second = ring_pass(second, n)
        b, blocks = choose_b(n, cols, owners, own_b, [swap_cores(x) for x in own_b], bases, plan[0])
        first, b = lax.optimization_barrier((first, b))
        done = 0
        outs = None

        def advance(chunks, blocks, outs, done):
            outs, blocks = merge(
                n, scale, cols, b, chunks, blocks, bases, outs, plan[done], plan[done + 1]
            )
            return blocks, outs, done + 1

        blocks, outs, done = advance(held, blocks, outs, done)
        ready = []
        for step in range(1, last + 1):
            if step > 1:
                blocks, outs, done = advance(ready.pop(0), blocks, outs, done)
            ready.append([first, swap_cores(first)])
            if step < last:
                first = ring_pass(first, n)
                second, outs = lax.optimization_barrier((second, outs))
                ready.append([second, swap_cores(second)])
                blocks, outs, done = advance(ready.pop(0), blocks, outs, done)
                first, outs = lax.optimization_barrier((first, outs))
                if step < last - 1:
                    second = ring_pass(second, n)
        for chunks in ready:
            blocks, outs, done = advance(chunks, blocks, outs, done)
        return tuple(outs)

    core = lax.axis_index("rollout")
    tensor = lax.axis_index("tensor")
    mine = owners == core
    a = jnp.where(mine[:, :, None, None], own_a, swap_cores(own_a))
    b = [jnp.where(mine[:, proj, None, None], x, swap_cores(x)) for proj, x in enumerate(own_b)]
    full = jnp.zeros((layers, projs, rank, n * cols), own_a.dtype)

    def put(full, piece, layer, step, from_core):
        start = place_of(n, step, from_core, tensor) * cols
        return lax.dynamic_update_slice(full, piece[None], (layer, 0, 0, start))

    first = jnp.where(core == 0, a[0], a[1])
    second = jnp.where(core == 0, a[1], a[0])
    full = put(full, first, core, 0, core)
    full = put(full, second, 1 - core, 0, core)
    for step in range(1, last + 1):
        first = ring_pass(first, n)
        full = put(full, first, core, step, core)
        full = put(full, swap_cores(first), 1 - core, step, 1 - core)
        if step < last:
            second = ring_pass(second, n)
            full = put(full, second, 1 - core, step, core)
            full = put(full, swap_cores(second), core, step, 1 - core)
    merged = []
    for proj in range(projs):
        delta = jnp.einsum("lkr,lkc->lrc", b[proj], full[:, proj], preferred_element_type=jnp.float32)
        merged.append((bases[proj].astype(jnp.float32) + scale * delta).astype(jnp.bfloat16))
    return tuple(merged)


def solution(mesh):
    return jax.shard_map(
        functools.partial(per_device, mesh.shape["tensor"]),
        mesh=mesh,
        in_specs=(
            P("copies", None),
            P("copies", "tensor", None),
            P("copies", "tensor", None),
            P("copies", "tensor", None),
            P("rollout", "copies", None, None, "tensor"),
            P("rollout", "copies", "tensor", None),
            P("rollout", "copies", "tensor", None),
            P("rollout", "copies", "tensor", None),
        ),
        out_specs=(
            P("copies", "tensor", None),
            P("copies", "tensor", None),
            P("copies", "tensor", None),
        ),
        check_vma=False,
    )
```

```python
import functools

import jax
import jax.numpy as jnp
from jax import lax
from jax.experimental import pallas as pl
from jax.experimental.pallas import tpu as pltpu
from jax.sharding import PartitionSpec as P

numerator_gain = 16.0
LANES = 128
MIB = 1024 * 1024
SMEM = pl.BlockSpec(memory_space=pltpu.SMEM)
VMEM = pl.BlockSpec(memory_space=pltpu.VMEM)
HBM = pl.BlockSpec(memory_space=pltpu.HBM)
ANY = pl.BlockSpec(memory_space=pl.ANY)


def in_hbm(array):
    return pltpu.with_memory_space_constraint(array, pltpu.HBM)


def in_vmem(array):
    return pltpu.with_memory_space_constraint(array, pltpu.VMEM)


def ring_order(n):
    return list(range(0, n, 2)) + list(range(n - 1, 0, -2))


def ring_pass(array, n):
    order = ring_order(n)
    pairs = []
    for k in range(n):
        pairs.append((order[k], order[(k + 1) % n]))
        pairs.append((n + order[k], n + order[(k - 1) % n]))
    return lax.ppermute(array, ("rollout", "tensor"), pairs)


def swap_cores(array):
    return lax.ppermute(array, "rollout", [(0, 1), (1, 0)])


def place_of(n, step, from_core, tensor):
    position = jnp.where(tensor % 2 == 0, tensor // 2, n - 1 - tensor // 2)
    k = position + jnp.where(from_core == 0, -step, step)
    k = jnp.where(k < 0, k + n, jnp.where(k >= n, k - n, k))
    return jnp.where(k < n // 2, 2 * k, 2 * n - 1 - 2 * k)


def column_blocks(n, pieces, cols):
    core = lax.axis_index("rollout")
    tensor = lax.axis_index("tensor")
    blocks = []
    for step, own_ring, own_layer in pieces:
        place = place_of(n, step, core if own_ring else 1 - core, tensor)
        blocks.append((core if own_layer else 1 - core, pl.ds(pl.multiple_of(place * cols, LANES), cols)))
    return blocks


def fetch_kernel(n, pieces, *refs):
    bases, blocks, sems = refs[0:3], refs[3:6], refs[6]
    loads = []
    for i, (layer, columns) in enumerate(column_blocks(n, pieces, blocks[0].shape[2])):
        for proj in range(3):
            load = pltpu.make_async_copy(bases[proj].at[layer, :, columns], blocks[proj].at[i], sems.at[3 * i + proj])
            load.start()
            loads.append(load)
    for load in loads:
        load.wait()


def fetch(n, cols, bases, pieces):
    shapes = [jax.ShapeDtypeStruct((len(pieces), base.shape[1], cols), base.dtype) for base in bases]
    return pl.pallas_call(
        functools.partial(fetch_kernel, n, pieces),
        in_specs=[HBM] * 3,
        out_specs=[VMEM] * 3,
        out_shape=shapes,
        scratch_shapes=[pltpu.SemaphoreType.DMA((3 * len(pieces),))],
        compiler_params=pltpu.CompilerParams(vmem_limit_bytes=4 * MIB),
        cost_estimate=pl.CostEstimate(
            flops=0, bytes_accessed=2 * sum(x.size * x.dtype.itemsize for x in shapes), transcendentals=0
        ),
    )(*[in_hbm(base) for base in bases])


def choose_a_kernel(owners, own, other, first, second):
    core = lax.axis_index("rollout")
    for out, layer in ((first, core), (second, 1 - core)):
        for proj in range(own.shape[1]):
            mine = owners[layer, proj] == core
            out[proj] = jnp.where(mine, own[layer, proj], other[layer, proj])


def choose_a(owners, own, other):
    piece = jax.ShapeDtypeStruct(own.shape[1:], own.dtype)
    return pl.pallas_call(
        choose_a_kernel,
        in_specs=[SMEM, VMEM, VMEM],
        out_specs=[VMEM, VMEM],
        out_shape=[piece, piece],
        compiler_params=pltpu.CompilerParams(vmem_limit_bytes=4 * MIB),
    )(in_hbm(owners), in_vmem(own), other)


def choose_b_kernel(owners, *refs):
    core = lax.axis_index("rollout")
    for proj in range(3):
        own, other, out = refs[proj], refs[3 + proj], refs[6 + proj]
        for layer in range(own.shape[0]):
            mine = owners[layer, proj] == core
            out[layer] = jnp.where(mine, own[layer], other[layer]).T


def choose_b(owners, own, other):
    return pl.pallas_call(
        choose_b_kernel,
        in_specs=[SMEM] + [VMEM] * 6,
        out_specs=[VMEM] * 3,
        out_shape=[jax.ShapeDtypeStruct((x.shape[0], x.shape[2], x.shape[1]), x.dtype) for x in own],
        compiler_params=pltpu.CompilerParams(vmem_limit_bytes=4 * MIB),
    )(in_hbm(owners), *[in_vmem(x) for x in own], *other)


def merge_kernel(n, pieces, scale, fresh, *refs):
    b_refs, a_refs, bases = refs[0:3], refs[3:5], refs[5:8]
    at = 8 if fresh else 11
    outs, bufs, sems = refs[at : at + 3], refs[at + 3 : at + 6], refs[at + 6]
    cols = a_refs[0].shape[2]
    stores = []
    for i, (layer, columns) in enumerate(column_blocks(n, pieces, cols)):
        for proj in range(3):
            delta = jnp.dot(b_refs[proj][layer], a_refs[i][proj], preferred_element_type=jnp.float32)
            block = bases[proj][i] if fresh else bases[proj][layer, :, columns]
            merged = block.astype(jnp.float32) + scale * delta
            bufs[proj][i] = merged.astype(jnp.bfloat16)
            store = pltpu.make_async_copy(bufs[proj].at[i], outs[proj].at[layer, :, columns], sems.at[3 * i + proj])
            store.start()
            stores.append(store)
    for store in stores:
        store.wait()


def merge(n, scale, b, a_list, bases, shapes, outs, pieces):
    fresh = outs is None
    rank, cols = a_list[0].shape[1:]
    rows = sum(base.shape[1] for base in bases)
    return pl.pallas_call(
        functools.partial(merge_kernel, n, pieces, scale, fresh),
        in_specs=[VMEM] * (3 + len(a_list) + 3) + [HBM] * (0 if fresh else 3),
        out_specs=[HBM] * 3,
        out_shape=shapes,
        scratch_shapes=[pltpu.VMEM((len(pieces), base.shape[1], cols), base.dtype) for base in bases]
        + [pltpu.SemaphoreType.DMA((3 * len(pieces),))],
        input_output_aliases={} if fresh else {6 + len(a_list) + i: i for i in range(3)},
        compiler_params=pltpu.CompilerParams(vmem_limit_bytes=16 * MIB),
        cost_estimate=pl.CostEstimate(
            flops=2 * len(pieces) * rows * cols * rank,
            bytes_accessed=4 * len(pieces) * rows * cols,
            transcendentals=0,
        ),
    )(*b, *a_list, *(bases if fresh else [in_vmem(base) for base in bases]), *([] if fresh else outs))


def per_device(
    n,
    owners,
    base_query,
    base_key,
    base_value,
    left_shared_matrix,
    right_queries_matrix,
    right_keys_matrix,
    right_values_matrix,
):
    layers, projs, rank, cols = left_shared_matrix.shape[1:]
    scale = numerator_gain / rank
    bases = (base_query, base_key, base_value)
    rights = (right_queries_matrix, right_keys_matrix, right_values_matrix)
    last = n // 2

    own_a = left_shared_matrix[0]
    own_b = [jnp.swapaxes(right[0], 1, 2) for right in rights]

    if cols % LANES == 0:
        own_pieces = [(0, True, True), (0, True, False)]
        blocks = fetch(n, cols, bases, own_pieces)
        other_a, blocks = lax.optimization_barrier((swap_cores(own_a), blocks))
        first, second = choose_a(owners, own_a, other_a)
        held = [first, second]
        first = ring_pass(first, n)
        second = ring_pass(second, n)
        b = choose_b(owners, own_b, [swap_cores(x) for x in own_b])
        first, b = lax.optimization_barrier((first, b))

        def go(chunks, pieces, outs=None):
            return merge(n, scale, b, chunks, bases if outs else blocks, shapes, outs, pieces)

        shapes = [jax.ShapeDtypeStruct(base.shape, base.dtype) for base in bases]
        outs = go(held, own_pieces)
        ready = []
        for step in range(1, last + 1):
            if step > 1:
                outs = go(*ready.pop(0), outs)
            ready.append(([first, swap_cores(first)], [(step, True, True), (step, False, False)]))
            if step < last:
                first = ring_pass(first, n)
                second, outs = lax.optimization_barrier((second, outs))
                ready.append(([second, swap_cores(second)], [(step, True, False), (step, False, True)]))
                outs = go(*ready.pop(0), outs)
                first, outs = lax.optimization_barrier((first, outs))
                if step < last - 1:
                    second = ring_pass(second, n)
        for item in ready:
            outs = go(*item, outs)
        return tuple(outs)

    core = lax.axis_index("rollout")
    tensor = lax.axis_index("tensor")
    mine = owners == core
    a = jnp.where(mine[:, :, None, None], own_a, swap_cores(own_a))
    b = [jnp.where(mine[:, proj, None, None], x, swap_cores(x)) for proj, x in enumerate(own_b)]
    full = jnp.zeros((layers, projs, rank, n * cols), own_a.dtype)

    def put(full, piece, layer, step, from_core):
        start = place_of(n, step, from_core, tensor) * cols
        return lax.dynamic_update_slice(full, piece[None], (layer, 0, 0, start))

    first = jnp.where(core == 0, a[0], a[1])
    second = jnp.where(core == 0, a[1], a[0])
    full = put(full, first, core, 0, core)
    full = put(full, second, 1 - core, 0, core)
    for step in range(1, last + 1):
        first = ring_pass(first, n)
        full = put(full, first, core, step, core)
        full = put(full, swap_cores(first), 1 - core, step, 1 - core)
        if step < last:
            second = ring_pass(second, n)
            full = put(full, second, 1 - core, step, core)
            full = put(full, swap_cores(second), core, step, 1 - core)
    merged = []
    for proj in range(projs):
        delta = jnp.einsum("lkr,lkc->lrc", b[proj], full[:, proj], preferred_element_type=jnp.float32)
        merged.append((bases[proj].astype(jnp.float32) + scale * delta).astype(jnp.bfloat16))
    return tuple(merged)


def solution(mesh):
    return jax.shard_map(
        functools.partial(per_device, mesh.shape["tensor"]),
        mesh=mesh,
        in_specs=(
            P("copies", None),
            P("copies", "tensor", None),
            P("copies", "tensor", None),
            P("copies", "tensor", None),
            P("rollout", "copies", None, None, "tensor"),
            P("rollout", "copies", "tensor", None),
            P("rollout", "copies", "tensor", None),
            P("rollout", "copies", "tensor", None),
        ),
        out_specs=(
            P("copies", "tensor", None),
            P("copies", "tensor", None),
            P("copies", "tensor", None),
        ),
        check_vma=False,
    )
```

```python
import functools

import jax
import jax.numpy as jnp
from jax import lax
from jax.experimental import pallas as pl
from jax.experimental.pallas import tpu as pltpu
from jax.sharding import PartitionSpec as P

numerator_gain = 16.0
LANES = 128
MIB = 1024 * 1024
TILE_ROWS = 128
TILE_COLS = 256
SMEM = pl.BlockSpec(memory_space=pltpu.SMEM)
VMEM = pl.BlockSpec(memory_space=pltpu.VMEM)
HBM = pl.BlockSpec(memory_space=pltpu.HBM)
ANY = pl.BlockSpec(memory_space=pl.ANY)


def in_hbm(array):
    return pltpu.with_memory_space_constraint(array, pltpu.HBM)


def in_vmem(array):
    return pltpu.with_memory_space_constraint(array, pltpu.VMEM)


def ring_order(n):
    return list(range(0, n, 2)) + list(range(n - 1, 0, -2))


def ring_pass(array, n):
    order = ring_order(n)
    pairs = []
    for k in range(n):
        pairs.append((order[k], order[(k + 1) % n]))
        pairs.append((n + order[k], n + order[(k - 1) % n]))
    return lax.ppermute(array, ("rollout", "tensor"), pairs)


def swap_cores(array):
    return lax.ppermute(array, "rollout", [(0, 1), (1, 0)])


def place_of(n, step, from_core, tensor):
    position = jnp.where(tensor % 2 == 0, tensor // 2, n - 1 - tensor // 2)
    k = position + jnp.where(from_core == 0, -step, step)
    k = jnp.where(k < 0, k + n, jnp.where(k >= n, k - n, k))
    return jnp.where(k < n // 2, 2 * k, 2 * n - 1 - 2 * k)


def column_starts(n, pieces, cols):
    core = lax.axis_index("rollout")
    tensor = lax.axis_index("tensor")
    blocks = []
    for step, own_ring, own_layer in pieces:
        place = place_of(n, step, core if own_ring else 1 - core, tensor)
        blocks.append((core if own_layer else 1 - core, pl.multiple_of(place * cols, LANES)))
    return blocks


def fetch_kernel(n, pieces, *refs):
    bases, blocks, sems = refs[0:3], refs[3:6], refs[6]
    loads = []
    cols = blocks[0].shape[2]
    for i, (layer, start) in enumerate(column_starts(n, pieces, cols)):
        columns = pl.ds(start, cols)
        for proj in range(3):
            load = pltpu.make_async_copy(bases[proj].at[layer, :, columns], blocks[proj].at[i], sems.at[3 * i + proj])
            load.start()
            loads.append(load)
    for load in loads:
        load.wait()


def fetch(n, cols, bases, pieces):
    shapes = [jax.ShapeDtypeStruct((len(pieces), base.shape[1], cols), base.dtype) for base in bases]
    return pl.pallas_call(
        functools.partial(fetch_kernel, n, pieces),
        in_specs=[HBM] * 3,
        out_specs=[VMEM] * 3,
        out_shape=shapes,
        scratch_shapes=[pltpu.SemaphoreType.DMA((3 * len(pieces),))],
        compiler_params=pltpu.CompilerParams(vmem_limit_bytes=4 * MIB),
        cost_estimate=pl.CostEstimate(
            flops=0, bytes_accessed=2 * sum(x.size * x.dtype.itemsize for x in shapes), transcendentals=0
        ),
    )(*[in_hbm(base) for base in bases])


def choose_a_kernel(owners, own, other, first, second):
    core = lax.axis_index("rollout")
    for out, layer in ((first, core), (second, 1 - core)):
        for proj in range(own.shape[1]):
            mine = owners[layer, proj] == core
            out[proj] = jnp.where(mine, own[layer, proj], other[layer, proj])


def choose_a(owners, own, other):
    piece = jax.ShapeDtypeStruct(own.shape[1:], own.dtype)
    return pl.pallas_call(
        choose_a_kernel,
        in_specs=[SMEM, VMEM, VMEM],
        out_specs=[VMEM, VMEM],
        out_shape=[piece, piece],
        compiler_params=pltpu.CompilerParams(vmem_limit_bytes=4 * MIB),
    )(in_hbm(owners), in_vmem(own), other)


def choose_b_kernel(owners, *refs):
    core = lax.axis_index("rollout")
    for proj in range(3):
        own, other, out = refs[proj], refs[3 + proj], refs[6 + proj]
        for layer in range(own.shape[0]):
            mine = owners[layer, proj] == core
            out[layer] = jnp.where(mine, own[layer], other[layer]).T


def choose_b(owners, own, other):
    return pl.pallas_call(
        choose_b_kernel,
        in_specs=[SMEM] + [VMEM] * 6,
        out_specs=[VMEM] * 3,
        out_shape=[jax.ShapeDtypeStruct((x.shape[0], x.shape[2], x.shape[1]), x.dtype) for x in own],
        compiler_params=pltpu.CompilerParams(vmem_limit_bytes=4 * MIB),
    )(in_hbm(owners), *[in_vmem(x) for x in own], *other)


def merge_kernel(n, pieces, scale, fresh, *refs):
    b_refs, a_refs, bases = refs[0:3], refs[3:5], refs[5:8]
    at = 8 if fresh else 11
    outs, bufs, sems = refs[at : at + 3], refs[at + 3 : at + 6], refs[at + 6]
    cols = a_refs[0].shape[2]
    stores = []
    for i, (layer, start) in enumerate(column_starts(n, pieces, cols)):
        columns = pl.ds(start, cols)
        for proj in range(3):
            for col in range(0, cols, TILE_COLS):
                width = min(TILE_COLS, cols - col)
                tile = pl.ds(col, width) if fresh else pl.ds(pl.multiple_of(start + col, LANES), width)
                for row in range(0, bufs[proj].shape[1], TILE_ROWS):
                    rows = pl.ds(row, min(TILE_ROWS, bufs[proj].shape[1] - row))
                    delta = jnp.dot(
                        b_refs[proj][layer, rows],
                        a_refs[i][proj, :, col : col + width],
                        preferred_element_type=jnp.float32,
                    )
                    block = bases[proj][i if fresh else layer, rows, tile]
                    merged = block.astype(jnp.float32) + scale * delta
                    bufs[proj][i, rows, col : col + width] = merged.astype(jnp.bfloat16)
            store = pltpu.make_async_copy(bufs[proj].at[i], outs[proj].at[layer, :, columns], sems.at[3 * i + proj])
            store.start()
            stores.append(store)
    for store in stores:
        store.wait()


def merge(n, scale, b, a_list, bases, shapes, outs, pieces):
    fresh = outs is None
    rank, cols = a_list[0].shape[1:]
    rows = sum(base.shape[1] for base in bases)
    return pl.pallas_call(
        functools.partial(merge_kernel, n, pieces, scale, fresh),
        in_specs=[VMEM] * (3 + len(a_list) + 3) + [HBM] * (0 if fresh else 3),
        out_specs=[HBM] * 3,
        out_shape=shapes,
        scratch_shapes=[pltpu.VMEM((len(pieces), base.shape[1], cols), base.dtype) for base in bases]
        + [pltpu.SemaphoreType.DMA((3 * len(pieces),))],
        input_output_aliases={} if fresh else {6 + len(a_list) + i: i for i in range(3)},
        compiler_params=pltpu.CompilerParams(vmem_limit_bytes=16 * MIB),
        cost_estimate=pl.CostEstimate(
            flops=2 * len(pieces) * rows * cols * rank,
            bytes_accessed=4 * len(pieces) * rows * cols,
            transcendentals=0,
        ),
    )(*b, *a_list, *(bases if fresh else [in_vmem(base) for base in bases]), *([] if fresh else outs))


def per_device(
    n,
    owners,
    base_query,
    base_key,
    base_value,
    left_shared_matrix,
    right_queries_matrix,
    right_keys_matrix,
    right_values_matrix,
):
    layers, projs, rank, cols = left_shared_matrix.shape[1:]
    scale = numerator_gain / rank
    bases = (base_query, base_key, base_value)
    rights = (right_queries_matrix, right_keys_matrix, right_values_matrix)
    last = n // 2

    own_a = left_shared_matrix[0]
    own_b = [jnp.swapaxes(right[0], 1, 2) for right in rights]

    if cols % LANES == 0:
        own_pieces = [(0, True, True), (0, True, False)]
        blocks = fetch(n, cols, bases, own_pieces)
        swapped = (swap_cores(own_a), [swap_cores(x) for x in own_b])
        (other_a, other_b), blocks = lax.optimization_barrier((swapped, blocks))
        first, second = choose_a(owners, own_a, other_a)
        held = [first, second]
        first = ring_pass(first, n)
        second = ring_pass(second, n)
        b = choose_b(owners, own_b, other_b)

        def go(chunks, pieces, outs=None):
            return merge(n, scale, b, chunks, bases if outs else blocks, shapes, outs, pieces)

        shapes = [jax.ShapeDtypeStruct(base.shape, base.dtype) for base in bases]
        outs = go(held, own_pieces)
        first, outs = lax.optimization_barrier((first, outs))
        ready = []
        for step in range(1, last + 1):
            if step > 1:
                outs = go(*ready.pop(0), outs)
            ready.append(([first, swap_cores(first)], [(step, True, True), (step, False, False)]))
            if step < last:
                first = ring_pass(first, n)
                second, outs = lax.optimization_barrier((second, outs))
                ready.append(([second, swap_cores(second)], [(step, True, False), (step, False, True)]))
                outs = go(*ready.pop(0), outs)
                first, outs = lax.optimization_barrier((first, outs))
                if step < last - 1:
                    second = ring_pass(second, n)
        for item in ready:
            outs = go(*item, outs)
        return tuple(outs)

    core = lax.axis_index("rollout")
    tensor = lax.axis_index("tensor")
    mine = owners == core
    a = jnp.where(mine[:, :, None, None], own_a, swap_cores(own_a))
    b = [jnp.where(mine[:, proj, None, None], x, swap_cores(x)) for proj, x in enumerate(own_b)]
    full = jnp.zeros((layers, projs, rank, n * cols), own_a.dtype)

    def put(full, piece, layer, step, from_core):
        start = place_of(n, step, from_core, tensor) * cols
        return lax.dynamic_update_slice(full, piece[None], (layer, 0, 0, start))

    first = jnp.where(core == 0, a[0], a[1])
    second = jnp.where(core == 0, a[1], a[0])
    full = put(full, first, core, 0, core)
    full = put(full, second, 1 - core, 0, core)
    for step in range(1, last + 1):
        first = ring_pass(first, n)
        full = put(full, first, core, step, core)
        full = put(full, swap_cores(first), 1 - core, step, 1 - core)
        if step < last:
            second = ring_pass(second, n)
            full = put(full, second, 1 - core, step, core)
            full = put(full, swap_cores(second), core, step, 1 - core)
    merged = []
    for proj in range(projs):
        delta = jnp.einsum("lkr,lkc->lrc", b[proj], full[:, proj], preferred_element_type=jnp.float32)
        merged.append((bases[proj].astype(jnp.float32) + scale * delta).astype(jnp.bfloat16))
    return tuple(merged)


def solution(mesh):
    return jax.shard_map(
        functools.partial(per_device, mesh.shape["tensor"]),
        mesh=mesh,
        in_specs=(
            P("copies", None),
            P("copies", "tensor", None),
            P("copies", "tensor", None),
            P("copies", "tensor", None),
            P("rollout", "copies", None, None, "tensor"),
            P("rollout", "copies", "tensor", None),
            P("rollout", "copies", "tensor", None),
            P("rollout", "copies", "tensor", None),
        ),
        out_specs=(
            P("copies", "tensor", None),
            P("copies", "tensor", None),
            P("copies", "tensor", None),
        ),
        check_vma=False,
    )
```

```python
import functools

import jax
import jax.numpy as jnp
from jax import lax
from jax.experimental import pallas as pl
from jax.experimental.pallas import tpu as pltpu
from jax.sharding import PartitionSpec as P

numerator_gain = 16.0
LANES = 128
MIB = 1024 * 1024
TILE_ROWS = 128
TILE_COLS = 256
SMEM = pl.BlockSpec(memory_space=pltpu.SMEM)
VMEM = pl.BlockSpec(memory_space=pltpu.VMEM)
HBM = pl.BlockSpec(memory_space=pltpu.HBM)
ANY = pl.BlockSpec(memory_space=pl.ANY)


def in_hbm(array):
    return pltpu.with_memory_space_constraint(array, pltpu.HBM)


def in_vmem(array):
    return pltpu.with_memory_space_constraint(array, pltpu.VMEM)


def ring_order(n):
    return list(range(0, n, 2)) + list(range(n - 1, 0, -2))


def ring_pass(array, n):
    order = ring_order(n)
    pairs = []
    for k in range(n):
        pairs.append((order[k], order[(k + 1) % n]))
        pairs.append((n + order[k], n + order[(k - 1) % n]))
    return lax.ppermute(array, ("rollout", "tensor"), pairs)


def swap_cores(array):
    return lax.ppermute(array, "rollout", [(0, 1), (1, 0)])


def place_of(n, step, from_core, tensor):
    position = jnp.where(tensor % 2 == 0, tensor // 2, n - 1 - tensor // 2)
    k = position + jnp.where(from_core == 0, -step, step)
    k = jnp.where(k < 0, k + n, jnp.where(k >= n, k - n, k))
    return jnp.where(k < n // 2, 2 * k, 2 * n - 1 - 2 * k)


def column_starts(n, pieces, cols):
    core = lax.axis_index("rollout")
    tensor = lax.axis_index("tensor")
    blocks = []
    for step, own_ring, own_layer in pieces:
        place = place_of(n, step, core if own_ring else 1 - core, tensor)
        blocks.append((core if own_layer else 1 - core, pl.multiple_of(place * cols, LANES)))
    return blocks


def choose_a_kernel(owners, own, other, first, second):
    core = lax.axis_index("rollout")
    for out, layer in ((first, core), (second, 1 - core)):
        for proj in range(own.shape[1]):
            mine = owners[layer, proj] == core
            out[proj] = jnp.where(mine, own[layer, proj], other[layer, proj])


def choose_a(owners, own, other):
    piece = jax.ShapeDtypeStruct(own.shape[1:], own.dtype)
    return pl.pallas_call(
        choose_a_kernel,
        in_specs=[SMEM, VMEM, VMEM],
        out_specs=[VMEM, VMEM],
        out_shape=[piece, piece],
        compiler_params=pltpu.CompilerParams(vmem_limit_bytes=4 * MIB),
    )(in_hbm(owners), in_vmem(own), other)


def start_fetches(n, pieces, bases, blocks, sems):
    cols = blocks[0].shape[2]
    fetches = []
    for i, (layer, start) in enumerate(column_starts(n, pieces, cols)):
        for base, block in zip(bases, blocks):
            source = base.at[layer, :, pl.ds(start, cols)]
            fetches.append(pltpu.make_async_copy(source, block.at[i], sems.at[len(fetches)]))
            fetches[-1].start()
    return fetches


def block_shapes(bases, pieces, cols):
    return [jax.ShapeDtypeStruct((len(pieces), base.shape[1], cols), base.dtype) for base in bases]


def moved(shapes):
    size = sum(x.size * x.dtype.itemsize for x in shapes)
    return pl.CostEstimate(flops=0, bytes_accessed=2 * size, transcendentals=0)


def fetch_kernel(n, pieces, *refs):
    count = len(refs) // 2
    for fetch in start_fetches(n, pieces, refs[:count], refs[count:-1], refs[-1]):
        fetch.wait()


def fetch_blocks(n, cols, bases, pieces):
    blocks = block_shapes(bases, pieces, cols)
    return pl.pallas_call(
        functools.partial(fetch_kernel, n, pieces),
        in_specs=[HBM] * len(bases),
        out_specs=[VMEM] * len(bases),
        out_shape=blocks,
        scratch_shapes=[pltpu.SemaphoreType.DMA((len(bases) * len(pieces),))],
        compiler_params=pltpu.CompilerParams(vmem_limit_bytes=4 * MIB),
        cost_estimate=moved(blocks),
    )(*[in_hbm(base) for base in bases])


def choose_b_kernel(n, pieces, owners, *refs):
    core = lax.axis_index("rollout")
    own, other, base, outs, block, sems = refs[0:3], refs[3:6], refs[6], refs[7:10], refs[10], refs[11]
    fetches = start_fetches(n, pieces, [base], [block], sems)
    for proj in range(3):
        for layer in range(own[proj].shape[0]):
            mine = owners[layer, proj] == core
            outs[proj][layer] = jnp.where(mine, own[proj][layer], other[proj][layer]).T
    for fetch in fetches:
        fetch.wait()


def choose_b(n, cols, owners, own, other, base, pieces):
    chosen = [jax.ShapeDtypeStruct((x.shape[0], x.shape[2], x.shape[1]), x.dtype) for x in own]
    blocks = block_shapes([base], pieces, cols)
    out = pl.pallas_call(
        functools.partial(choose_b_kernel, n, pieces),
        in_specs=[SMEM] + [VMEM] * 6 + [HBM],
        out_specs=[VMEM] * 4,
        out_shape=chosen + blocks,
        scratch_shapes=[pltpu.SemaphoreType.DMA((len(pieces),))],
        compiler_params=pltpu.CompilerParams(vmem_limit_bytes=4 * MIB),
        cost_estimate=moved(blocks),
    )(in_hbm(owners), *[in_vmem(x) for x in own], *other, in_hbm(base))
    return out[:3], out[3]


def merge_kernel(n, pieces, scale, fresh, *refs):
    b_refs, a_refs, bases = refs[0:3], refs[3:5], refs[5:8]
    at = 8 if fresh else 11
    outs, bufs, sem = refs[at : at + 3], refs[at + 3 : at + 6], refs[at + 6]
    cols = a_refs[0].shape[-1]
    stores = []
    for i, (layer, start) in enumerate(column_starts(n, pieces, cols)):
        for proj in (1, 2, 0):
            for row in range(0, bufs[proj].shape[1], TILE_ROWS):
                rows = pl.ds(row, min(TILE_ROWS, bufs[proj].shape[1] - row))
                for col in range(0, cols, TILE_COLS):
                    width = min(TILE_COLS, cols - col)
                    tile = pl.ds(col, width) if fresh else pl.ds(pl.multiple_of(start + col, LANES), width)
                    delta = jnp.dot(
                        b_refs[proj][layer, rows],
                        a_refs[i][proj, :, col : col + width],
                        preferred_element_type=jnp.float32,
                    )
                    block = bases[proj][i if fresh else layer, rows, tile]
                    merged = block.astype(jnp.float32) + scale * delta
                    bufs[proj][i, rows, col : col + width] = merged.astype(jnp.bfloat16)
                store = pltpu.make_async_copy(
                    bufs[proj].at[i, rows], outs[proj].at[layer, rows, pl.ds(start, cols)], sem.at[len(stores)]
                )
                store.start()
                stores.append(store)
    for store in stores:
        store.wait()


def merge(n, scale, b, a_list, bases, shapes, outs, pieces):
    fresh = outs is None
    rank, cols = a_list[0].shape[-2:]
    rows = sum(base.shape[1] for base in bases)
    stores = len(pieces) * sum(-(-base.shape[1] // TILE_ROWS) for base in bases)
    return pl.pallas_call(
        functools.partial(merge_kernel, n, pieces, scale, fresh),
        in_specs=[VMEM] * (3 + len(a_list) + 3) + [HBM] * (0 if fresh else 3),
        out_specs=[HBM] * 3,
        out_shape=shapes,
        scratch_shapes=[pltpu.VMEM((len(pieces), base.shape[1], cols), base.dtype) for base in bases]
        + [pltpu.SemaphoreType.DMA((stores,))],
        input_output_aliases={} if fresh else {6 + len(a_list) + i: i for i in range(3)},
        compiler_params=pltpu.CompilerParams(vmem_limit_bytes=16 * MIB),
        cost_estimate=pl.CostEstimate(
            flops=2 * len(pieces) * rows * cols * rank,
            bytes_accessed=4 * len(pieces) * rows * cols,
            transcendentals=0,
        ),
    )(*b, *a_list, *(bases if fresh else [in_vmem(base) for base in bases]), *([] if fresh else outs))

def per_device(
    n,
    owners,
    base_query,
    base_key,
    base_value,
    left_shared_matrix,
    right_queries_matrix,
    right_keys_matrix,
    right_values_matrix,
):
    layers, projs, rank, cols = left_shared_matrix.shape[1:]
    scale = numerator_gain / rank
    bases = (base_query, base_key, base_value)
    rights = (right_queries_matrix, right_keys_matrix, right_values_matrix)
    last = n // 2

    own_a = left_shared_matrix[0]
    own_b = [jnp.swapaxes(right[0], 1, 2) for right in rights]

    if cols % LANES == 0:
        tie = lax.optimization_barrier
        shapes = [jax.ShapeDtypeStruct(base.shape, base.dtype) for base in bases]
        swapped = (swap_cores(own_a), [swap_cores(x) for x in own_b])
        pieces = [(0, True, True), (0, True, False)]
        small_blocks = fetch_blocks(n, cols, bases[1:], pieces)
        (other_a, other_b), small_blocks = tie((swapped, small_blocks))
        first, second = choose_a(owners, own_a, other_a)
        held = [first, second]
        first = ring_pass(first, n)
        second = ring_pass(second, n)
        b, block = choose_b(n, cols, owners, own_b, other_b, base_query, pieces)
        outs = merge(n, scale, b, held, [block, *small_blocks], shapes, None, pieces)
        first, _ = tie((first, outs))

        def go(pieces, chunks, outs):
            return merge(n, scale, b, chunks, bases, shapes, outs, pieces)

        def later(array, *others):
            return tie((array, others))[0]

        others = None
        for step in range(1, last):
            onward = ring_pass(first, n)
            if step > 1:
                outs = go([(step - 1, False, False), (step - 1, False, True)], others, outs)
            onward_second = ring_pass(later(second, outs), n) if step < last - 1 else None
            others = [swap_cores(later(first, second)), swap_cores(second)]
            outs = go([(step, True, True), (step, True, False)], [first, second], outs)
            first, second = later(onward, outs), onward_second
        outs = go([(last - 1, False, False), (last - 1, False, True)], others, outs)
        first = later(first, outs)
        return tuple(go([(last, True, True), (last, False, False)], [first, swap_cores(first)], outs))

    core = lax.axis_index("rollout")
    tensor = lax.axis_index("tensor")
    mine = owners == core
    a = jnp.where(mine[:, :, None, None], own_a, swap_cores(own_a))
    b = [jnp.where(mine[:, proj, None, None], x, swap_cores(x)) for proj, x in enumerate(own_b)]
    full = jnp.zeros((layers, projs, rank, n * cols), own_a.dtype)

    def put(full, piece, layer, step, from_core):
        start = place_of(n, step, from_core, tensor) * cols
        return lax.dynamic_update_slice(full, piece[None], (layer, 0, 0, start))

    first = jnp.where(core == 0, a[0], a[1])
    second = jnp.where(core == 0, a[1], a[0])
    full = put(full, first, core, 0, core)
    full = put(full, second, 1 - core, 0, core)
    for step in range(1, last + 1):
        first = ring_pass(first, n)
        full = put(full, first, core, step, core)
        full = put(full, swap_cores(first), 1 - core, step, 1 - core)
        if step < last:
            second = ring_pass(second, n)
            full = put(full, second, 1 - core, step, core)
            full = put(full, swap_cores(second), core, step, 1 - core)
    merged = []
    for proj in range(projs):
        delta = jnp.einsum("lkr,lkc->lrc", b[proj], full[:, proj], preferred_element_type=jnp.float32)
        merged.append((bases[proj].astype(jnp.float32) + scale * delta).astype(jnp.bfloat16))
    return tuple(merged)


def solution(mesh):
    return jax.shard_map(
        functools.partial(per_device, mesh.shape["tensor"]),
        mesh=mesh,
        in_specs=(
            P("copies", None),
            P("copies", "tensor", None),
            P("copies", "tensor", None),
            P("copies", "tensor", None),
            P("rollout", "copies", None, None, "tensor"),
            P("rollout", "copies", "tensor", None),
            P("rollout", "copies", "tensor", None),
            P("rollout", "copies", "tensor", None),
        ),
        out_specs=(
            P("copies", "tensor", None),
            P("copies", "tensor", None),
            P("copies", "tensor", None),
        ),
        check_vma=False,
    )
```

```python
import functools

import jax
import jax.numpy as jnp
from jax import lax
from jax.experimental import pallas as pl
from jax.experimental.pallas import tpu as pltpu
from jax.sharding import PartitionSpec as P

numerator_gain = 16.0
LANES = 128
MIB = 1024 * 1024
TILE_ROWS = 128
TILE_COLS = 256
SMEM = pl.BlockSpec(memory_space=pltpu.SMEM)
VMEM = pl.BlockSpec(memory_space=pltpu.VMEM)
HBM = pl.BlockSpec(memory_space=pltpu.HBM)
ANY = pl.BlockSpec(memory_space=pl.ANY)


def in_hbm(array):
    return pltpu.with_memory_space_constraint(array, pltpu.HBM)


def in_vmem(array):
    return pltpu.with_memory_space_constraint(array, pltpu.VMEM)


def ring_order(n):
    return list(range(0, n, 2)) + list(range(n - 1, 0, -2))


def ring_pass(array, n):
    order = ring_order(n)
    pairs = []
    for k in range(n):
        pairs.append((order[k], order[(k + 1) % n]))
        pairs.append((n + order[k], n + order[(k - 1) % n]))
    return lax.ppermute(array, ("rollout", "tensor"), pairs)


def swap_cores(array):
    return lax.ppermute(array, "rollout", [(0, 1), (1, 0)])


def place_of(n, step, from_core, tensor):
    position = jnp.where(tensor % 2 == 0, tensor // 2, n - 1 - tensor // 2)
    k = position + jnp.where(from_core == 0, -step, step)
    k = jnp.where(k < 0, k + n, jnp.where(k >= n, k - n, k))
    return jnp.where(k < n // 2, 2 * k, 2 * n - 1 - 2 * k)


def column_starts(n, pieces, cols):
    core = lax.axis_index("rollout")
    tensor = lax.axis_index("tensor")
    blocks = []
    for step, own_ring, own_layer in pieces:
        place = place_of(n, step, core if own_ring else 1 - core, tensor)
        blocks.append((core if own_layer else 1 - core, pl.multiple_of(place * cols, LANES)))
    return blocks


def choose_a_kernel(owners, own, other, first, second):
    core = lax.axis_index("rollout")
    for out, layer in ((first, core), (second, 1 - core)):
        for proj in range(own.shape[1]):
            mine = owners[layer, proj] == core
            out[proj] = jnp.where(mine, own[layer, proj], other[layer, proj])


def choose_a(owners, own, other):
    piece = jax.ShapeDtypeStruct(own.shape[1:], own.dtype)
    return pl.pallas_call(
        choose_a_kernel,
        in_specs=[SMEM, VMEM, VMEM],
        out_specs=[VMEM, VMEM],
        out_shape=[piece, piece],
        compiler_params=pltpu.CompilerParams(vmem_limit_bytes=4 * MIB),
    )(in_hbm(owners), in_vmem(own), other)


def start_fetches(n, pieces, bases, blocks, sems):
    cols = blocks[0].shape[2]
    fetches = []
    for i, (layer, start) in enumerate(column_starts(n, pieces, cols)):
        for base, block in zip(bases, blocks):
            source = base.at[layer, :, pl.ds(start, cols)]
            fetches.append(pltpu.make_async_copy(source, block.at[i], sems.at[len(fetches)]))
            fetches[-1].start()
    return fetches


def block_shapes(bases, pieces, cols):
    return [jax.ShapeDtypeStruct((len(pieces), base.shape[1], cols), base.dtype) for base in bases]


def moved(shapes):
    size = sum(x.size * x.dtype.itemsize for x in shapes)
    return pl.CostEstimate(flops=0, bytes_accessed=2 * size, transcendentals=0)


def fetch_kernel(n, pieces, *refs):
    count = len(refs) // 2
    for fetch in start_fetches(n, pieces, refs[:count], refs[count:-1], refs[-1]):
        fetch.wait()


def fetch_blocks(n, cols, bases, pieces):
    blocks = block_shapes(bases, pieces, cols)
    return pl.pallas_call(
        functools.partial(fetch_kernel, n, pieces),
        in_specs=[HBM] * len(bases),
        out_specs=[VMEM] * len(bases),
        out_shape=blocks,
        scratch_shapes=[pltpu.SemaphoreType.DMA((len(bases) * len(pieces),))],
        compiler_params=pltpu.CompilerParams(vmem_limit_bytes=4 * MIB),
        cost_estimate=moved(blocks),
    )(*[in_hbm(base) for base in bases])


def choose_b_kernel(n, pieces, owners, *refs):
    core = lax.axis_index("rollout")
    own, other, base, outs, block, sems = refs[0:3], refs[3:6], refs[6], refs[7:10], refs[10], refs[11]
    fetches = start_fetches(n, pieces, [base], [block], sems)
    for proj in range(3):
        for layer in range(own[proj].shape[0]):
            mine = owners[layer, proj] == core
            outs[proj][layer] = jnp.where(mine, own[proj][layer], other[proj][layer]).T
    for fetch in fetches:
        fetch.wait()


def choose_b(n, cols, owners, own, other, base, pieces):
    chosen = [jax.ShapeDtypeStruct((x.shape[0], x.shape[2], x.shape[1]), x.dtype) for x in own]
    blocks = block_shapes([base], pieces, cols)
    out = pl.pallas_call(
        functools.partial(choose_b_kernel, n, pieces),
        in_specs=[SMEM] + [VMEM] * 6 + [HBM],
        out_specs=[VMEM] * 4,
        out_shape=chosen + blocks,
        scratch_shapes=[pltpu.SemaphoreType.DMA((len(pieces),))],
        compiler_params=pltpu.CompilerParams(vmem_limit_bytes=4 * MIB),
        cost_estimate=moved(blocks),
    )(in_hbm(owners), *[in_vmem(x) for x in own], *other, in_hbm(base))
    return out[:3], out[3]


def merge_kernel(n, pieces, scale, fresh, *refs):
    b_refs, a_refs, bases = refs[0:3], refs[3:5], refs[5:8]
    at = 8 if fresh else 11
    outs, bufs, sem = refs[at : at + 3], refs[at + 3 : at + 6], refs[at + 6]
    cols = a_refs[0].shape[-1]
    stores = []
    for i, (layer, start) in enumerate(column_starts(n, pieces, cols)):
        for proj in (1, 2, 0):
            for row in range(0, bufs[proj].shape[1], TILE_ROWS):
                rows = pl.ds(row, min(TILE_ROWS, bufs[proj].shape[1] - row))
                for col in range(0, cols, TILE_COLS):
                    width = min(TILE_COLS, cols - col)
                    tile = pl.ds(col, width) if fresh else pl.ds(pl.multiple_of(start + col, LANES), width)
                    delta = jnp.dot(
                        b_refs[proj][layer, rows],
                        a_refs[i][proj, :, col : col + width],
                        preferred_element_type=jnp.float32,
                    )
                    block = bases[proj][i if fresh else layer, rows, tile]
                    merged = block.astype(jnp.float32) + scale * delta
                    bufs[proj][i, rows, col : col + width] = merged.astype(jnp.bfloat16)
                store = pltpu.make_async_copy(
                    bufs[proj].at[i, rows], outs[proj].at[layer, rows, pl.ds(start, cols)], sem.at[len(stores)]
                )
                store.start()
                stores.append(store)
    for store in stores:
        store.wait()


def merge(n, scale, b, a_list, bases, shapes, outs, pieces):
    fresh = outs is None
    rank, cols = a_list[0].shape[-2:]
    rows = sum(base.shape[1] for base in bases)
    stores = len(pieces) * sum(-(-base.shape[1] // TILE_ROWS) for base in bases)
    return pl.pallas_call(
        functools.partial(merge_kernel, n, pieces, scale, fresh),
        in_specs=[VMEM] * (3 + len(a_list) + 3) + [HBM] * (0 if fresh else 3),
        out_specs=[HBM] * 3,
        out_shape=shapes,
        scratch_shapes=[pltpu.VMEM((len(pieces), base.shape[1], cols), base.dtype) for base in bases]
        + [pltpu.SemaphoreType.DMA((stores,))],
        input_output_aliases={} if fresh else {6 + len(a_list) + i: i for i in range(3)},
        compiler_params=pltpu.CompilerParams(vmem_limit_bytes=16 * MIB),
        cost_estimate=pl.CostEstimate(
            flops=2 * len(pieces) * rows * cols * rank,
            bytes_accessed=4 * len(pieces) * rows * cols,
            transcendentals=0,
        ),
    )(*b, *a_list, *(bases if fresh else [in_vmem(base) for base in bases]), *([] if fresh else outs))

def per_device(
    n,
    owners,
    base_query,
    base_key,
    base_value,
    left_shared_matrix,
    right_queries_matrix,
    right_keys_matrix,
    right_values_matrix,
):
    layers, projs, rank, cols = left_shared_matrix.shape[1:]
    scale = numerator_gain / rank
    bases = (base_query, base_key, base_value)
    rights = (right_queries_matrix, right_keys_matrix, right_values_matrix)
    last = n // 2

    own_a = left_shared_matrix[0]
    own_b = [jnp.swapaxes(right[0], 1, 2) for right in rights]

    if cols % LANES == 0:
        tie = lax.optimization_barrier
        shapes = [jax.ShapeDtypeStruct(base.shape, base.dtype) for base in bases]
        swapped = (swap_cores(own_a), [swap_cores(x) for x in own_b])
        pieces = [(0, True, True), (0, True, False)]
        small_blocks = fetch_blocks(n, cols, bases[1:], pieces)
        (other_a, other_b), small_blocks = tie((swapped, small_blocks))
        first, second = choose_a(owners, own_a, other_a)
        held = [first, second]
        first = ring_pass(first, n)
        second = ring_pass(second, n)
        b, block = choose_b(n, cols, owners, own_b, other_b, base_query, pieces)
        outs = merge(n, scale, b, held, [block, *small_blocks], shapes, None, pieces)
        first, outs = tie((first, outs))

        def go(pieces, chunks, outs):
            return merge(n, scale, b, chunks, bases, shapes, outs, pieces)

        ready = []
        for step in range(1, last + 1):
            if step > 1:
                outs = go(*ready.pop(0), outs)
            ready.append(([(step, True, True), (step, False, False)], [first, swap_cores(first)]))
            if step < last:
                first = ring_pass(first, n)
                second, outs = tie((second, outs))
                ready.append(([(step, True, False), (step, False, True)], [second, swap_cores(second)]))
                outs = go(*ready.pop(0), outs)
                first, outs = tie((first, outs))
                if step < last - 1:
                    second = ring_pass(second, n)
        for item in ready:
            outs = go(*item, outs)
        return tuple(outs)

    core = lax.axis_index("rollout")
    tensor = lax.axis_index("tensor")
    mine = owners == core
    a = jnp.where(mine[:, :, None, None], own_a, swap_cores(own_a))
    b = [jnp.where(mine[:, proj, None, None], x, swap_cores(x)) for proj, x in enumerate(own_b)]
    full = jnp.zeros((layers, projs, rank, n * cols), own_a.dtype)

    def put(full, piece, layer, step, from_core):
        start = place_of(n, step, from_core, tensor) * cols
        return lax.dynamic_update_slice(full, piece[None], (layer, 0, 0, start))

    first = jnp.where(core == 0, a[0], a[1])
    second = jnp.where(core == 0, a[1], a[0])
    full = put(full, first, core, 0, core)
    full = put(full, second, 1 - core, 0, core)
    for step in range(1, last + 1):
        first = ring_pass(first, n)
        full = put(full, first, core, step, core)
        full = put(full, swap_cores(first), 1 - core, step, 1 - core)
        if step < last:
            second = ring_pass(second, n)
            full = put(full, second, 1 - core, step, core)
            full = put(full, swap_cores(second), core, step, 1 - core)
    merged = []
    for proj in range(projs):
        delta = jnp.einsum("lkr,lkc->lrc", b[proj], full[:, proj], preferred_element_type=jnp.float32)
        merged.append((bases[proj].astype(jnp.float32) + scale * delta).astype(jnp.bfloat16))
    return tuple(merged)


def solution(mesh):
    return jax.shard_map(
        functools.partial(per_device, mesh.shape["tensor"]),
        mesh=mesh,
        in_specs=(
            P("copies", None),
            P("copies", "tensor", None),
            P("copies", "tensor", None),
            P("copies", "tensor", None),
            P("rollout", "copies", None, None, "tensor"),
            P("rollout", "copies", "tensor", None),
            P("rollout", "copies", "tensor", None),
            P("rollout", "copies", "tensor", None),
        ),
        out_specs=(
            P("copies", "tensor", None),
            P("copies", "tensor", None),
            P("copies", "tensor", None),
        ),
        check_vma=False,
    )
```

```python
import functools

import jax
import jax.numpy as jnp
from jax import lax
from jax.experimental import pallas as pl
from jax.experimental.pallas import tpu as pltpu
from jax.sharding import PartitionSpec as P

numerator_gain = 16.0
LANES = 128
MIB = 1024 * 1024
TILE_ROWS = 128
TILE_COLS = 256
VMEM = pl.BlockSpec(memory_space=pltpu.VMEM)
HBM = pl.BlockSpec(memory_space=pltpu.HBM)
ANY = pl.BlockSpec(memory_space=pl.ANY)


def in_hbm(array):
    return pltpu.with_memory_space_constraint(array, pltpu.HBM)


def in_vmem(array):
    return pltpu.with_memory_space_constraint(array, pltpu.VMEM)


def ring_order(n):
    return list(range(0, n, 2)) + list(range(n - 1, 0, -2))


def ring_pass(array, n):
    order = ring_order(n)
    pairs = []
    for k in range(n):
        pairs.append((order[k], order[(k + 1) % n]))
        pairs.append((n + order[k], n + order[(k - 1) % n]))
    return lax.ppermute(array, ("rollout", "tensor"), pairs)


def swap_cores(array):
    return lax.ppermute(array, "rollout", [(0, 1), (1, 0)])


def place_of(n, step, from_core, tensor):
    position = jnp.where(tensor % 2 == 0, tensor // 2, n - 1 - tensor // 2)
    k = position + jnp.where(from_core == 0, -step, step)
    k = jnp.where(k < 0, k + n, jnp.where(k >= n, k - n, k))
    return jnp.where(k < n // 2, 2 * k, 2 * n - 1 - 2 * k)


def column_starts(n, pieces, cols):
    core = lax.axis_index("rollout")
    tensor = lax.axis_index("tensor")
    blocks = []
    for step, own_ring, own_layer in pieces:
        place = place_of(n, step, core if own_ring else 1 - core, tensor)
        blocks.append((core if own_layer else 1 - core, pl.multiple_of(place * cols, LANES)))
    return blocks


def owned(owners, layer, proj, core, shape):
    return jnp.broadcast_to(owners[pl.ds(layer, 1), proj : proj + 1] == core, shape)


def choose_a_kernel(owners, own, other, first, second):
    core = lax.axis_index("rollout")
    for out, layer in ((first, core), (second, 1 - core)):
        for proj in range(own.shape[1]):
            mine = owned(owners, layer, proj, core, out.shape[1:])
            out[proj] = jnp.where(mine, own[layer, proj], other[layer, proj])


def choose_a(owners, own, other):
    piece = jax.ShapeDtypeStruct(own.shape[1:], own.dtype)
    return pl.pallas_call(
        choose_a_kernel,
        in_specs=[VMEM, VMEM, VMEM],
        out_specs=[VMEM, VMEM],
        out_shape=[piece, piece],
        compiler_params=pltpu.CompilerParams(vmem_limit_bytes=4 * MIB),
    )(in_vmem(owners), in_vmem(own), other)


def start_fetches(n, pieces, bases, blocks, sems):
    cols = blocks[0].shape[2]
    fetches = []
    for i, (layer, start) in enumerate(column_starts(n, pieces, cols)):
        for base, block in zip(bases, blocks):
            source = base.at[layer, :, pl.ds(start, cols)]
            fetches.append(pltpu.make_async_copy(source, block.at[i], sems.at[len(fetches)]))
            fetches[-1].start()
    return fetches


def block_shapes(bases, pieces, cols):
    return [jax.ShapeDtypeStruct((len(pieces), base.shape[1], cols), base.dtype) for base in bases]


def moved(shapes):
    size = sum(x.size * x.dtype.itemsize for x in shapes)
    return pl.CostEstimate(flops=0, bytes_accessed=2 * size, transcendentals=0)


def fetch_kernel(n, pieces, *refs):
    count = len(refs) // 2
    for fetch in start_fetches(n, pieces, refs[:count], refs[count:-1], refs[-1]):
        fetch.wait()


def fetch_blocks(n, cols, bases, pieces):
    blocks = block_shapes(bases, pieces, cols)
    return pl.pallas_call(
        functools.partial(fetch_kernel, n, pieces),
        in_specs=[HBM] * len(bases),
        out_specs=[VMEM] * len(bases),
        out_shape=blocks,
        scratch_shapes=[pltpu.SemaphoreType.DMA((len(bases) * len(pieces),))],
        compiler_params=pltpu.CompilerParams(vmem_limit_bytes=4 * MIB),
        cost_estimate=moved(blocks),
    )(*[in_hbm(base) for base in bases])


def choose_b_kernel(n, pieces, owners, *refs):
    core = lax.axis_index("rollout")
    own, other, refs, sems = refs[0:3], refs[3:6], refs[6:-1], refs[-1]
    count = (len(refs) - 3) // 2
    bases, outs, blocks = refs[:count], refs[count : count + 3], refs[count + 3 :]
    fetches = start_fetches(n, pieces, bases, blocks, sems)
    for proj in range(3):
        for layer in range(own[proj].shape[0]):
            mine = owned(owners, layer, proj, core, own[proj].shape[1:])
            outs[proj][layer] = jnp.where(mine, own[proj][layer], other[proj][layer]).T
    for fetch in fetches:
        fetch.wait()


def choose_b(n, cols, owners, own, other, bases, pieces):
    chosen = [jax.ShapeDtypeStruct((x.shape[0], x.shape[2], x.shape[1]), x.dtype) for x in own]
    blocks = block_shapes(bases, pieces, cols)
    out = pl.pallas_call(
        functools.partial(choose_b_kernel, n, pieces),
        in_specs=[VMEM] * 7 + [HBM] * len(bases),
        out_specs=[VMEM] * (3 + len(blocks)),
        out_shape=chosen + blocks,
        scratch_shapes=[pltpu.SemaphoreType.DMA((len(bases) * len(pieces),))],
        compiler_params=pltpu.CompilerParams(vmem_limit_bytes=4 * MIB),
        cost_estimate=moved(blocks),
    )(in_vmem(owners), *[in_vmem(x) for x in own], *other, *[in_hbm(base) for base in bases])
    return out[:3], out[3:]


def merge_kernel(n, pieces, scale, fresh, *refs):
    count = len(pieces)
    b_refs, a_refs, bases = refs[0:3], refs[3 : 3 + count], refs[3 + count : 6 + count]
    at = 6 + count + (0 if fresh else 3)
    outs, bufs, sem = refs[at : at + 3], refs[at + 3 : at + 6], refs[at + 6]
    cols = a_refs[0].shape[-1]
    stores = []
    for i, (layer, start) in enumerate(column_starts(n, pieces, cols)):
        for proj in (1, 2, 0):
            for row in range(0, bufs[proj].shape[1], TILE_ROWS):
                rows = pl.ds(row, min(TILE_ROWS, bufs[proj].shape[1] - row))
                for col in range(0, cols, TILE_COLS):
                    width = min(TILE_COLS, cols - col)
                    tile = pl.ds(col, width) if fresh else pl.ds(pl.multiple_of(start + col, LANES), width)
                    delta = jnp.dot(
                        b_refs[proj][layer, rows],
                        a_refs[i][proj, :, col : col + width],
                        preferred_element_type=jnp.float32,
                    )
                    block = bases[proj][i if fresh else layer, rows, tile]
                    merged = block.astype(jnp.float32) + scale * delta
                    bufs[proj][i, rows, col : col + width] = merged.astype(jnp.bfloat16)
                store = pltpu.make_async_copy(
                    bufs[proj].at[i, rows], outs[proj].at[layer, rows, pl.ds(start, cols)], sem.at[len(stores)]
                )
                store.start()
                stores.append(store)
    for store in stores:
        store.wait()


def merge(n, scale, b, a_list, bases, shapes, outs, pieces):
    fresh = outs is None
    rank, cols = a_list[0].shape[-2:]
    rows = sum(base.shape[1] for base in bases)
    stores = len(pieces) * sum(-(-base.shape[1] // TILE_ROWS) for base in bases)
    return pl.pallas_call(
        functools.partial(merge_kernel, n, pieces, scale, fresh),
        in_specs=[VMEM] * (3 + len(a_list) + 3) + [HBM] * (0 if fresh else 3),
        out_specs=[HBM] * 3,
        out_shape=shapes,
        scratch_shapes=[pltpu.VMEM((len(pieces), base.shape[1], cols), base.dtype) for base in bases]
        + [pltpu.SemaphoreType.DMA((stores,))],
        input_output_aliases={} if fresh else {6 + len(a_list) + i: i for i in range(3)},
        compiler_params=pltpu.CompilerParams(vmem_limit_bytes=16 * MIB),
        cost_estimate=pl.CostEstimate(
            flops=2 * len(pieces) * rows * cols * rank,
            bytes_accessed=4 * len(pieces) * rows * cols,
            transcendentals=0,
        ),
    )(*b, *a_list, *(bases if fresh else [in_vmem(base) for base in bases]), *([] if fresh else outs))

def per_device(
    n,
    owners,
    base_query,
    base_key,
    base_value,
    left_shared_matrix,
    right_queries_matrix,
    right_keys_matrix,
    right_values_matrix,
):
    layers, projs, rank, cols = left_shared_matrix.shape[1:]
    scale = numerator_gain / rank
    bases = (base_query, base_key, base_value)
    rights = (right_queries_matrix, right_keys_matrix, right_values_matrix)
    last = n // 2

    own_a = left_shared_matrix[0]
    own_b = [jnp.swapaxes(right[0], 1, 2) for right in rights]

    if cols % LANES == 0:
        tie = lax.optimization_barrier
        shapes = [jax.ShapeDtypeStruct(base.shape, base.dtype) for base in bases]
        swapped = (swap_cores(own_a), [swap_cores(x) for x in own_b])
        pieces = [(0, True, True), (0, True, False)]
        key_block = fetch_blocks(n, cols, [base_key], pieces)
        (other_a, other_b), key_block = tie((swapped, key_block))
        first, second = choose_a(owners, own_a, other_a)
        held = [first, second]
        first = ring_pass(first, n)
        second = ring_pass(second, n)
        b, blocks = choose_b(n, cols, owners, own_b, other_b, [base_query, base_value], pieces)
        outs = merge(n, scale, b, held, [blocks[0], key_block[0], blocks[1]], shapes, None, pieces)
        first, outs = tie((first, outs))

        def go(pieces, chunks, outs):
            return merge(n, scale, b, chunks, bases, shapes, outs, pieces)

        waiting = None
        for step in range(1, last):
            if step > 1:
                outs = go(*waiting, outs)
            pieces = [(step, True, True), (step, False, False)]
            chunks = [first, swap_cores(first)]
            first = ring_pass(first, n)
            second, outs = tie((second, outs))
            waiting = [(step, True, False), (step, False, True)], [second, swap_cores(second)]
            if step == last - 1:
                pieces, chunks = pieces + waiting[0][:1], chunks + waiting[1][:1]
            outs = go(pieces, chunks, outs)
            first, outs = tie((first, outs))
            if step < last - 1:
                second = ring_pass(second, n)
        swapped = swap_cores(first)
        outs = go([waiting[0][1], (last, True, True)], [waiting[1][1], first], outs)
        return tuple(go([(last, False, False)], [swapped], outs))

    core = lax.axis_index("rollout")
    tensor = lax.axis_index("tensor")
    mine = owners == core
    a = jnp.where(mine[:, :, None, None], own_a, swap_cores(own_a))
    b = [jnp.where(mine[:, proj, None, None], x, swap_cores(x)) for proj, x in enumerate(own_b)]
    full = jnp.zeros((layers, projs, rank, n * cols), own_a.dtype)

    def put(full, piece, layer, step, from_core):
        start = place_of(n, step, from_core, tensor) * cols
        return lax.dynamic_update_slice(full, piece[None], (layer, 0, 0, start))

    first = jnp.where(core == 0, a[0], a[1])
    second = jnp.where(core == 0, a[1], a[0])
    full = put(full, first, core, 0, core)
    full = put(full, second, 1 - core, 0, core)
    for step in range(1, last + 1):
        first = ring_pass(first, n)
        full = put(full, first, core, step, core)
        full = put(full, swap_cores(first), 1 - core, step, 1 - core)
        if step < last:
            second = ring_pass(second, n)
            full = put(full, second, 1 - core, step, core)
            full = put(full, swap_cores(second), core, step, 1 - core)
    merged = []
    for proj in range(projs):
        delta = jnp.einsum("lkr,lkc->lrc", b[proj], full[:, proj], preferred_element_type=jnp.float32)
        merged.append((bases[proj].astype(jnp.float32) + scale * delta).astype(jnp.bfloat16))
    return tuple(merged)


def solution(mesh):
    return jax.shard_map(
        functools.partial(per_device, mesh.shape["tensor"]),
        mesh=mesh,
        in_specs=(
            P("copies", None),
            P("copies", "tensor", None),
            P("copies", "tensor", None),
            P("copies", "tensor", None),
            P("rollout", "copies", None, None, "tensor"),
            P("rollout", "copies", "tensor", None),
            P("rollout", "copies", "tensor", None),
            P("rollout", "copies", "tensor", None),
        ),
        out_specs=(
            P("copies", "tensor", None),
            P("copies", "tensor", None),
            P("copies", "tensor", None),
        ),
        check_vma=False,
    )
```

```python
import functools

import jax
import jax.numpy as jnp
from jax import lax
from jax.experimental import pallas as pl
from jax.experimental.pallas import tpu as pltpu
from jax.sharding import PartitionSpec as P

numerator_gain = 16.0
LANES = 128
MIB = 1024 * 1024
TILE_ROWS = 128
TILE_COLS = 256
VMEM = pl.BlockSpec(memory_space=pltpu.VMEM)
HBM = pl.BlockSpec(memory_space=pltpu.HBM)
ANY = pl.BlockSpec(memory_space=pl.ANY)


def in_hbm(array):
    return pltpu.with_memory_space_constraint(array, pltpu.HBM)


def in_vmem(array):
    return pltpu.with_memory_space_constraint(array, pltpu.VMEM)


def ring_order(n):
    return list(range(0, n, 2)) + list(range(n - 1, 0, -2))


def ring_pass(array, n, places=1):
    order = ring_order(n)
    pairs = []
    for k in range(n):
        pairs.append((order[k], order[(k + places) % n]))
        pairs.append((n + order[k], n + order[(k - places) % n]))
    return lax.ppermute(array, ("rollout", "tensor"), pairs)


def swap_cores(array):
    return lax.ppermute(array, "rollout", [(0, 1), (1, 0)])


def place_of(n, step, from_core, tensor):
    position = jnp.where(tensor % 2 == 0, tensor // 2, n - 1 - tensor // 2)
    k = position + jnp.where(from_core == 0, -step, step)
    k = jnp.where(k < 0, k + n, jnp.where(k >= n, k - n, k))
    return jnp.where(k < n // 2, 2 * k, 2 * n - 1 - 2 * k)


def column_starts(n, pieces, cols):
    core = lax.axis_index("rollout")
    tensor = lax.axis_index("tensor")
    blocks = []
    for step, own_ring, own_layer in pieces:
        place = place_of(n, step, core if own_ring else 1 - core, tensor)
        blocks.append((core if own_layer else 1 - core, pl.multiple_of(place * cols, LANES)))
    return blocks


def owned(owners, layer, proj, core, shape):
    return jnp.broadcast_to(owners[pl.ds(layer, 1), proj : proj + 1] == core, shape)


def choose_a_kernel(owners, own, other, first, second):
    core = lax.axis_index("rollout")
    for out, layer in ((first, core), (second, 1 - core)):
        for proj in range(own.shape[1]):
            mine = owned(owners, layer, proj, core, out.shape[1:])
            out[proj] = jnp.where(mine, own[layer, proj], other[layer, proj])


def choose_a(owners, own, other):
    piece = jax.ShapeDtypeStruct(own.shape[1:], own.dtype)
    return pl.pallas_call(
        choose_a_kernel,
        in_specs=[VMEM, VMEM, VMEM],
        out_specs=[VMEM, VMEM],
        out_shape=[piece, piece],
        compiler_params=pltpu.CompilerParams(vmem_limit_bytes=4 * MIB),
    )(in_vmem(owners), in_vmem(own), other)


def start_fetches(n, pieces, bases, blocks, sems):
    cols = blocks[0].shape[2]
    fetches = []
    for i, (layer, start) in enumerate(column_starts(n, pieces, cols)):
        for base, block in zip(bases, blocks):
            source = base.at[layer, :, pl.ds(start, cols)]
            fetches.append(pltpu.make_async_copy(source, block.at[i], sems.at[len(fetches)]))
            fetches[-1].start()
    return fetches


def block_shapes(bases, pieces, cols):
    return [jax.ShapeDtypeStruct((len(pieces), base.shape[1], cols), base.dtype) for base in bases]


def moved(shapes):
    size = sum(x.size * x.dtype.itemsize for x in shapes)
    return pl.CostEstimate(flops=0, bytes_accessed=2 * size, transcendentals=0)


def fetch_kernel(n, pieces, *refs):
    count = len(refs) // 2
    for fetch in start_fetches(n, pieces, refs[:count], refs[count:-1], refs[-1]):
        fetch.wait()


def fetch_blocks(n, cols, bases, pieces):
    blocks = block_shapes(bases, pieces, cols)
    return pl.pallas_call(
        functools.partial(fetch_kernel, n, pieces),
        in_specs=[HBM] * len(bases),
        out_specs=[VMEM] * len(bases),
        out_shape=blocks,
        scratch_shapes=[pltpu.SemaphoreType.DMA((len(bases) * len(pieces),))],
        compiler_params=pltpu.CompilerParams(vmem_limit_bytes=4 * MIB),
        cost_estimate=moved(blocks),
    )(*[in_hbm(base) for base in bases])


def choose_b_kernel(n, pieces, owners, *refs):
    core = lax.axis_index("rollout")
    own, other, refs, sems = refs[0:3], refs[3:6], refs[6:-1], refs[-1]
    count = (len(refs) - 3) // 2
    bases, outs, blocks = refs[:count], refs[count : count + 3], refs[count + 3 :]
    fetches = start_fetches(n, pieces, bases, blocks, sems)
    for proj in range(3):
        for layer in range(own[proj].shape[0]):
            mine = owned(owners, layer, proj, core, own[proj].shape[1:])
            outs[proj][layer] = jnp.where(mine, own[proj][layer], other[proj][layer]).T
    for fetch in fetches:
        fetch.wait()


def choose_b(n, cols, owners, own, other, bases, pieces):
    chosen = [jax.ShapeDtypeStruct((x.shape[0], x.shape[2], x.shape[1]), x.dtype) for x in own]
    blocks = block_shapes(bases, pieces, cols)
    out = pl.pallas_call(
        functools.partial(choose_b_kernel, n, pieces),
        in_specs=[VMEM] * 7 + [HBM] * len(bases),
        out_specs=[VMEM] * (3 + len(blocks)),
        out_shape=chosen + blocks,
        scratch_shapes=[pltpu.SemaphoreType.DMA((len(bases) * len(pieces),))],
        compiler_params=pltpu.CompilerParams(vmem_limit_bytes=4 * MIB),
        cost_estimate=moved(blocks),
    )(in_vmem(owners), *[in_vmem(x) for x in own], *other, *[in_hbm(base) for base in bases])
    return out[:3], out[3:]


def merge_kernel(n, pieces, scale, fresh, *refs):
    count = len(pieces)
    b_refs, a_refs, bases = refs[0:3], refs[3 : 3 + count], refs[3 + count : 6 + count]
    at = 6 + count + (0 if fresh else 3)
    outs, bufs, sem = refs[at : at + 3], refs[at + 3 : at + 6], refs[at + 6]
    cols = a_refs[0].shape[-1]
    stores = []
    for i, (layer, start) in enumerate(column_starts(n, pieces, cols)):
        for proj in (1, 2, 0):
            for row in range(0, bufs[proj].shape[1], TILE_ROWS):
                rows = pl.ds(row, min(TILE_ROWS, bufs[proj].shape[1] - row))
                for col in range(0, cols, TILE_COLS):
                    width = min(TILE_COLS, cols - col)
                    tile = pl.ds(col, width) if fresh else pl.ds(pl.multiple_of(start + col, LANES), width)
                    delta = jnp.dot(
                        b_refs[proj][layer, rows],
                        a_refs[i][proj, :, col : col + width],
                        preferred_element_type=jnp.float32,
                    )
                    block = bases[proj][i if fresh else layer, rows, tile]
                    merged = block.astype(jnp.float32) + scale * delta
                    bufs[proj][i, rows, col : col + width] = merged.astype(jnp.bfloat16)
                store = pltpu.make_async_copy(
                    bufs[proj].at[i, rows], outs[proj].at[layer, rows, pl.ds(start, cols)], sem.at[len(stores)]
                )
                store.start()
                stores.append(store)
    for store in stores:
        store.wait()


def merge(n, scale, b, a_list, bases, shapes, outs, pieces):
    fresh = outs is None
    rank, cols = a_list[0].shape[-2:]
    rows = sum(base.shape[1] for base in bases)
    stores = len(pieces) * sum(-(-base.shape[1] // TILE_ROWS) for base in bases)
    return pl.pallas_call(
        functools.partial(merge_kernel, n, pieces, scale, fresh),
        in_specs=[VMEM] * (3 + len(a_list) + 3) + [HBM] * (0 if fresh else 3),
        out_specs=[HBM] * 3,
        out_shape=shapes,
        scratch_shapes=[pltpu.VMEM((len(pieces), base.shape[1], cols), base.dtype) for base in bases]
        + [pltpu.SemaphoreType.DMA((stores,))],
        input_output_aliases={} if fresh else {6 + len(a_list) + i: i for i in range(3)},
        compiler_params=pltpu.CompilerParams(vmem_limit_bytes=16 * MIB),
        cost_estimate=pl.CostEstimate(
            flops=2 * len(pieces) * rows * cols * rank,
            bytes_accessed=4 * len(pieces) * rows * cols,
            transcendentals=0,
        ),
    )(*b, *a_list, *(bases if fresh else [in_vmem(base) for base in bases]), *([] if fresh else outs))

def per_device(
    n,
    owners,
    base_query,
    base_key,
    base_value,
    left_shared_matrix,
    right_queries_matrix,
    right_keys_matrix,
    right_values_matrix,
):
    layers, projs, rank, cols = left_shared_matrix.shape[1:]
    scale = numerator_gain / rank
    bases = (base_query, base_key, base_value)
    rights = (right_queries_matrix, right_keys_matrix, right_values_matrix)
    last = n // 2

    own_a = left_shared_matrix[0]
    own_b = [jnp.swapaxes(right[0], 1, 2) for right in rights]

    if cols % LANES == 0 and n == 8:
        tie = lax.optimization_barrier
        shapes = [jax.ShapeDtypeStruct(base.shape, base.dtype) for base in bases]
        swapped = (swap_cores(own_a), [swap_cores(x) for x in own_b])
        pieces = [(0, True, True), (0, True, False)]
        key_block = fetch_blocks(n, cols, [base_key], pieces)
        (other_a, other_b), key_block = tie((swapped, key_block))
        first, second = choose_a(owners, own_a, other_a)
        a1 = ring_pass(first, n)
        b1 = ring_pass(second, n)
        b, blocks = choose_b(n, cols, owners, own_b, other_b, [base_query, base_value], pieces)
        own_blocks = [blocks[0], key_block[0], blocks[1]]
        outs = merge(n, scale, b, [first, second], own_blocks, shapes, None, pieces)

        def go(outs, **chunks):
            pieces = []
            for name in chunks:
                swapped = name.startswith("x")
                pieces.append((int(name[-1]), not swapped, (name[-2] == "a") != swapped))
            return merge(n, scale, b, list(chunks.values()), bases, shapes, outs, pieces)

        a1, outs = tie((a1, outs))
        a2, a3, xa1 = ring_pass(a1, n), ring_pass(a1, n, 2), swap_cores(a1)
        b1, outs = tie((b1, outs))
        b2, xb1 = ring_pass(b1, n), swap_cores(b1)
        outs = go(outs, a1=a1, xa1=xa1)
        a2, outs = tie((a2, outs))
        xa2 = swap_cores(a2)
        outs = go(outs, b1=b1, xb1=xb1)
        a3, outs = tie((a3, outs))
        a4, xa3 = ring_pass(a3, n), swap_cores(a3)
        b2, outs = tie((b2, outs))
        b3, xb2 = ring_pass(b2, n), swap_cores(b2)
        outs = go(outs, a2=a2, xa2=xa2)
        outs = go(outs, b2=b2, xb2=xb2)
        a4, outs = tie((a4, outs))
        xa4 = swap_cores(a4)
        outs = go(outs, a3=a3, xa3=xa3)
        b3, outs = tie((b3, outs))
        xb3 = swap_cores(b3)
        outs = go(outs, a4=a4, xa4=xa4, b3=b3)
        return tuple(go(outs, xb3=xb3))

    core = lax.axis_index("rollout")
    tensor = lax.axis_index("tensor")
    mine = owners == core
    a = jnp.where(mine[:, :, None, None], own_a, swap_cores(own_a))
    b = [jnp.where(mine[:, proj, None, None], x, swap_cores(x)) for proj, x in enumerate(own_b)]
    full = jnp.zeros((layers, projs, rank, n * cols), own_a.dtype)

    def put(full, piece, layer, step, from_core):
        start = place_of(n, step, from_core, tensor) * cols
        return lax.dynamic_update_slice(full, piece[None], (layer, 0, 0, start))

    first = jnp.where(core == 0, a[0], a[1])
    second = jnp.where(core == 0, a[1], a[0])
    full = put(full, first, core, 0, core)
    full = put(full, second, 1 - core, 0, core)
    for step in range(1, last + 1):
        first = ring_pass(first, n)
        full = put(full, first, core, step, core)
        full = put(full, swap_cores(first), 1 - core, step, 1 - core)
        if step < last:
            second = ring_pass(second, n)
            full = put(full, second, 1 - core, step, core)
            full = put(full, swap_cores(second), core, step, 1 - core)
    merged = []
    for proj in range(projs):
        delta = jnp.einsum("lkr,lkc->lrc", b[proj], full[:, proj], preferred_element_type=jnp.float32)
        merged.append((bases[proj].astype(jnp.float32) + scale * delta).astype(jnp.bfloat16))
    return tuple(merged)


def solution(mesh):
    return jax.shard_map(
        functools.partial(per_device, mesh.shape["tensor"]),
        mesh=mesh,
        in_specs=(
            P("copies", None),
            P("copies", "tensor", None),
            P("copies", "tensor", None),
            P("copies", "tensor", None),
            P("rollout", "copies", None, None, "tensor"),
            P("rollout", "copies", "tensor", None),
            P("rollout", "copies", "tensor", None),
            P("rollout", "copies", "tensor", None),
        ),
        out_specs=(
            P("copies", "tensor", None),
            P("copies", "tensor", None),
            P("copies", "tensor", None),
        ),
        check_vma=False,
    )
```

```python
import functools

import jax
import jax.numpy as jnp
from jax import lax
from jax.experimental import pallas as pl
from jax.experimental.pallas import tpu as pltpu
from jax.sharding import PartitionSpec as P

numerator_gain = 16.0
LANES = 128
MIB = 1024 * 1024
TILE_ROWS = 128
TILE_COLS = 256
VMEM = pl.BlockSpec(memory_space=pltpu.VMEM)
HBM = pl.BlockSpec(memory_space=pltpu.HBM)
ANY = pl.BlockSpec(memory_space=pl.ANY)


def in_hbm(array):
    return pltpu.with_memory_space_constraint(array, pltpu.HBM)


def in_vmem(array):
    return pltpu.with_memory_space_constraint(array, pltpu.VMEM)


def ring_order(n):
    return list(range(0, n, 2)) + list(range(n - 1, 0, -2))


def ring_pass(array, n):
    order = ring_order(n)
    pairs = []
    for k in range(n):
        pairs.append((order[k], order[(k + 1) % n]))
        pairs.append((n + order[k], n + order[(k - 1) % n]))
    return lax.ppermute(array, ("rollout", "tensor"), pairs)


def swap_cores(array):
    return lax.ppermute(array, "rollout", [(0, 1), (1, 0)])


def place_of(n, step, from_core, tensor):
    position = jnp.where(tensor % 2 == 0, tensor // 2, n - 1 - tensor // 2)
    k = position + jnp.where(from_core == 0, -step, step)
    k = jnp.where(k < 0, k + n, jnp.where(k >= n, k - n, k))
    return jnp.where(k < n // 2, 2 * k, 2 * n - 1 - 2 * k)


def column_starts(n, pieces, cols):
    core = lax.axis_index("rollout")
    tensor = lax.axis_index("tensor")
    blocks = []
    for step, own_ring, own_layer in pieces:
        place = place_of(n, step, core if own_ring else 1 - core, tensor)
        blocks.append((core if own_layer else 1 - core, pl.multiple_of(place * cols, LANES)))
    return blocks


def owned(owners, layer, proj, core, shape):
    return jnp.broadcast_to(owners[pl.ds(layer, 1), proj : proj + 1] == core, shape)


def choose_a_kernel(owners, own, other, first, second):
    core = lax.axis_index("rollout")
    for out, layer in ((first, core), (second, 1 - core)):
        for proj in range(own.shape[1]):
            mine = owned(owners, layer, proj, core, out.shape[1:])
            out[proj] = jnp.where(mine, own[layer, proj], other[layer, proj])


def choose_a(owners, own, other):
    piece = jax.ShapeDtypeStruct(own.shape[1:], own.dtype)
    return pl.pallas_call(
        choose_a_kernel,
        in_specs=[VMEM, VMEM, VMEM],
        out_specs=[VMEM, VMEM],
        out_shape=[piece, piece],
        compiler_params=pltpu.CompilerParams(vmem_limit_bytes=4 * MIB),
    )(in_vmem(owners), in_vmem(own), other)


def start_fetches(n, pieces, bases, blocks, sems):
    cols = blocks[0].shape[2]
    fetches = []
    for i, (layer, start) in enumerate(column_starts(n, pieces, cols)):
        for base, block in zip(bases, blocks):
            source = base.at[layer, :, pl.ds(start, cols)]
            fetches.append(pltpu.make_async_copy(source, block.at[i], sems.at[len(fetches)]))
            fetches[-1].start()
    return fetches


def block_shapes(bases, pieces, cols):
    return [jax.ShapeDtypeStruct((len(pieces), base.shape[1], cols), base.dtype) for base in bases]


def moved(shapes):
    size = sum(x.size * x.dtype.itemsize for x in shapes)
    return pl.CostEstimate(flops=0, bytes_accessed=2 * size, transcendentals=0)


def fetch_kernel(n, pieces, *refs):
    count = len(refs) // 2
    for fetch in start_fetches(n, pieces, refs[:count], refs[count:-1], refs[-1]):
        fetch.wait()


def fetch_blocks(n, cols, bases, pieces):
    blocks = block_shapes(bases, pieces, cols)
    return pl.pallas_call(
        functools.partial(fetch_kernel, n, pieces),
        in_specs=[HBM] * len(bases),
        out_specs=[VMEM] * len(bases),
        out_shape=blocks,
        scratch_shapes=[pltpu.SemaphoreType.DMA((len(bases) * len(pieces),))],
        compiler_params=pltpu.CompilerParams(vmem_limit_bytes=4 * MIB),
        cost_estimate=moved(blocks),
    )(*[in_hbm(base) for base in bases])


def choose_b_kernel(n, pieces, owners, *refs):
    core = lax.axis_index("rollout")
    own, other, refs, sems = refs[0:3], refs[3:6], refs[6:-1], refs[-1]
    count = (len(refs) - 3) // 2
    bases, outs, blocks = refs[:count], refs[count : count + 3], refs[count + 3 :]
    fetches = start_fetches(n, pieces, bases, blocks, sems)
    for proj in range(3):
        for layer in range(own[proj].shape[0]):
            mine = owned(owners, layer, proj, core, own[proj].shape[1:])
            outs[proj][layer] = jnp.where(mine, own[proj][layer], other[proj][layer]).T
    for fetch in fetches:
        fetch.wait()


def choose_b(n, cols, owners, own, other, bases, pieces):
    chosen = [jax.ShapeDtypeStruct((x.shape[0], x.shape[2], x.shape[1]), x.dtype) for x in own]
    blocks = block_shapes(bases, pieces, cols)
    out = pl.pallas_call(
        functools.partial(choose_b_kernel, n, pieces),
        in_specs=[VMEM] * 7 + [HBM] * len(bases),
        out_specs=[VMEM] * (3 + len(blocks)),
        out_shape=chosen + blocks,
        scratch_shapes=[pltpu.SemaphoreType.DMA((len(bases) * len(pieces),))],
        compiler_params=pltpu.CompilerParams(vmem_limit_bytes=4 * MIB),
        cost_estimate=moved(blocks),
    )(in_vmem(owners), *[in_vmem(x) for x in own], *other, *[in_hbm(base) for base in bases])
    return out[:3], out[3:]


def merge_kernel(n, pieces, scale, fresh, *refs):
    count = len(pieces)
    b_refs, a_refs, bases = refs[0:3], refs[3 : 3 + count], refs[3 + count : 6 + count]
    at = 6 + count + (0 if fresh else 3)
    outs, bufs, sem = refs[at : at + 3], refs[at + 3 : at + 6], refs[at + 6]
    cols = a_refs[0].shape[-1]
    stores = []
    for i, (layer, start) in enumerate(column_starts(n, pieces, cols)):
        for proj in (1, 2, 0):
            for row in range(0, bufs[proj].shape[1], TILE_ROWS):
                rows = pl.ds(row, min(TILE_ROWS, bufs[proj].shape[1] - row))
                for col in range(0, cols, TILE_COLS):
                    width = min(TILE_COLS, cols - col)
                    tile = pl.ds(col, width) if fresh else pl.ds(pl.multiple_of(start + col, LANES), width)
                    delta = jnp.dot(
                        b_refs[proj][layer, rows],
                        a_refs[i][proj, :, col : col + width],
                        preferred_element_type=jnp.float32,
                    )
                    block = bases[proj][i if fresh else layer, rows, tile]
                    merged = block.astype(jnp.float32) + scale * delta
                    bufs[proj][i, rows, col : col + width] = merged.astype(jnp.bfloat16)
                store = pltpu.make_async_copy(
                    bufs[proj].at[i, rows], outs[proj].at[layer, rows, pl.ds(start, cols)], sem.at[len(stores)]
                )
                store.start()
                stores.append(store)
    for store in stores:
        store.wait()


def merge(n, scale, b, a_list, bases, shapes, outs, pieces):
    fresh = outs is None
    rank, cols = a_list[0].shape[-2:]
    rows = sum(base.shape[1] for base in bases)
    stores = len(pieces) * sum(-(-base.shape[1] // TILE_ROWS) for base in bases)
    return pl.pallas_call(
        functools.partial(merge_kernel, n, pieces, scale, fresh),
        in_specs=[VMEM] * (3 + len(a_list) + 3) + [HBM] * (0 if fresh else 3),
        out_specs=[HBM] * 3,
        out_shape=shapes,
        scratch_shapes=[pltpu.VMEM((len(pieces), base.shape[1], cols), base.dtype) for base in bases]
        + [pltpu.SemaphoreType.DMA((stores,))],
        input_output_aliases={} if fresh else {6 + len(a_list) + i: i for i in range(3)},
        compiler_params=pltpu.CompilerParams(vmem_limit_bytes=16 * MIB),
        cost_estimate=pl.CostEstimate(
            flops=2 * len(pieces) * rows * cols * rank,
            bytes_accessed=4 * len(pieces) * rows * cols,
            transcendentals=0,
        ),
    )(*b, *a_list, *(bases if fresh else [in_vmem(base) for base in bases]), *([] if fresh else outs))

def per_device(
    n,
    owners,
    base_query,
    base_key,
    base_value,
    left_shared_matrix,
    right_queries_matrix,
    right_keys_matrix,
    right_values_matrix,
):
    layers, projs, rank, cols = left_shared_matrix.shape[1:]
    scale = numerator_gain / rank
    bases = (base_query, base_key, base_value)
    rights = (right_queries_matrix, right_keys_matrix, right_values_matrix)
    last = n // 2

    own_a = left_shared_matrix[0]
    own_b = [jnp.swapaxes(right[0], 1, 2) for right in rights]

    if cols % LANES == 0:
        tie = lax.optimization_barrier
        shapes = [jax.ShapeDtypeStruct(base.shape, base.dtype) for base in bases]
        pieces = [(0, True, True), (0, True, False)]
        key_block = fetch_blocks(n, cols, [base_key], pieces)
        other_a, key_block = tie((swap_cores(own_a), key_block))
        first, second = choose_a(owners, own_a, other_a)
        other_b = [swap_cores(x) for x in own_b]
        second, other_b[1] = tie((second, other_b[1]))
        held = [first, second]
        first = ring_pass(first, n)
        second = ring_pass(second, n)
        b, blocks = choose_b(n, cols, owners, own_b, other_b, [base_query, base_value], pieces)
        first, b = tie((first, b))
        outs = merge(n, scale, b, held, [blocks[0], key_block[0], blocks[1]], shapes, None, pieces)

        def go(pieces, chunks, outs):
            return merge(n, scale, b, chunks, bases, shapes, outs, pieces)

        waiting = None
        for step in range(1, last):
            if step > 1:
                outs = go(*waiting, outs)
            pieces = [(step, True, True), (step, False, False)]
            chunks = [first, swap_cores(first)]
            first = ring_pass(first, n)
            second, outs = tie((second, outs))
            waiting = [(step, True, False), (step, False, True)], [second, swap_cores(second)]
            if step == last - 1:
                pieces, chunks = pieces + waiting[0][:1], chunks + waiting[1][:1]
            outs = go(pieces, chunks, outs)
            first, outs = tie((first, outs))
            if step < last - 1:
                second = ring_pass(second, n)
        swapped = swap_cores(first)
        outs = go([waiting[0][1], (last, True, True)], [waiting[1][1], first], outs)
        return tuple(go([(last, False, False)], [swapped], outs))

    core = lax.axis_index("rollout")
    tensor = lax.axis_index("tensor")
    mine = owners == core
    a = jnp.where(mine[:, :, None, None], own_a, swap_cores(own_a))
    b = [jnp.where(mine[:, proj, None, None], x, swap_cores(x)) for proj, x in enumerate(own_b)]
    full = jnp.zeros((layers, projs, rank, n * cols), own_a.dtype)

    def put(full, piece, layer, step, from_core):
        start = place_of(n, step, from_core, tensor) * cols
        return lax.dynamic_update_slice(full, piece[None], (layer, 0, 0, start))

    first = jnp.where(core == 0, a[0], a[1])
    second = jnp.where(core == 0, a[1], a[0])
    full = put(full, first, core, 0, core)
    full = put(full, second, 1 - core, 0, core)
    for step in range(1, last + 1):
        first = ring_pass(first, n)
        full = put(full, first, core, step, core)
        full = put(full, swap_cores(first), 1 - core, step, 1 - core)
        if step < last:
            second = ring_pass(second, n)
            full = put(full, second, 1 - core, step, core)
            full = put(full, swap_cores(second), core, step, 1 - core)
    merged = []
    for proj in range(projs):
        delta = jnp.einsum("lkr,lkc->lrc", b[proj], full[:, proj], preferred_element_type=jnp.float32)
        merged.append((bases[proj].astype(jnp.float32) + scale * delta).astype(jnp.bfloat16))
    return tuple(merged)


def solution(mesh):
    return jax.shard_map(
        functools.partial(per_device, mesh.shape["tensor"]),
        mesh=mesh,
        in_specs=(
            P("copies", None),
            P("copies", "tensor", None),
            P("copies", "tensor", None),
            P("copies", "tensor", None),
            P("rollout", "copies", None, None, "tensor"),
            P("rollout", "copies", "tensor", None),
            P("rollout", "copies", "tensor", None),
            P("rollout", "copies", "tensor", None),
        ),
        out_specs=(
            P("copies", "tensor", None),
            P("copies", "tensor", None),
            P("copies", "tensor", None),
        ),
        check_vma=False,
    )
```

```python
import functools

import jax
import jax.numpy as jnp
from jax import lax
from jax.experimental import pallas as pl
from jax.experimental.pallas import tpu as pltpu
from jax.sharding import PartitionSpec as P

numerator_gain = 16.0
LANES = 128
MIB = 1024 * 1024
TILE_ROWS = 128
TILE_COLS = 256
VMEM = pl.BlockSpec(memory_space=pltpu.VMEM)
HBM = pl.BlockSpec(memory_space=pltpu.HBM)
ANY = pl.BlockSpec(memory_space=pl.ANY)


def in_hbm(array):
    return pltpu.with_memory_space_constraint(array, pltpu.HBM)


def in_vmem(array):
    return pltpu.with_memory_space_constraint(array, pltpu.VMEM)


def ring_order(n):
    return list(range(0, n, 2)) + list(range(n - 1, 0, -2))


def ring_pass(array, n):
    order = ring_order(n)
    pairs = []
    for k in range(n):
        pairs.append((order[k], order[(k + 1) % n]))
        pairs.append((n + order[k], n + order[(k - 1) % n]))
    return lax.ppermute(array, ("rollout", "tensor"), pairs)


def swap_cores(array):
    return lax.ppermute(array, "rollout", [(0, 1), (1, 0)])


def place_of(n, step, from_core, tensor):
    position = jnp.where(tensor % 2 == 0, tensor // 2, n - 1 - tensor // 2)
    k = position + jnp.where(from_core == 0, -step, step)
    k = jnp.where(k < 0, k + n, jnp.where(k >= n, k - n, k))
    return jnp.where(k < n // 2, 2 * k, 2 * n - 1 - 2 * k)


def column_starts(n, pieces, cols):
    core = lax.axis_index("rollout")
    tensor = lax.axis_index("tensor")
    blocks = []
    for step, own_ring, own_layer in pieces:
        place = place_of(n, step, core if own_ring else 1 - core, tensor)
        blocks.append((core if own_layer else 1 - core, pl.multiple_of(place * cols, LANES)))
    return blocks


def owned(owners, layer, proj, core, shape):
    return jnp.broadcast_to(owners[pl.ds(layer, 1), proj : proj + 1] == core, shape)


def choose_a_kernel(owners, own, other, first, second):
    core = lax.axis_index("rollout")
    for out, layer in ((first, core), (second, 1 - core)):
        for proj in range(own.shape[1]):
            mine = owned(owners, layer, proj, core, out.shape[1:])
            out[proj] = jnp.where(mine, own[layer, proj], other[layer, proj])


def choose_a(owners, own, other):
    piece = jax.ShapeDtypeStruct(own.shape[1:], own.dtype)
    return pl.pallas_call(
        choose_a_kernel,
        in_specs=[VMEM, VMEM, VMEM],
        out_specs=[VMEM, VMEM],
        out_shape=[piece, piece],
        compiler_params=pltpu.CompilerParams(vmem_limit_bytes=4 * MIB),
    )(in_vmem(owners), in_vmem(own), other)


def start_fetches(n, pieces, bases, blocks, sems):
    cols = blocks[0].shape[2]
    fetches = []
    for i, (layer, start) in enumerate(column_starts(n, pieces, cols)):
        for base, block in zip(bases, blocks):
            source = base.at[layer, :, pl.ds(start, cols)]
            fetches.append(pltpu.make_async_copy(source, block.at[i], sems.at[len(fetches)]))
            fetches[-1].start()
    return fetches


def block_shapes(bases, pieces, cols):
    return [jax.ShapeDtypeStruct((len(pieces), base.shape[1], cols), base.dtype) for base in bases]


def moved(shapes):
    size = sum(x.size * x.dtype.itemsize for x in shapes)
    return pl.CostEstimate(flops=0, bytes_accessed=2 * size, transcendentals=0)


def fetch_kernel(n, pieces, *refs):
    count = len(refs) // 2
    for fetch in start_fetches(n, pieces, refs[:count], refs[count:-1], refs[-1]):
        fetch.wait()


def fetch_blocks(n, cols, bases, pieces):
    blocks = block_shapes(bases, pieces, cols)
    return pl.pallas_call(
        functools.partial(fetch_kernel, n, pieces),
        in_specs=[HBM] * len(bases),
        out_specs=[VMEM] * len(bases),
        out_shape=blocks,
        scratch_shapes=[pltpu.SemaphoreType.DMA((len(bases) * len(pieces),))],
        compiler_params=pltpu.CompilerParams(vmem_limit_bytes=4 * MIB),
        cost_estimate=moved(blocks),
    )(*[in_hbm(base) for base in bases])


def choose_b_kernel(n, pieces, owners, *refs):
    core = lax.axis_index("rollout")
    own, other, refs, sems = refs[0:3], refs[3:6], refs[6:-1], refs[-1]
    count = (len(refs) - 3) // 2
    bases, outs, blocks = refs[:count], refs[count : count + 3], refs[count + 3 :]
    fetches = start_fetches(n, pieces, bases, blocks, sems)
    for proj in range(3):
        for layer in range(own[proj].shape[0]):
            mine = owned(owners, layer, proj, core, own[proj].shape[1:])
            outs[proj][layer] = jnp.where(mine, own[proj][layer], other[proj][layer]).T
    for fetch in fetches:
        fetch.wait()


def choose_b(n, cols, owners, own, other, bases, pieces):
    chosen = [jax.ShapeDtypeStruct((x.shape[0], x.shape[2], x.shape[1]), x.dtype) for x in own]
    blocks = block_shapes(bases, pieces, cols)
    out = pl.pallas_call(
        functools.partial(choose_b_kernel, n, pieces),
        in_specs=[VMEM] * 7 + [HBM] * len(bases),
        out_specs=[VMEM] * (3 + len(blocks)),
        out_shape=chosen + blocks,
        scratch_shapes=[pltpu.SemaphoreType.DMA((len(bases) * len(pieces),))],
        compiler_params=pltpu.CompilerParams(vmem_limit_bytes=4 * MIB),
        cost_estimate=moved(blocks),
    )(in_vmem(owners), *[in_vmem(x) for x in own], *other, *[in_hbm(base) for base in bases])
    return out[:3], out[3:]


def merge_kernel(n, pieces, scale, fresh, *refs):
    count = len(pieces)
    b_refs, a_refs, bases = refs[0:3], refs[3 : 3 + count], refs[3 + count : 6 + count]
    at = 6 + count + (0 if fresh else 3)
    outs, bufs, sem = refs[at : at + 3], refs[at + 3 : at + 6], refs[at + 6]
    cols = a_refs[0].shape[-1]
    stores = []
    for i, (layer, start) in enumerate(column_starts(n, pieces, cols)):
        for proj in (1, 2, 0):
            for row in range(0, bufs[proj].shape[1], TILE_ROWS):
                rows = pl.ds(row, min(TILE_ROWS, bufs[proj].shape[1] - row))
                for col in range(0, cols, TILE_COLS):
                    width = min(TILE_COLS, cols - col)
                    tile = pl.ds(col, width) if fresh else pl.ds(pl.multiple_of(start + col, LANES), width)
                    delta = jnp.dot(
                        b_refs[proj][layer, rows],
                        a_refs[i][proj, :, col : col + width],
                        preferred_element_type=jnp.float32,
                    )
                    block = bases[proj][i if fresh else layer, rows, tile]
                    merged = block.astype(jnp.float32) + scale * delta
                    bufs[proj][i, rows, col : col + width] = merged.astype(jnp.bfloat16)
                store = pltpu.make_async_copy(
                    bufs[proj].at[i, rows], outs[proj].at[layer, rows, pl.ds(start, cols)], sem.at[len(stores)]
                )
                store.start()
                stores.append(store)
    for store in stores:
        store.wait()


def merge(n, scale, b, a_list, bases, shapes, outs, pieces):
    fresh = outs is None
    rank, cols = a_list[0].shape[-2:]
    rows = sum(base.shape[1] for base in bases)
    stores = len(pieces) * sum(-(-base.shape[1] // TILE_ROWS) for base in bases)
    return pl.pallas_call(
        functools.partial(merge_kernel, n, pieces, scale, fresh),
        in_specs=[VMEM] * (3 + len(a_list) + 3) + [HBM] * (0 if fresh else 3),
        out_specs=[HBM] * 3,
        out_shape=shapes,
        scratch_shapes=[pltpu.VMEM((len(pieces), base.shape[1], cols), base.dtype) for base in bases]
        + [pltpu.SemaphoreType.DMA((stores,))],
        input_output_aliases={} if fresh else {6 + len(a_list) + i: i for i in range(3)},
        compiler_params=pltpu.CompilerParams(vmem_limit_bytes=16 * MIB),
        cost_estimate=pl.CostEstimate(
            flops=2 * len(pieces) * rows * cols * rank,
            bytes_accessed=4 * len(pieces) * rows * cols,
            transcendentals=0,
        ),
    )(*b, *a_list, *(bases if fresh else [in_vmem(base) for base in bases]), *([] if fresh else outs))

def per_device(
    n,
    owners,
    base_query,
    base_key,
    base_value,
    left_shared_matrix,
    right_queries_matrix,
    right_keys_matrix,
    right_values_matrix,
):
    layers, projs, rank, cols = left_shared_matrix.shape[1:]
    scale = numerator_gain / rank
    bases = (base_query, base_key, base_value)
    rights = (right_queries_matrix, right_keys_matrix, right_values_matrix)
    last = n // 2

    own_a = left_shared_matrix[0]
    own_b = [jnp.swapaxes(right[0], 1, 2) for right in rights]

    if cols % LANES == 0:
        tie = lax.optimization_barrier
        shapes = [jax.ShapeDtypeStruct(base.shape, base.dtype) for base in bases]
        pieces = [(0, True, True), (0, True, False)]
        query_block = fetch_blocks(n, cols, [base_query], pieces)
        other_a, query_block = tie((swap_cores(own_a), query_block))
        first, second = choose_a(owners, own_a, other_a)
        other_b = [swap_cores(x) for x in own_b]
        second, other_b[1] = tie((second, other_b[1]))
        held = [first, second]
        first = ring_pass(first, n)
        second = ring_pass(second, n)
        b, blocks = choose_b(n, cols, owners, own_b, other_b, [base_key, base_value], pieces)
        first, b = tie((first, b))
        outs = merge(n, scale, b, held, [*query_block, *blocks], shapes, None, pieces)

        def go(pieces, chunks, outs):
            return merge(n, scale, b, chunks, bases, shapes, outs, pieces)

        waiting = None
        for step in range(1, last):
            if step > 1:
                outs = go(*waiting, outs)
            pieces = [(step, True, True), (step, False, False)]
            chunks = [first, swap_cores(first)]
            first = ring_pass(first, n)
            second, outs = tie((second, outs))
            waiting = [(step, True, False), (step, False, True)], [second, swap_cores(second)]
            if step == last - 1:
                pieces, chunks = pieces + waiting[0][:1], chunks + waiting[1][:1]
            outs = go(pieces, chunks, outs)
            first, outs = tie((first, outs))
            if step < last - 1:
                second = ring_pass(second, n)
        swapped = swap_cores(first)
        outs = go([waiting[0][1], (last, True, True)], [waiting[1][1], first], outs)
        return tuple(go([(last, False, False)], [swapped], outs))

    core = lax.axis_index("rollout")
    tensor = lax.axis_index("tensor")
    mine = owners == core
    a = jnp.where(mine[:, :, None, None], own_a, swap_cores(own_a))
    b = [jnp.where(mine[:, proj, None, None], x, swap_cores(x)) for proj, x in enumerate(own_b)]
    full = jnp.zeros((layers, projs, rank, n * cols), own_a.dtype)

    def put(full, piece, layer, step, from_core):
        start = place_of(n, step, from_core, tensor) * cols
        return lax.dynamic_update_slice(full, piece[None], (layer, 0, 0, start))

    first = jnp.where(core == 0, a[0], a[1])
    second = jnp.where(core == 0, a[1], a[0])
    full = put(full, first, core, 0, core)
    full = put(full, second, 1 - core, 0, core)
    for step in range(1, last + 1):
        first = ring_pass(first, n)
        full = put(full, first, core, step, core)
        full = put(full, swap_cores(first), 1 - core, step, 1 - core)
        if step < last:
            second = ring_pass(second, n)
            full = put(full, second, 1 - core, step, core)
            full = put(full, swap_cores(second), core, step, 1 - core)
    merged = []
    for proj in range(projs):
        delta = jnp.einsum("lkr,lkc->lrc", b[proj], full[:, proj], preferred_element_type=jnp.float32)
        merged.append((bases[proj].astype(jnp.float32) + scale * delta).astype(jnp.bfloat16))
    return tuple(merged)


def solution(mesh):
    return jax.shard_map(
        functools.partial(per_device, mesh.shape["tensor"]),
        mesh=mesh,
        in_specs=(
            P("copies", None),
            P("copies", "tensor", None),
            P("copies", "tensor", None),
            P("copies", "tensor", None),
            P("rollout", "copies", None, None, "tensor"),
            P("rollout", "copies", "tensor", None),
            P("rollout", "copies", "tensor", None),
            P("rollout", "copies", "tensor", None),
        ),
        out_specs=(
            P("copies", "tensor", None),
            P("copies", "tensor", None),
            P("copies", "tensor", None),
        ),
        check_vma=False,
    )
```

```python
import functools

import jax
import jax.numpy as jnp
from jax import lax
from jax.experimental import pallas as pl
from jax.experimental.pallas import tpu as pltpu
from jax.sharding import PartitionSpec as P

numerator_gain = 16.0
LANES = 128
MIB = 1024 * 1024
TILE_ROWS = 128
TILE_COLS = 256
VMEM = pl.BlockSpec(memory_space=pltpu.VMEM)
HBM = pl.BlockSpec(memory_space=pltpu.HBM)
ANY = pl.BlockSpec(memory_space=pl.ANY)


def in_hbm(array):
    return pltpu.with_memory_space_constraint(array, pltpu.HBM)


def in_vmem(array):
    return pltpu.with_memory_space_constraint(array, pltpu.VMEM)


def ring_order(n):
    return list(range(0, n, 2)) + list(range(n - 1, 0, -2))


def ring_pass(array, n):
    order = ring_order(n)
    pairs = []
    for k in range(n):
        up, down = k % 2, 1 - k % 2
        pairs.append((up * n + order[k], (1 - up) * n + order[(k + 1) % n]))
        pairs.append((down * n + order[k], (1 - down) * n + order[(k - 1) % n]))
    return lax.ppermute(array, ("rollout", "tensor"), pairs)


def swap_cores(array):
    return lax.ppermute(array, "rollout", [(0, 1), (1, 0)])


def place_of(n, step, from_core, tensor):
    position = jnp.where(tensor % 2 == 0, tensor // 2, n - 1 - tensor // 2)
    k = position + jnp.where(from_core == position % 2, -step, step)
    k = jnp.where(k < 0, k + n, jnp.where(k >= n, k - n, k))
    return jnp.where(k < n // 2, 2 * k, 2 * n - 1 - 2 * k)


def column_starts(n, pieces, cols):
    core = lax.axis_index("rollout")
    tensor = lax.axis_index("tensor")
    blocks = []
    for step, own_ring, own_layer in pieces:
        place = place_of(n, step, core if own_ring else 1 - core, tensor)
        blocks.append((core if own_layer else 1 - core, pl.multiple_of(place * cols, LANES)))
    return blocks


def owned(owners, layer, proj, core, shape):
    return jnp.broadcast_to(owners[pl.ds(layer, 1), proj : proj + 1] == core, shape)


def choose_a_kernel(owners, own, other, first, second):
    core = lax.axis_index("rollout")
    for out, layer in ((first, core), (second, 1 - core)):
        for proj in range(own.shape[1]):
            mine = owned(owners, layer, proj, core, out.shape[1:])
            out[proj] = jnp.where(mine, own[layer, proj], other[layer, proj])


def choose_a(owners, own, other):
    piece = jax.ShapeDtypeStruct(own.shape[1:], own.dtype)
    return pl.pallas_call(
        choose_a_kernel,
        in_specs=[VMEM, VMEM, VMEM],
        out_specs=[VMEM, VMEM],
        out_shape=[piece, piece],
        compiler_params=pltpu.CompilerParams(vmem_limit_bytes=4 * MIB),
    )(in_vmem(owners), in_vmem(own), other)


def start_fetches(n, pieces, bases, blocks, sems):
    cols = blocks[0].shape[2]
    fetches = []
    for i, (layer, start) in enumerate(column_starts(n, pieces, cols)):
        for base, block in zip(bases, blocks):
            source = base.at[layer, :, pl.ds(start, cols)]
            fetches.append(pltpu.make_async_copy(source, block.at[i], sems.at[len(fetches)]))
            fetches[-1].start()
    return fetches


def block_shapes(bases, pieces, cols):
    return [jax.ShapeDtypeStruct((len(pieces), base.shape[1], cols), base.dtype) for base in bases]


def moved(shapes):
    size = sum(x.size * x.dtype.itemsize for x in shapes)
    return pl.CostEstimate(flops=0, bytes_accessed=2 * size, transcendentals=0)


def fetch_kernel(n, pieces, *refs):
    count = len(refs) // 2
    for fetch in start_fetches(n, pieces, refs[:count], refs[count:-1], refs[-1]):
        fetch.wait()


def fetch_blocks(n, cols, bases, pieces):
    blocks = block_shapes(bases, pieces, cols)
    return pl.pallas_call(
        functools.partial(fetch_kernel, n, pieces),
        in_specs=[HBM] * len(bases),
        out_specs=[VMEM] * len(bases),
        out_shape=blocks,
        scratch_shapes=[pltpu.SemaphoreType.DMA((len(bases) * len(pieces),))],
        compiler_params=pltpu.CompilerParams(vmem_limit_bytes=4 * MIB),
        cost_estimate=moved(blocks),
    )(*[in_hbm(base) for base in bases])


def choose_b_kernel(n, pieces, owners, *refs):
    core = lax.axis_index("rollout")
    own, other, refs, sems = refs[0:3], refs[3:6], refs[6:-1], refs[-1]
    count = (len(refs) - 3) // 2
    bases, outs, blocks = refs[:count], refs[count : count + 3], refs[count + 3 :]
    fetches = start_fetches(n, pieces, bases, blocks, sems)
    for proj in range(3):
        for layer in range(own[proj].shape[0]):
            mine = owned(owners, layer, proj, core, own[proj].shape[1:])
            outs[proj][layer] = jnp.where(mine, own[proj][layer], other[proj][layer]).T
    for fetch in fetches:
        fetch.wait()


def choose_b(n, cols, owners, own, other, bases, pieces):
    chosen = [jax.ShapeDtypeStruct((x.shape[0], x.shape[2], x.shape[1]), x.dtype) for x in own]
    blocks = block_shapes(bases, pieces, cols)
    out = pl.pallas_call(
        functools.partial(choose_b_kernel, n, pieces),
        in_specs=[VMEM] * 7 + [HBM] * len(bases),
        out_specs=[VMEM] * (3 + len(blocks)),
        out_shape=chosen + blocks,
        scratch_shapes=[pltpu.SemaphoreType.DMA((len(bases) * len(pieces),))],
        compiler_params=pltpu.CompilerParams(vmem_limit_bytes=4 * MIB),
        cost_estimate=moved(blocks),
    )(in_vmem(owners), *[in_vmem(x) for x in own], *other, *[in_hbm(base) for base in bases])
    return out[:3], out[3:]


def merge_kernel(n, pieces, scale, fresh, *refs):
    count = len(pieces)
    b_refs, a_refs, bases = refs[0:3], refs[3 : 3 + count], refs[3 + count : 6 + count]
    at = 6 + count + (0 if fresh else 3)
    outs, bufs, sem = refs[at : at + 3], refs[at + 3 : at + 6], refs[at + 6]
    cols = a_refs[0].shape[-1]
    stores = []
    for i, (layer, start) in enumerate(column_starts(n, pieces, cols)):
        for proj in (1, 2, 0):
            for row in range(0, bufs[proj].shape[1], TILE_ROWS):
                rows = pl.ds(row, min(TILE_ROWS, bufs[proj].shape[1] - row))
                for col in range(0, cols, TILE_COLS):
                    width = min(TILE_COLS, cols - col)
                    tile = pl.ds(col, width) if fresh else pl.ds(pl.multiple_of(start + col, LANES), width)
                    delta = jnp.dot(
                        b_refs[proj][layer, rows],
                        a_refs[i][proj, :, col : col + width],
                        preferred_element_type=jnp.float32,
                    )
                    block = bases[proj][i if fresh else layer, rows, tile]
                    merged = block.astype(jnp.float32) + scale * delta
                    bufs[proj][i, rows, col : col + width] = merged.astype(jnp.bfloat16)
                store = pltpu.make_async_copy(
                    bufs[proj].at[i, rows], outs[proj].at[layer, rows, pl.ds(start, cols)], sem.at[len(stores)]
                )
                store.start()
                stores.append(store)
    for store in stores:
        store.wait()


def merge(n, scale, b, a_list, bases, shapes, outs, pieces):
    fresh = outs is None
    rank, cols = a_list[0].shape[-2:]
    rows = sum(base.shape[1] for base in bases)
    stores = len(pieces) * sum(-(-base.shape[1] // TILE_ROWS) for base in bases)
    return pl.pallas_call(
        functools.partial(merge_kernel, n, pieces, scale, fresh),
        in_specs=[VMEM] * (3 + len(a_list) + 3) + [HBM] * (0 if fresh else 3),
        out_specs=[HBM] * 3,
        out_shape=shapes,
        scratch_shapes=[pltpu.VMEM((len(pieces), base.shape[1], cols), base.dtype) for base in bases]
        + [pltpu.SemaphoreType.DMA((stores,))],
        input_output_aliases={} if fresh else {6 + len(a_list) + i: i for i in range(3)},
        compiler_params=pltpu.CompilerParams(vmem_limit_bytes=16 * MIB),
        cost_estimate=pl.CostEstimate(
            flops=2 * len(pieces) * rows * cols * rank,
            bytes_accessed=4 * len(pieces) * rows * cols,
            transcendentals=0,
        ),
    )(*b, *a_list, *(bases if fresh else [in_vmem(base) for base in bases]), *([] if fresh else outs))

def per_device(
    n,
    owners,
    base_query,
    base_key,
    base_value,
    left_shared_matrix,
    right_queries_matrix,
    right_keys_matrix,
    right_values_matrix,
):
    layers, projs, rank, cols = left_shared_matrix.shape[1:]
    scale = numerator_gain / rank
    bases = (base_query, base_key, base_value)
    rights = (right_queries_matrix, right_keys_matrix, right_values_matrix)
    last = n // 2

    own_a = left_shared_matrix[0]
    own_b = [jnp.swapaxes(right[0], 1, 2) for right in rights]

    if cols % LANES == 0:
        tie = lax.optimization_barrier
        shapes = [jax.ShapeDtypeStruct(base.shape, base.dtype) for base in bases]
        pieces = [(0, True, True), (0, True, False)]
        query_block = fetch_blocks(n, cols, [base_query], pieces)
        other_a, query_block = tie((swap_cores(own_a), query_block))
        first, second = choose_a(owners, own_a, other_a)
        other_b = [swap_cores(x) for x in own_b]
        second, other_b[1] = tie((second, other_b[1]))
        held = [first, second]
        first = ring_pass(first, n)
        second = ring_pass(second, n)
        b, blocks = choose_b(n, cols, owners, own_b, other_b, [base_key, base_value], pieces)
        first, b = tie((first, b))
        outs = merge(n, scale, b, held, [*query_block, *blocks], shapes, None, pieces)

        def go(pieces, chunks, outs):
            return merge(n, scale, b, chunks, bases, shapes, outs, pieces)

        waiting = None
        for step in range(1, last):
            if step > 1:
                outs = go(*waiting, outs)
            even = step % 2 == 0
            pieces = [(step, True, even), (step, False, not even)]
            chunks = [first, swap_cores(first)]
            first = ring_pass(first, n)
            second, outs = tie((second, outs))
            waiting = [(step, True, not even), (step, False, even)], [second, swap_cores(second)]
            if step == last - 1:
                pieces, chunks = pieces + waiting[0][:1], chunks + waiting[1][:1]
            outs = go(pieces, chunks, outs)
            first, outs = tie((first, outs))
            if step < last - 1:
                second = ring_pass(second, n)
        swapped = swap_cores(first)
        even = last % 2 == 0
        outs = go([waiting[0][1], (last, True, even)], [waiting[1][1], first], outs)
        return tuple(go([(last, False, not even)], [swapped], outs))

    core = lax.axis_index("rollout")
    tensor = lax.axis_index("tensor")
    mine = owners == core
    a = jnp.where(mine[:, :, None, None], own_a, swap_cores(own_a))
    b = [jnp.where(mine[:, proj, None, None], x, swap_cores(x)) for proj, x in enumerate(own_b)]
    full = jnp.zeros((layers, projs, rank, n * cols), own_a.dtype)

    def put(full, piece, layer, step, from_core):
        start = place_of(n, step, from_core, tensor) * cols
        return lax.dynamic_update_slice(full, piece[None], (layer, 0, 0, start))

    first = jnp.where(core == 0, a[0], a[1])
    second = jnp.where(core == 0, a[1], a[0])
    full = put(full, first, core, 0, core)
    full = put(full, second, 1 - core, 0, core)
    for step in range(1, last + 1):
        layer = (core + step) % 2
        first = ring_pass(first, n)
        full = put(full, first, layer, step, core)
        full = put(full, swap_cores(first), 1 - layer, step, 1 - core)
        if step < last:
            second = ring_pass(second, n)
            full = put(full, second, 1 - layer, step, core)
            full = put(full, swap_cores(second), layer, step, 1 - core)
    merged = []
    for proj in range(projs):
        delta = jnp.einsum("lkr,lkc->lrc", b[proj], full[:, proj], preferred_element_type=jnp.float32)
        merged.append((bases[proj].astype(jnp.float32) + scale * delta).astype(jnp.bfloat16))
    return tuple(merged)


def solution(mesh):
    return jax.shard_map(
        functools.partial(per_device, mesh.shape["tensor"]),
        mesh=mesh,
        in_specs=(
            P("copies", None),
            P("copies", "tensor", None),
            P("copies", "tensor", None),
            P("copies", "tensor", None),
            P("rollout", "copies", None, None, "tensor"),
            P("rollout", "copies", "tensor", None),
            P("rollout", "copies", "tensor", None),
            P("rollout", "copies", "tensor", None),
        ),
        out_specs=(
            P("copies", "tensor", None),
            P("copies", "tensor", None),
            P("copies", "tensor", None),
        ),
        check_vma=False,
    )
```

```python
import functools

import jax
import jax.numpy as jnp
from jax import lax
from jax.experimental import pallas as pl
from jax.experimental.pallas import tpu as pltpu
from jax.sharding import PartitionSpec as P

numerator_gain = 16.0
LANES = 128
MIB = 1024 * 1024
TILE_ROWS = 128
TILE_COLS = 256
VMEM = pl.BlockSpec(memory_space=pltpu.VMEM)
HBM = pl.BlockSpec(memory_space=pltpu.HBM)
ANY = pl.BlockSpec(memory_space=pl.ANY)


def in_hbm(array):
    return pltpu.with_memory_space_constraint(array, pltpu.HBM)


def in_vmem(array):
    return pltpu.with_memory_space_constraint(array, pltpu.VMEM)


def ring_order(n):
    return list(range(0, n, 2)) + list(range(n - 1, 0, -2))


def ring_pass(array, n):
    order = ring_order(n)
    pairs = []
    for k in range(n):
        up, down = k % 2, 1 - k % 2
        pairs.append((up * n + order[k], (1 - up) * n + order[(k + 1) % n]))
        pairs.append((down * n + order[k], (1 - down) * n + order[(k - 1) % n]))
    return lax.ppermute(array, ("rollout", "tensor"), pairs)


def swap_cores(array):
    return lax.ppermute(array, "rollout", [(0, 1), (1, 0)])


def place_of(n, step, from_core, tensor):
    position = jnp.where(tensor % 2 == 0, tensor // 2, n - 1 - tensor // 2)
    k = position + jnp.where(from_core == position % 2, -step, step)
    k = jnp.where(k < 0, k + n, jnp.where(k >= n, k - n, k))
    return jnp.where(k < n // 2, 2 * k, 2 * n - 1 - 2 * k)


def column_starts(n, pieces, cols):
    core = lax.axis_index("rollout")
    tensor = lax.axis_index("tensor")
    blocks = []
    for step, own_ring, own_layer in pieces:
        place = place_of(n, step, core if own_ring else 1 - core, tensor)
        blocks.append((core if own_layer else 1 - core, pl.multiple_of(place * cols, LANES)))
    return blocks


def owned(owners, layer, proj, core, shape):
    return jnp.broadcast_to(owners[pl.ds(layer, 1), proj : proj + 1] == core, shape)


def choose_a_kernel(owners, own, other, first, second):
    core = lax.axis_index("rollout")
    for out, layer in ((first, core), (second, 1 - core)):
        for proj in range(own.shape[1]):
            mine = owned(owners, layer, proj, core, out.shape[1:])
            out[proj] = jnp.where(mine, own[layer, proj], other[layer, proj])


def choose_a(owners, own, other):
    piece = jax.ShapeDtypeStruct(own.shape[1:], own.dtype)
    return pl.pallas_call(
        choose_a_kernel,
        in_specs=[VMEM, VMEM, VMEM],
        out_specs=[VMEM, VMEM],
        out_shape=[piece, piece],
        compiler_params=pltpu.CompilerParams(vmem_limit_bytes=4 * MIB),
    )(in_vmem(owners), in_vmem(own), other)


def start_fetches(n, pieces, bases, blocks, sems):
    cols = blocks[0].shape[2]
    fetches = []
    for i, (layer, start) in enumerate(column_starts(n, pieces, cols)):
        for base, block in zip(bases, blocks):
            source = base.at[layer, :, pl.ds(start, cols)]
            fetches.append(pltpu.make_async_copy(source, block.at[i], sems.at[len(fetches)]))
            fetches[-1].start()
    return fetches


def block_shapes(bases, pieces, cols):
    return [jax.ShapeDtypeStruct((len(pieces), base.shape[1], cols), base.dtype) for base in bases]


def moved(shapes):
    size = sum(x.size * x.dtype.itemsize for x in shapes)
    return pl.CostEstimate(flops=0, bytes_accessed=2 * size, transcendentals=0)


def fetch_kernel(n, pieces, *refs):
    count = len(refs) // 2
    for fetch in start_fetches(n, pieces, refs[:count], refs[count:-1], refs[-1]):
        fetch.wait()


def fetch_blocks(n, cols, bases, pieces):
    blocks = block_shapes(bases, pieces, cols)
    return pl.pallas_call(
        functools.partial(fetch_kernel, n, pieces),
        in_specs=[HBM] * len(bases),
        out_specs=[VMEM] * len(bases),
        out_shape=blocks,
        scratch_shapes=[pltpu.SemaphoreType.DMA((len(bases) * len(pieces),))],
        compiler_params=pltpu.CompilerParams(vmem_limit_bytes=4 * MIB),
        cost_estimate=moved(blocks),
    )(*[in_hbm(base) for base in bases])


def choose_b_kernel(n, pieces, owners, *refs):
    core = lax.axis_index("rollout")
    own, other, refs, sems = refs[0:3], refs[3:6], refs[6:-1], refs[-1]
    count = (len(refs) - 3) // 2
    bases, outs, blocks = refs[:count], refs[count : count + 3], refs[count + 3 :]
    fetches = start_fetches(n, pieces, bases, blocks, sems)
    for proj in range(3):
        for layer in range(own[proj].shape[0]):
            mine = owned(owners, layer, proj, core, own[proj].shape[1:])
            outs[proj][layer] = jnp.where(mine, own[proj][layer], other[proj][layer]).T
    for fetch in fetches:
        fetch.wait()


def choose_b(n, cols, owners, own, other, bases, pieces):
    chosen = [jax.ShapeDtypeStruct((x.shape[0], x.shape[2], x.shape[1]), x.dtype) for x in own]
    blocks = block_shapes(bases, pieces, cols)
    out = pl.pallas_call(
        functools.partial(choose_b_kernel, n, pieces),
        in_specs=[VMEM] * 7 + [HBM] * len(bases),
        out_specs=[VMEM] * (3 + len(blocks)),
        out_shape=chosen + blocks,
        scratch_shapes=[pltpu.SemaphoreType.DMA((len(bases) * len(pieces),))],
        compiler_params=pltpu.CompilerParams(vmem_limit_bytes=4 * MIB),
        cost_estimate=moved(blocks),
    )(in_vmem(owners), *[in_vmem(x) for x in own], *other, *[in_hbm(base) for base in bases])
    return out[:3], out[3:]


def merge_kernel(n, pieces, scale, fresh, *refs):
    count = len(pieces)
    b_refs, a_refs, bases = refs[0:3], refs[3 : 3 + count], refs[3 + count : 6 + count]
    at = 6 + count + (0 if fresh else 3)
    outs, bufs, sem = refs[at : at + 3], refs[at + 3 : at + 6], refs[at + 6]
    cols = a_refs[0].shape[-1]
    stores = []
    for i, (layer, start) in enumerate(column_starts(n, pieces, cols)):
        for proj in (1, 2, 0):
            for row in range(0, bufs[proj].shape[1], TILE_ROWS):
                rows = pl.ds(row, min(TILE_ROWS, bufs[proj].shape[1] - row))
                for col in range(0, cols, TILE_COLS):
                    width = min(TILE_COLS, cols - col)
                    tile = pl.ds(col, width) if fresh else pl.ds(pl.multiple_of(start + col, LANES), width)
                    delta = jnp.dot(
                        b_refs[proj][layer, rows],
                        a_refs[i][proj, :, col : col + width],
                        preferred_element_type=jnp.float32,
                    )
                    block = bases[proj][i if fresh else layer, rows, tile]
                    merged = block.astype(jnp.float32) + scale * delta
                    bufs[proj][i, rows, col : col + width] = merged.astype(jnp.bfloat16)
                store = pltpu.make_async_copy(
                    bufs[proj].at[i, rows], outs[proj].at[layer, rows, pl.ds(start, cols)], sem.at[len(stores)]
                )
                store.start()
                stores.append(store)
    for store in stores:
        store.wait()


def merge(n, scale, b, a_list, bases, shapes, outs, pieces):
    fresh = outs is None
    rank, cols = a_list[0].shape[-2:]
    rows = sum(base.shape[1] for base in bases)
    stores = len(pieces) * sum(-(-base.shape[1] // TILE_ROWS) for base in bases)
    return pl.pallas_call(
        functools.partial(merge_kernel, n, pieces, scale, fresh),
        in_specs=[VMEM] * (3 + len(a_list) + 3) + [HBM] * (0 if fresh else 3),
        out_specs=[HBM] * 3,
        out_shape=shapes,
        scratch_shapes=[pltpu.VMEM((len(pieces), base.shape[1], cols), base.dtype) for base in bases]
        + [pltpu.SemaphoreType.DMA((stores,))],
        input_output_aliases={} if fresh else {6 + len(a_list) + i: i for i in range(3)},
        compiler_params=pltpu.CompilerParams(vmem_limit_bytes=16 * MIB),
        cost_estimate=pl.CostEstimate(
            flops=2 * len(pieces) * rows * cols * rank,
            bytes_accessed=4 * len(pieces) * rows * cols,
            transcendentals=0,
        ),
    )(*b, *a_list, *(bases if fresh else [in_vmem(base) for base in bases]), *([] if fresh else outs))

def per_device(
    n,
    owners,
    base_query,
    base_key,
    base_value,
    left_shared_matrix,
    right_queries_matrix,
    right_keys_matrix,
    right_values_matrix,
):
    layers, projs, rank, cols = left_shared_matrix.shape[1:]
    scale = numerator_gain / rank
    bases = (base_query, base_key, base_value)
    rights = (right_queries_matrix, right_keys_matrix, right_values_matrix)
    last = n // 2

    own_a = left_shared_matrix[0]
    own_b = [jnp.swapaxes(right[0], 1, 2) for right in rights]

    if cols % LANES == 0:
        tie = lax.optimization_barrier
        shapes = [jax.ShapeDtypeStruct(base.shape, base.dtype) for base in bases]
        pieces = [(0, True, True), (0, True, False)]
        query_block = fetch_blocks(n, cols, [base_query], pieces)
        other_a, query_block = tie((swap_cores(own_a), query_block))
        first, second = choose_a(owners, own_a, other_a)
        other_b = [swap_cores(x) for x in own_b]
        second, other_b[1] = tie((second, other_b[1]))
        held = [first, second]
        first = ring_pass(first, n)
        second = ring_pass(second, n)
        b, blocks = choose_b(n, cols, owners, own_b, other_b, [base_key, base_value], pieces)
        first, b = tie((first, b))
        outs = merge(n, scale, b, held, [*query_block, *blocks], shapes, None, pieces)

        def go(outs, *named):
            pieces = [(step, not swapped, ((step % 2 == 0) == (ring == "a")) != swapped) for step, ring, swapped, _ in named]
            return merge(n, scale, b, [chunk for *_, chunk in named], bases, shapes, outs, pieces)

        swapped_a = swapped_b = None
        for step in range(1, last):
            a_here = (step, "a", False, first)
            a_there = (step, "a", True, swap_cores(first))
            first = ring_pass(first, n)
            if step > 1:
                outs = go(outs, a_here, swapped_a)
            second, outs = tie((second, outs))
            b_here = (step, "b", False, second)
            b_there = (step, "b", True, swap_cores(second))
            if step < last - 1:
                second = ring_pass(second, n)
            batch = [b_here, a_here if step == 1 else swapped_b]
            outs = go(outs, *batch, *([a_there] if step == last - 1 else []))
            first, outs = tie((first, outs))
            swapped_a, swapped_b = a_there, b_there
        a_there = (last, "a", True, swap_cores(first))
        outs = go(outs, swapped_b, (last, "a", False, first))
        return tuple(go(outs, a_there))

    core = lax.axis_index("rollout")
    tensor = lax.axis_index("tensor")
    mine = owners == core
    a = jnp.where(mine[:, :, None, None], own_a, swap_cores(own_a))
    b = [jnp.where(mine[:, proj, None, None], x, swap_cores(x)) for proj, x in enumerate(own_b)]
    full = jnp.zeros((layers, projs, rank, n * cols), own_a.dtype)

    def put(full, piece, layer, step, from_core):
        start = place_of(n, step, from_core, tensor) * cols
        return lax.dynamic_update_slice(full, piece[None], (layer, 0, 0, start))

    first = jnp.where(core == 0, a[0], a[1])
    second = jnp.where(core == 0, a[1], a[0])
    full = put(full, first, core, 0, core)
    full = put(full, second, 1 - core, 0, core)
    for step in range(1, last + 1):
        layer = (core + step) % 2
        first = ring_pass(first, n)
        full = put(full, first, layer, step, core)
        full = put(full, swap_cores(first), 1 - layer, step, 1 - core)
        if step < last:
            second = ring_pass(second, n)
            full = put(full, second, 1 - layer, step, core)
            full = put(full, swap_cores(second), layer, step, 1 - core)
    merged = []
    for proj in range(projs):
        delta = jnp.einsum("lkr,lkc->lrc", b[proj], full[:, proj], preferred_element_type=jnp.float32)
        merged.append((bases[proj].astype(jnp.float32) + scale * delta).astype(jnp.bfloat16))
    return tuple(merged)


def solution(mesh):
    return jax.shard_map(
        functools.partial(per_device, mesh.shape["tensor"]),
        mesh=mesh,
        in_specs=(
            P("copies", None),
            P("copies", "tensor", None),
            P("copies", "tensor", None),
            P("copies", "tensor", None),
            P("rollout", "copies", None, None, "tensor"),
            P("rollout", "copies", "tensor", None),
            P("rollout", "copies", "tensor", None),
            P("rollout", "copies", "tensor", None),
        ),
        out_specs=(
            P("copies", "tensor", None),
            P("copies", "tensor", None),
            P("copies", "tensor", None),
        ),
        check_vma=False,
    )
```

```python
import functools

import jax
import jax.numpy as jnp
from jax import lax
from jax.experimental import pallas as pl
from jax.experimental.pallas import tpu as pltpu
from jax.sharding import PartitionSpec as P

numerator_gain = 16.0
LANES = 128
MIB = 1024 * 1024
TILE_ROWS = 160
TILE_COLS = 256
STORE_ROWS = 320
VMEM = pl.BlockSpec(memory_space=pltpu.VMEM)
HBM = pl.BlockSpec(memory_space=pltpu.HBM)
ANY = pl.BlockSpec(memory_space=pl.ANY)


def in_hbm(array):
    return pltpu.with_memory_space_constraint(array, pltpu.HBM)


def in_vmem(array):
    return pltpu.with_memory_space_constraint(array, pltpu.VMEM)


def ring_order(n):
    return list(range(0, n, 2)) + list(range(n - 1, 0, -2))


def ring_pass(array, n):
    order = ring_order(n)
    pairs = []
    for k in range(n):
        up, down = k % 2, 1 - k % 2
        pairs.append((up * n + order[k], (1 - up) * n + order[(k + 1) % n]))
        pairs.append((down * n + order[k], (1 - down) * n + order[(k - 1) % n]))
    return lax.ppermute(array, ("rollout", "tensor"), pairs)


def swap_cores(array):
    return lax.ppermute(array, "rollout", [(0, 1), (1, 0)])


def place_of(n, step, from_core, tensor):
    position = jnp.where(tensor % 2 == 0, tensor // 2, n - 1 - tensor // 2)
    k = position + jnp.where(from_core == position % 2, -step, step)
    k = jnp.where(k < 0, k + n, jnp.where(k >= n, k - n, k))
    return jnp.where(k < n // 2, 2 * k, 2 * n - 1 - 2 * k)


def column_starts(n, pieces, cols):
    core = lax.axis_index("rollout")
    tensor = lax.axis_index("tensor")
    blocks = []
    for step, own_ring, own_layer in pieces:
        place = place_of(n, step, core if own_ring else 1 - core, tensor)
        blocks.append((core if own_layer else 1 - core, pl.multiple_of(place * cols, LANES)))
    return blocks


def owned(owners, layer, proj, core, shape):
    return jnp.broadcast_to(owners[pl.ds(layer, 1), proj : proj + 1] == core, shape)


def choose_a_kernel(owners, own, other, first, second):
    core = lax.axis_index("rollout")
    for out, layer in ((first, core), (second, 1 - core)):
        for proj in range(own.shape[1]):
            mine = owned(owners, layer, proj, core, out.shape[1:])
            out[proj] = jnp.where(mine, own[layer, proj], other[layer, proj])


def choose_a(owners, own, other):
    piece = jax.ShapeDtypeStruct(own.shape[1:], own.dtype)
    return pl.pallas_call(
        choose_a_kernel,
        in_specs=[VMEM, VMEM, VMEM],
        out_specs=[VMEM, VMEM],
        out_shape=[piece, piece],
        compiler_params=pltpu.CompilerParams(vmem_limit_bytes=4 * MIB),
    )(in_vmem(owners), in_vmem(own), other)


def start_fetches(n, pieces, bases, blocks, sems):
    cols = blocks[0].shape[2]
    fetches = []
    for i, (layer, start) in enumerate(column_starts(n, pieces, cols)):
        for base, block in zip(bases, blocks):
            source = base.at[layer, :, pl.ds(start, cols)]
            fetches.append(pltpu.make_async_copy(source, block.at[i], sems.at[len(fetches)]))
            fetches[-1].start()
    return fetches


def block_shapes(bases, pieces, cols):
    return [jax.ShapeDtypeStruct((len(pieces), base.shape[1], cols), base.dtype) for base in bases]


def moved(shapes):
    size = sum(x.size * x.dtype.itemsize for x in shapes)
    return pl.CostEstimate(flops=0, bytes_accessed=2 * size, transcendentals=0)


def fetch_kernel(n, pieces, *refs):
    count = len(refs) // 2
    for fetch in start_fetches(n, pieces, refs[:count], refs[count:-1], refs[-1]):
        fetch.wait()


def fetch_blocks(n, cols, bases, pieces):
    blocks = block_shapes(bases, pieces, cols)
    return pl.pallas_call(
        functools.partial(fetch_kernel, n, pieces),
        in_specs=[HBM] * len(bases),
        out_specs=[VMEM] * len(bases),
        out_shape=blocks,
        scratch_shapes=[pltpu.SemaphoreType.DMA((len(bases) * len(pieces),))],
        compiler_params=pltpu.CompilerParams(vmem_limit_bytes=4 * MIB),
        cost_estimate=moved(blocks),
    )(*[in_hbm(base) for base in bases])


def choose_b_kernel(n, pieces, owners, *refs):
    core = lax.axis_index("rollout")
    own, other, refs, sems = refs[0:3], refs[3:6], refs[6:-1], refs[-1]
    count = (len(refs) - 3) // 2
    bases, outs, blocks = refs[:count], refs[count : count + 3], refs[count + 3 :]
    fetches = start_fetches(n, pieces, bases, blocks, sems)
    for proj in range(3):
        for layer in range(own[proj].shape[0]):
            mine = owned(owners, layer, proj, core, own[proj].shape[1:])
            outs[proj][layer] = jnp.where(mine, own[proj][layer], other[proj][layer]).T
    for fetch in fetches:
        fetch.wait()


def choose_b(n, cols, owners, own, other, bases, pieces):
    chosen = [jax.ShapeDtypeStruct((x.shape[0], x.shape[2], x.shape[1]), x.dtype) for x in own]
    blocks = block_shapes(bases, pieces, cols)
    out = pl.pallas_call(
        functools.partial(choose_b_kernel, n, pieces),
        in_specs=[VMEM] * 7 + [HBM] * len(bases),
        out_specs=[VMEM] * (3 + len(blocks)),
        out_shape=chosen + blocks,
        scratch_shapes=[pltpu.SemaphoreType.DMA((len(bases) * len(pieces),))],
        compiler_params=pltpu.CompilerParams(vmem_limit_bytes=4 * MIB),
        cost_estimate=moved(blocks),
    )(in_vmem(owners), *[in_vmem(x) for x in own], *other, *[in_hbm(base) for base in bases])
    return out[:3], out[3:]


def merge_kernel(n, pieces, scale, fresh, *refs):
    count = len(pieces)
    b_refs, a_refs, bases = refs[0:3], refs[3 : 3 + count], refs[3 + count : 6 + count]
    at = 6 + count + (0 if fresh else 3)
    outs, bufs, sem = refs[at : at + 3], refs[at + 3 : at + 6], refs[at + 6]
    cols = a_refs[0].shape[-1]
    for i, (layer, start) in enumerate(column_starts(n, pieces, cols)):
        for proj in (1, 2, 0):
            last_row = bufs[proj].shape[1]
            for row in range(0, last_row, TILE_ROWS):
                rows = pl.ds(row, min(TILE_ROWS, last_row - row))
                for col in range(0, cols, TILE_COLS):
                    width = min(TILE_COLS, cols - col)
                    tile = pl.ds(col, width) if fresh else pl.ds(pl.multiple_of(start + col, LANES), width)
                    delta = jnp.dot(
                        b_refs[proj][layer, rows],
                        a_refs[i][proj, :, col : col + width],
                        preferred_element_type=jnp.float32,
                    )
                    block = bases[proj][i if fresh else layer, rows, tile]
                    merged = block.astype(jnp.float32) + scale * delta
                    bufs[proj][i, rows, col : col + width] = merged.astype(jnp.bfloat16)
                end = min(row + TILE_ROWS, last_row)
                if end % STORE_ROWS == 0 or end == last_row:
                    begin = (end - 1) // STORE_ROWS * STORE_ROWS
                    done = pl.ds(begin, end - begin)
                    target = outs[proj].at[layer, done, pl.ds(start, cols)]
                    pltpu.make_async_copy(bufs[proj].at[i, done], target, sem.at[proj]).start()
    for proj in range(3):
        pltpu.make_async_copy(bufs[proj], bufs[proj], sem.at[proj]).wait()


def merge(n, scale, b, a_list, bases, shapes, outs, pieces):
    fresh = outs is None
    rank, cols = a_list[0].shape[-2:]
    rows = sum(base.shape[1] for base in bases)
    return pl.pallas_call(
        functools.partial(merge_kernel, n, pieces, scale, fresh),
        in_specs=[VMEM] * (3 + len(a_list) + 3) + [HBM] * (0 if fresh else 3),
        out_specs=[HBM] * 3,
        out_shape=shapes,
        scratch_shapes=[pltpu.VMEM((len(pieces), base.shape[1], cols), base.dtype) for base in bases]
        + [pltpu.SemaphoreType.DMA((3,))],
        input_output_aliases={} if fresh else {6 + len(a_list) + i: i for i in range(3)},
        compiler_params=pltpu.CompilerParams(vmem_limit_bytes=16 * MIB),
        cost_estimate=pl.CostEstimate(
            flops=2 * len(pieces) * rows * cols * rank,
            bytes_accessed=4 * len(pieces) * rows * cols,
            transcendentals=0,
        ),
    )(*b, *a_list, *(bases if fresh else [in_vmem(base) for base in bases]), *([] if fresh else outs))

def per_device(
    n,
    owners,
    base_query,
    base_key,
    base_value,
    left_shared_matrix,
    right_queries_matrix,
    right_keys_matrix,
    right_values_matrix,
):
    layers, projs, rank, cols = left_shared_matrix.shape[1:]
    scale = numerator_gain / rank
    bases = (base_query, base_key, base_value)
    rights = (right_queries_matrix, right_keys_matrix, right_values_matrix)
    last = n // 2

    own_a = left_shared_matrix[0]
    own_b = [jnp.swapaxes(right[0], 1, 2) for right in rights]

    if cols % LANES == 0:
        tie = lax.optimization_barrier
        shapes = [jax.ShapeDtypeStruct(base.shape, base.dtype) for base in bases]
        pieces = [(0, True, True), (0, True, False)]
        query_block = fetch_blocks(n, cols, [base_query], pieces)
        other_a, query_block = tie((swap_cores(own_a), query_block))
        first, second = choose_a(owners, own_a, other_a)
        other_b = [swap_cores(x) for x in own_b]
        second, other_b[1] = tie((second, other_b[1]))
        held = [first, second]
        first = ring_pass(first, n)
        second = ring_pass(second, n)
        b, blocks = choose_b(n, cols, owners, own_b, other_b, [base_key, base_value], pieces)
        first, b = tie((first, b))
        outs = merge(n, scale, b, held, [*query_block, *blocks], shapes, None, pieces)

        def go(outs, *named):
            pieces = [(step, not swapped, ((step % 2 == 0) == (ring == "a")) != swapped) for step, ring, swapped, _ in named]
            return merge(n, scale, b, [chunk for *_, chunk in named], bases, shapes, outs, pieces)

        swapped_a = swapped_b = None
        for step in range(1, last):
            a_here = (step, "a", False, first)
            a_there = (step, "a", True, swap_cores(first))
            first = ring_pass(first, n)
            if step > 1:
                outs = go(outs, a_here, swapped_a)
            second, outs = tie((second, outs))
            b_here = (step, "b", False, second)
            b_there = (step, "b", True, swap_cores(second))
            if step < last - 1:
                second = ring_pass(second, n)
            if step == 1:
                outs, late = go(outs, a_here), b_here
            else:
                outs = go(outs, b_here, swapped_b, *([a_there, late] if step == last - 1 else []))
            first, outs = tie((first, outs))
            swapped_a, swapped_b = a_there, b_there
        a_there = (last, "a", True, swap_cores(first))
        outs = go(outs, swapped_b, (last, "a", False, first))
        return tuple(go(outs, a_there))

    core = lax.axis_index("rollout")
    tensor = lax.axis_index("tensor")
    mine = owners == core
    a = jnp.where(mine[:, :, None, None], own_a, swap_cores(own_a))
    b = [jnp.where(mine[:, proj, None, None], x, swap_cores(x)) for proj, x in enumerate(own_b)]
    full = jnp.zeros((layers, projs, rank, n * cols), own_a.dtype)

    def put(full, piece, layer, step, from_core):
        start = place_of(n, step, from_core, tensor) * cols
        return lax.dynamic_update_slice(full, piece[None], (layer, 0, 0, start))

    first = jnp.where(core == 0, a[0], a[1])
    second = jnp.where(core == 0, a[1], a[0])
    full = put(full, first, core, 0, core)
    full = put(full, second, 1 - core, 0, core)
    for step in range(1, last + 1):
        layer = (core + step) % 2
        first = ring_pass(first, n)
        full = put(full, first, layer, step, core)
        full = put(full, swap_cores(first), 1 - layer, step, 1 - core)
        if step < last:
            second = ring_pass(second, n)
            full = put(full, second, 1 - layer, step, core)
            full = put(full, swap_cores(second), layer, step, 1 - core)
    merged = []
    for proj in range(projs):
        delta = jnp.einsum("lkr,lkc->lrc", b[proj], full[:, proj], preferred_element_type=jnp.float32)
        merged.append((bases[proj].astype(jnp.float32) + scale * delta).astype(jnp.bfloat16))
    return tuple(merged)


def solution(mesh):
    return jax.shard_map(
        functools.partial(per_device, mesh.shape["tensor"]),
        mesh=mesh,
        in_specs=(
            P("copies", None),
            P("copies", "tensor", None),
            P("copies", "tensor", None),
            P("copies", "tensor", None),
            P("rollout", "copies", None, None, "tensor"),
            P("rollout", "copies", "tensor", None),
            P("rollout", "copies", "tensor", None),
            P("rollout", "copies", "tensor", None),
        ),
        out_specs=(
            P("copies", "tensor", None),
            P("copies", "tensor", None),
            P("copies", "tensor", None),
        ),
        check_vma=False,
    )
```

```python
import functools

import jax
import jax.numpy as jnp
from jax import lax
from jax.experimental import pallas as pl
from jax.experimental.pallas import tpu as pltpu
from jax.sharding import PartitionSpec as P

numerator_gain = 16.0
LANES = 128
MIB = 1024 * 1024
TILE_ROWS = 160
TILE_COLS = 256
STORE_ROWS = 320
VMEM = pl.BlockSpec(memory_space=pltpu.VMEM)
HBM = pl.BlockSpec(memory_space=pltpu.HBM)
ANY = pl.BlockSpec(memory_space=pl.ANY)


def in_hbm(array):
    return pltpu.with_memory_space_constraint(array, pltpu.HBM)


def in_vmem(array):
    return pltpu.with_memory_space_constraint(array, pltpu.VMEM)


def ring_order(n):
    return list(range(0, n, 2)) + list(range(n - 1, 0, -2))


def ring_pass(array, n):
    order = ring_order(n)
    pairs = []
    for k in range(n):
        up, down = k % 2, 1 - k % 2
        pairs.append((up * n + order[k], (1 - up) * n + order[(k + 1) % n]))
        pairs.append((down * n + order[k], (1 - down) * n + order[(k - 1) % n]))
    return lax.ppermute(array, ("rollout", "tensor"), pairs)


def swap_cores(array):
    return lax.ppermute(array, "rollout", [(0, 1), (1, 0)])


def place_of(n, step, from_core, tensor):
    position = jnp.where(tensor % 2 == 0, tensor // 2, n - 1 - tensor // 2)
    k = position + jnp.where(from_core == position % 2, -step, step)
    k = jnp.where(k < 0, k + n, jnp.where(k >= n, k - n, k))
    return jnp.where(k < n // 2, 2 * k, 2 * n - 1 - 2 * k)


def column_starts(n, pieces, cols):
    core = lax.axis_index("rollout")
    tensor = lax.axis_index("tensor")
    blocks = []
    for step, own_ring, own_layer in pieces:
        place = place_of(n, step, core if own_ring else 1 - core, tensor)
        blocks.append((core if own_layer else 1 - core, pl.multiple_of(place * cols, LANES)))
    return blocks


def owned(owners, layer, proj, core, shape):
    return jnp.broadcast_to(owners[pl.ds(layer, 1), proj : proj + 1] == core, shape)


def choose_a_kernel(owners, own, other, first, second):
    core = lax.axis_index("rollout")
    for out, layer in ((first, core), (second, 1 - core)):
        for proj in range(own.shape[1]):
            mine = owned(owners, layer, proj, core, out.shape[1:])
            out[proj] = jnp.where(mine, own[layer, proj], other[layer, proj])


def choose_a(owners, own, other):
    piece = jax.ShapeDtypeStruct(own.shape[1:], own.dtype)
    return pl.pallas_call(
        choose_a_kernel,
        in_specs=[VMEM, VMEM, VMEM],
        out_specs=[VMEM, VMEM],
        out_shape=[piece, piece],
        compiler_params=pltpu.CompilerParams(vmem_limit_bytes=4 * MIB),
    )(in_vmem(owners), in_vmem(own), other)


def start_fetches(n, pieces, bases, blocks, sems):
    cols = blocks[0].shape[2]
    fetches = []
    for i, (layer, start) in enumerate(column_starts(n, pieces, cols)):
        for base, block in zip(bases, blocks):
            source = base.at[layer, :, pl.ds(start, cols)]
            fetches.append(pltpu.make_async_copy(source, block.at[i], sems.at[len(fetches)]))
            fetches[-1].start()
    return fetches


def block_shapes(bases, pieces, cols):
    return [jax.ShapeDtypeStruct((len(pieces), base.shape[1], cols), base.dtype) for base in bases]


def moved(shapes):
    size = sum(x.size * x.dtype.itemsize for x in shapes)
    return pl.CostEstimate(flops=0, bytes_accessed=2 * size, transcendentals=0)


def fetch_kernel(n, pieces, *refs):
    count = len(refs) // 2
    for fetch in start_fetches(n, pieces, refs[:count], refs[count:-1], refs[-1]):
        fetch.wait()


def fetch_blocks(n, cols, bases, pieces):
    blocks = block_shapes(bases, pieces, cols)
    return pl.pallas_call(
        functools.partial(fetch_kernel, n, pieces),
        in_specs=[HBM] * len(bases),
        out_specs=[VMEM] * len(bases),
        out_shape=blocks,
        scratch_shapes=[pltpu.SemaphoreType.DMA((len(bases) * len(pieces),))],
        compiler_params=pltpu.CompilerParams(vmem_limit_bytes=4 * MIB),
        cost_estimate=moved(blocks),
    )(*[in_hbm(base) for base in bases])


def choose_b_kernel(n, pieces, owners, *refs):
    core = lax.axis_index("rollout")
    own, other, refs, sems = refs[0:3], refs[3:6], refs[6:-1], refs[-1]
    count = (len(refs) - 3) // 2
    bases, outs, blocks = refs[:count], refs[count : count + 3], refs[count + 3 :]
    fetches = start_fetches(n, pieces, bases, blocks, sems)
    for proj in range(3):
        for layer in range(own[proj].shape[0]):
            mine = owned(owners, layer, proj, core, own[proj].shape[1:])
            outs[proj][layer] = jnp.where(mine, own[proj][layer], other[proj][layer]).T
    for fetch in fetches:
        fetch.wait()


def choose_b(n, cols, owners, own, other, bases, pieces):
    chosen = [jax.ShapeDtypeStruct((x.shape[0], x.shape[2], x.shape[1]), x.dtype) for x in own]
    blocks = block_shapes(bases, pieces, cols)
    out = pl.pallas_call(
        functools.partial(choose_b_kernel, n, pieces),
        in_specs=[VMEM] * 7 + [HBM] * len(bases),
        out_specs=[VMEM] * (3 + len(blocks)),
        out_shape=chosen + blocks,
        scratch_shapes=[pltpu.SemaphoreType.DMA((len(bases) * len(pieces),))],
        compiler_params=pltpu.CompilerParams(vmem_limit_bytes=4 * MIB),
        cost_estimate=moved(blocks),
    )(in_vmem(owners), *[in_vmem(x) for x in own], *other, *[in_hbm(base) for base in bases])
    return out[:3], out[3:]


def merge_kernel(n, pieces, scale, fresh, *refs):
    count = len(pieces)
    b_refs, a_refs, bases = refs[0:3], refs[3 : 3 + count], refs[3 + count : 6 + count]
    at = 6 + count + (0 if fresh else 3)
    outs, bufs, sem = refs[at : at + 3], refs[at + 3 : at + 6], refs[at + 6]
    cols = a_refs[0].shape[-1]
    for i, (layer, start) in enumerate(column_starts(n, pieces, cols)):
        for proj in (1, 2, 0):
            last_row = bufs[proj].shape[1]
            for row in range(0, last_row, TILE_ROWS):
                rows = pl.ds(row, min(TILE_ROWS, last_row - row))
                for col in range(0, cols, TILE_COLS):
                    width = min(TILE_COLS, cols - col)
                    tile = pl.ds(col, width) if fresh else pl.ds(pl.multiple_of(start + col, LANES), width)
                    delta = jnp.dot(
                        b_refs[proj][layer, rows],
                        a_refs[i][proj, :, col : col + width],
                        preferred_element_type=jnp.float32,
                    )
                    block = bases[proj][i if fresh else layer, rows, tile]
                    merged = block.astype(jnp.float32) + scale * delta
                    bufs[proj][i, rows, col : col + width] = merged.astype(jnp.bfloat16)
                end = min(row + TILE_ROWS, last_row)
                if end % STORE_ROWS == 0 or end == last_row:
                    begin = (end - 1) // STORE_ROWS * STORE_ROWS
                    done = pl.ds(begin, end - begin)
                    target = outs[proj].at[layer, done, pl.ds(start, cols)]
                    pltpu.make_async_copy(bufs[proj].at[i, done], target, sem.at[proj]).start()
    for proj in range(3):
        pltpu.make_async_copy(bufs[proj], bufs[proj], sem.at[proj]).wait()


def merge(n, scale, b, a_list, bases, shapes, outs, pieces):
    fresh = outs is None
    rank, cols = a_list[0].shape[-2:]
    rows = sum(base.shape[1] for base in bases)
    return pl.pallas_call(
        functools.partial(merge_kernel, n, pieces, scale, fresh),
        in_specs=[VMEM] * (3 + len(a_list) + 3) + [HBM] * (0 if fresh else 3),
        out_specs=[HBM] * 3,
        out_shape=shapes,
        scratch_shapes=[pltpu.VMEM((len(pieces), base.shape[1], cols), base.dtype) for base in bases]
        + [pltpu.SemaphoreType.DMA((3,))],
        input_output_aliases={} if fresh else {6 + len(a_list) + i: i for i in range(3)},
        compiler_params=pltpu.CompilerParams(vmem_limit_bytes=16 * MIB),
        cost_estimate=pl.CostEstimate(
            flops=2 * len(pieces) * rows * cols * rank,
            bytes_accessed=4 * len(pieces) * rows * cols,
            transcendentals=0,
        ),
    )(*b, *a_list, *(bases if fresh else [in_vmem(base) for base in bases]), *([] if fresh else outs))

def per_device(
    n,
    owners,
    base_query,
    base_key,
    base_value,
    left_shared_matrix,
    right_queries_matrix,
    right_keys_matrix,
    right_values_matrix,
):
    layers, projs, rank, cols = left_shared_matrix.shape[1:]
    scale = numerator_gain / rank
    bases = (base_query, base_key, base_value)
    rights = (right_queries_matrix, right_keys_matrix, right_values_matrix)
    last = n // 2

    own_a = left_shared_matrix[0]
    own_b = [jnp.swapaxes(right[0], 1, 2) for right in rights]

    if cols % LANES == 0:
        tie = lax.optimization_barrier
        shapes = [jax.ShapeDtypeStruct(base.shape, base.dtype) for base in bases]
        pieces = [(0, True, True), (0, True, False)]
        query_block = fetch_blocks(n, cols, [base_query], pieces)
        other_a, query_block = tie((swap_cores(own_a), query_block))
        first, second = choose_a(owners, own_a, other_a)
        other_b = [swap_cores(x) for x in own_b]
        second, other_b[1] = tie((second, other_b[1]))
        held = [first, second]
        first = ring_pass(first, n)
        second = ring_pass(second, n)
        b, blocks = choose_b(n, cols, owners, own_b, other_b, [base_key, base_value], pieces)
        first, b = tie((first, b))
        outs = merge(n, scale, b, held, [*query_block, *blocks], shapes, None, pieces)

        def go(outs, *named):
            pieces = [(step, not swapped, ((step % 2 == 0) == (ring == "a")) != swapped) for step, ring, swapped, _ in named]
            return merge(n, scale, b, [chunk for *_, chunk in named], bases, shapes, outs, pieces)

        before = []
        for step in range(1, last):
            a_here = (step, "a", False, first)
            a_there = (step, "a", True, swap_cores(first))
            first = ring_pass(first, n)
            if step > 1:
                outs = go(outs, *before)
            second, outs = tie((second, outs))
            b_here = (step, "b", False, second)
            swapped_b = (step, "b", True, swap_cores(second))
            before = [a_there, b_here, swapped_b]
            if step < last - 1:
                second = ring_pass(second, n)
            outs = go(outs, a_here, *(before[:2] if step == last - 1 else []))
            first, outs = tie((first, outs))
        a_there = (last, "a", True, swap_cores(first))
        outs = go(outs, swapped_b, (last, "a", False, first))
        return tuple(go(outs, a_there))

    core = lax.axis_index("rollout")
    tensor = lax.axis_index("tensor")
    mine = owners == core
    a = jnp.where(mine[:, :, None, None], own_a, swap_cores(own_a))
    b = [jnp.where(mine[:, proj, None, None], x, swap_cores(x)) for proj, x in enumerate(own_b)]
    full = jnp.zeros((layers, projs, rank, n * cols), own_a.dtype)

    def put(full, piece, layer, step, from_core):
        start = place_of(n, step, from_core, tensor) * cols
        return lax.dynamic_update_slice(full, piece[None], (layer, 0, 0, start))

    first = jnp.where(core == 0, a[0], a[1])
    second = jnp.where(core == 0, a[1], a[0])
    full = put(full, first, core, 0, core)
    full = put(full, second, 1 - core, 0, core)
    for step in range(1, last + 1):
        layer = (core + step) % 2
        first = ring_pass(first, n)
        full = put(full, first, layer, step, core)
        full = put(full, swap_cores(first), 1 - layer, step, 1 - core)
        if step < last:
            second = ring_pass(second, n)
            full = put(full, second, 1 - layer, step, core)
            full = put(full, swap_cores(second), layer, step, 1 - core)
    merged = []
    for proj in range(projs):
        delta = jnp.einsum("lkr,lkc->lrc", b[proj], full[:, proj], preferred_element_type=jnp.float32)
        merged.append((bases[proj].astype(jnp.float32) + scale * delta).astype(jnp.bfloat16))
    return tuple(merged)


def solution(mesh):
    return jax.shard_map(
        functools.partial(per_device, mesh.shape["tensor"]),
        mesh=mesh,
        in_specs=(
            P("copies", None),
            P("copies", "tensor", None),
            P("copies", "tensor", None),
            P("copies", "tensor", None),
            P("rollout", "copies", None, None, "tensor"),
            P("rollout", "copies", "tensor", None),
            P("rollout", "copies", "tensor", None),
            P("rollout", "copies", "tensor", None),
        ),
        out_specs=(
            P("copies", "tensor", None),
            P("copies", "tensor", None),
            P("copies", "tensor", None),
        ),
        check_vma=False,
    )
```

```python
import functools

import jax
import jax.numpy as jnp
from jax import lax
from jax.experimental import pallas as pl
from jax.experimental.pallas import tpu as pltpu
from jax.sharding import PartitionSpec as P

numerator_gain = 16.0
LANES = 128
MIB = 1024 * 1024
TILE_ROWS = 160
TILE_COLS = 256
STORE_ROWS = 320
VMEM = pl.BlockSpec(memory_space=pltpu.VMEM)
HBM = pl.BlockSpec(memory_space=pltpu.HBM)
ANY = pl.BlockSpec(memory_space=pl.ANY)


def in_hbm(array):
    return pltpu.with_memory_space_constraint(array, pltpu.HBM)


def in_vmem(array):
    return pltpu.with_memory_space_constraint(array, pltpu.VMEM)


def ring_order(n):
    return list(range(0, n, 2)) + list(range(n - 1, 0, -2))


def ring_pass(array, n):
    order = ring_order(n)
    pairs = []
    for k in range(n):
        up, down = k % 2, 1 - k % 2
        pairs.append((up * n + order[k], (1 - up) * n + order[(k + 1) % n]))
        pairs.append((down * n + order[k], (1 - down) * n + order[(k - 1) % n]))
    return lax.ppermute(array, ("rollout", "tensor"), pairs)


def swap_cores(array):
    return lax.ppermute(array, "rollout", [(0, 1), (1, 0)])


def place_of(n, step, from_core, tensor):
    position = jnp.where(tensor % 2 == 0, tensor // 2, n - 1 - tensor // 2)
    k = position + jnp.where(from_core == position % 2, -step, step)
    k = jnp.where(k < 0, k + n, jnp.where(k >= n, k - n, k))
    return jnp.where(k < n // 2, 2 * k, 2 * n - 1 - 2 * k)


def column_starts(n, pieces, cols):
    core = lax.axis_index("rollout")
    tensor = lax.axis_index("tensor")
    blocks = []
    for step, own_ring, own_layer in pieces:
        place = place_of(n, step, core if own_ring else 1 - core, tensor)
        blocks.append((core if own_layer else 1 - core, pl.multiple_of(place * cols, LANES)))
    return blocks


def owned(owners, layer, proj, core, shape):
    return jnp.broadcast_to(owners[pl.ds(layer, 1), proj : proj + 1] == core, shape)


def choose_a_kernel(owners, own, other, first, second):
    core = lax.axis_index("rollout")
    for out, layer in ((first, core), (second, 1 - core)):
        for proj in range(own.shape[1]):
            mine = owned(owners, layer, proj, core, out.shape[1:])
            out[proj] = jnp.where(mine, own[layer, proj], other[layer, proj])


def choose_a(owners, own, other):
    piece = jax.ShapeDtypeStruct(own.shape[1:], own.dtype)
    return pl.pallas_call(
        choose_a_kernel,
        in_specs=[VMEM, VMEM, VMEM],
        out_specs=[VMEM, VMEM],
        out_shape=[piece, piece],
        compiler_params=pltpu.CompilerParams(vmem_limit_bytes=4 * MIB),
    )(in_vmem(owners), in_vmem(own), other)


def start_fetches(n, pieces, bases, blocks, sems):
    cols = blocks[0].shape[2]
    fetches = []
    for i, (layer, start) in enumerate(column_starts(n, pieces, cols)):
        for base, block in zip(bases, blocks):
            source = base.at[layer, :, pl.ds(start, cols)]
            fetches.append(pltpu.make_async_copy(source, block.at[i], sems.at[len(fetches)]))
            fetches[-1].start()
    return fetches


def block_shapes(bases, pieces, cols):
    return [jax.ShapeDtypeStruct((len(pieces), base.shape[1], cols), base.dtype) for base in bases]


def moved(shapes):
    size = sum(x.size * x.dtype.itemsize for x in shapes)
    return pl.CostEstimate(flops=0, bytes_accessed=2 * size, transcendentals=0)


def fetch_kernel(n, pieces, *refs):
    count = len(refs) // 2
    for fetch in start_fetches(n, pieces, refs[:count], refs[count:-1], refs[-1]):
        fetch.wait()


def fetch_blocks(n, cols, bases, pieces):
    blocks = block_shapes(bases, pieces, cols)
    return pl.pallas_call(
        functools.partial(fetch_kernel, n, pieces),
        in_specs=[HBM] * len(bases),
        out_specs=[VMEM] * len(bases),
        out_shape=blocks,
        scratch_shapes=[pltpu.SemaphoreType.DMA((len(bases) * len(pieces),))],
        compiler_params=pltpu.CompilerParams(vmem_limit_bytes=4 * MIB),
        cost_estimate=moved(blocks),
    )(*[in_hbm(base) for base in bases])


def merge_pieces(n, pieces, scale, b_refs, a_refs, base_of, outs, bufs, sem):
    cols = a_refs[0].shape[-1]
    for i, (layer, start) in enumerate(column_starts(n, pieces, cols)):
        for proj in (1, 2, 0):
            last_row = bufs[proj].shape[1]
            for row in range(0, last_row, TILE_ROWS):
                rows = pl.ds(row, min(TILE_ROWS, last_row - row))
                for col in range(0, cols, TILE_COLS):
                    width = min(TILE_COLS, cols - col)
                    delta = jnp.dot(
                        b_refs[proj][layer, rows],
                        a_refs[i][proj, :, col : col + width],
                        preferred_element_type=jnp.float32,
                    )
                    block = base_of(proj, i, layer, rows, start, col, width)
                    merged = block.astype(jnp.float32) + scale * delta
                    bufs[proj][i, rows, col : col + width] = merged.astype(jnp.bfloat16)
                end = min(row + TILE_ROWS, last_row)
                if end % STORE_ROWS == 0 or end == last_row:
                    begin = (end - 1) // STORE_ROWS * STORE_ROWS
                    done = pl.ds(begin, end - begin)
                    target = outs[proj].at[layer, done, pl.ds(start, cols)]
                    pltpu.make_async_copy(bufs[proj].at[i, done], target, sem.at[proj]).start()
    for proj in range(3):
        pltpu.make_async_copy(bufs[proj], bufs[proj], sem.at[proj]).wait()


def merge_own_kernel(n, pieces, scale, owners, *refs):
    own, other, small_bases, query_block = refs[0:3], refs[3:6], refs[6:8], refs[8]
    a_refs, outs, b_refs = refs[9:11], refs[11:14], refs[14:17]
    small_blocks, bufs, load_sems, sem = refs[17:19], refs[19:22], refs[22], refs[23]
    core = lax.axis_index("rollout")
    fetches = start_fetches(n, pieces, small_bases, small_blocks, load_sems)
    for proj in range(3):
        for layer in range(own[proj].shape[0]):
            mine = owned(owners, layer, proj, core, own[proj].shape[1:])
            b_refs[proj][layer] = jnp.where(mine, own[proj][layer], other[proj][layer]).T
    for fetch in fetches:
        fetch.wait()
    blocks = (query_block, *small_blocks)

    def base_of(proj, i, layer, rows, start, col, width):
        return blocks[proj][i, rows, col : col + width]

    merge_pieces(n, pieces, scale, b_refs, a_refs, base_of, outs, bufs, sem)


def merge_kernel(n, pieces, scale, *refs):
    count = len(pieces)
    b_refs, a_refs, bases = refs[0:3], refs[3 : 3 + count], refs[3 + count : 6 + count]
    outs, bufs, sem = refs[9 + count : 12 + count], refs[12 + count : 15 + count], refs[15 + count]

    def base_of(proj, i, layer, rows, start, col, width):
        return bases[proj][layer, rows, pl.ds(pl.multiple_of(start + col, LANES), width)]

    merge_pieces(n, pieces, scale, b_refs, a_refs, base_of, outs, bufs, sem)


def merge_cost(bases, a_list):
    rank, cols = a_list[0].shape[-2:]
    cells = len(a_list) * sum(base.shape[1] for base in bases) * cols
    return pl.CostEstimate(flops=2 * cells * rank, bytes_accessed=4 * cells, transcendentals=0)


def buffers(bases, a_list):
    cols = a_list[0].shape[-1]
    return [pltpu.VMEM((len(a_list), base.shape[1], cols), base.dtype) for base in bases]


def merge_own(n, scale, owners, own, other, query_block, a_list, bases, pieces):
    chosen = [jax.ShapeDtypeStruct((x.shape[0], x.shape[2], x.shape[1]), x.dtype) for x in own]
    bufs = buffers(bases, a_list)
    out = pl.pallas_call(
        functools.partial(merge_own_kernel, n, pieces, scale),
        in_specs=[VMEM] * 7 + [HBM] * 2 + [VMEM] * (1 + len(a_list)),
        out_specs=[HBM] * 3 + [VMEM] * 3,
        out_shape=[jax.ShapeDtypeStruct(base.shape, base.dtype) for base in bases] + chosen,
        scratch_shapes=bufs[1:]
        + bufs
        + [pltpu.SemaphoreType.DMA((2 * len(pieces),)), pltpu.SemaphoreType.DMA((3,))],
        compiler_params=pltpu.CompilerParams(vmem_limit_bytes=16 * MIB),
        cost_estimate=merge_cost(bases, a_list),
    )(
        in_vmem(owners),
        *[in_vmem(x) for x in own],
        *other,
        *[in_hbm(base) for base in bases[1:]],
        query_block,
        *a_list,
    )
    return out[:3], out[3:]


def merge(n, scale, b, a_list, bases, outs, pieces):
    return pl.pallas_call(
        functools.partial(merge_kernel, n, pieces, scale),
        in_specs=[VMEM] * (3 + len(a_list) + 3) + [HBM] * 3,
        out_specs=[HBM] * 3,
        out_shape=[jax.ShapeDtypeStruct(base.shape, base.dtype) for base in bases],
        scratch_shapes=buffers(bases, a_list) + [pltpu.SemaphoreType.DMA((3,))],
        input_output_aliases={6 + len(a_list) + i: i for i in range(3)},
        compiler_params=pltpu.CompilerParams(vmem_limit_bytes=16 * MIB),
        cost_estimate=merge_cost(bases, a_list),
    )(*b, *a_list, *[in_vmem(base) for base in bases], *outs)


def per_device(
    n,
    owners,
    base_query,
    base_key,
    base_value,
    left_shared_matrix,
    right_queries_matrix,
    right_keys_matrix,
    right_values_matrix,
):
    layers, projs, rank, cols = left_shared_matrix.shape[1:]
    scale = numerator_gain / rank
    bases = (base_query, base_key, base_value)
    rights = (right_queries_matrix, right_keys_matrix, right_values_matrix)
    last = n // 2

    own_a = left_shared_matrix[0]
    own_b = [jnp.swapaxes(right[0], 1, 2) for right in rights]

    if cols % LANES == 0:
        tie = lax.optimization_barrier
        pieces = [(0, True, True), (0, True, False)]
        query_block = fetch_blocks(n, cols, [base_query], pieces)
        other_a, query_block = tie((swap_cores(own_a), query_block))
        first, second = choose_a(owners, own_a, other_a)
        other_b = [swap_cores(x) for x in own_b]
        held = [first, second]
        first = ring_pass(first, n)
        second = ring_pass(second, n)
        outs, b = merge_own(n, scale, owners, own_b, other_b, *query_block, held, bases, pieces)
        first, outs = tie((first, outs))

        def go(outs, *named):
            pieces = [(step, not swapped, ((step % 2 == 0) == (ring == "a")) != swapped) for step, ring, swapped, _ in named]
            return merge(n, scale, b, [chunk for *_, chunk in named], bases, outs, pieces)

        swapped_a = swapped_b = ()
        for step in range(1, last):
            a_here = (step, "a", False, first)
            a_there = (step, "a", True, swap_cores(first))
            first = ring_pass(first, n)
            outs = go(outs, a_here, *swapped_a)
            second, outs = tie((second, outs))
            b_here = (step, "b", False, second)
            b_there = (step, "b", True, swap_cores(second))
            if step < last - 1:
                second = ring_pass(second, n)
            outs = go(outs, b_here, *swapped_b, *([a_there] if step == last - 1 else []))
            first, outs = tie((first, outs))
            swapped_a, swapped_b = (a_there,), (b_there,)
        a_there = (last, "a", True, swap_cores(first))
        outs = go(outs, *swapped_b, (last, "a", False, first))
        return tuple(go(outs, a_there))

    core = lax.axis_index("rollout")
    tensor = lax.axis_index("tensor")
    mine = owners == core
    a = jnp.where(mine[:, :, None, None], own_a, swap_cores(own_a))
    b = [jnp.where(mine[:, proj, None, None], x, swap_cores(x)) for proj, x in enumerate(own_b)]
    full = jnp.zeros((layers, projs, rank, n * cols), own_a.dtype)

    def put(full, piece, layer, step, from_core):
        start = place_of(n, step, from_core, tensor) * cols
        return lax.dynamic_update_slice(full, piece[None], (layer, 0, 0, start))

    first = jnp.where(core == 0, a[0], a[1])
    second = jnp.where(core == 0, a[1], a[0])
    full = put(full, first, core, 0, core)
    full = put(full, second, 1 - core, 0, core)
    for step in range(1, last + 1):
        layer = (core + step) % 2
        first = ring_pass(first, n)
        full = put(full, first, layer, step, core)
        full = put(full, swap_cores(first), 1 - layer, step, 1 - core)
        if step < last:
            second = ring_pass(second, n)
            full = put(full, second, 1 - layer, step, core)
            full = put(full, swap_cores(second), layer, step, 1 - core)
    merged = []
    for proj in range(projs):
        delta = jnp.einsum("lkr,lkc->lrc", b[proj], full[:, proj], preferred_element_type=jnp.float32)
        merged.append((bases[proj].astype(jnp.float32) + scale * delta).astype(jnp.bfloat16))
    return tuple(merged)


def solution(mesh):
    return jax.shard_map(
        functools.partial(per_device, mesh.shape["tensor"]),
        mesh=mesh,
        in_specs=(
            P("copies", None),
            P("copies", "tensor", None),
            P("copies", "tensor", None),
            P("copies", "tensor", None),
            P("rollout", "copies", None, None, "tensor"),
            P("rollout", "copies", "tensor", None),
            P("rollout", "copies", "tensor", None),
            P("rollout", "copies", "tensor", None),
        ),
        out_specs=(
            P("copies", "tensor", None),
            P("copies", "tensor", None),
            P("copies", "tensor", None),
        ),
        check_vma=False,
    )
```

```python
import functools

import jax
import jax.numpy as jnp
from jax import lax
from jax.experimental import pallas as pl
from jax.experimental.pallas import tpu as pltpu
from jax.sharding import PartitionSpec as P

numerator_gain = 16.0
LANES = 128
MIB = 1024 * 1024
TILE_ROWS = 160
TILE_COLS = 256
STORE_ROWS = 320
VMEM = pl.BlockSpec(memory_space=pltpu.VMEM)
HBM = pl.BlockSpec(memory_space=pltpu.HBM)
ANY = pl.BlockSpec(memory_space=pl.ANY)


def in_hbm(array):
    return pltpu.with_memory_space_constraint(array, pltpu.HBM)


def in_vmem(array):
    return pltpu.with_memory_space_constraint(array, pltpu.VMEM)


def ring_order(n):
    return list(range(0, n, 2)) + list(range(n - 1, 0, -2))


def ring_pass(array, n):
    order = ring_order(n)
    pairs = []
    for k in range(n):
        up, down = k % 2, 1 - k % 2
        pairs.append((up * n + order[k], (1 - up) * n + order[(k + 1) % n]))
        pairs.append((down * n + order[k], (1 - down) * n + order[(k - 1) % n]))
    return lax.ppermute(array, ("rollout", "tensor"), pairs)


def swap_cores(array):
    return lax.ppermute(array, "rollout", [(0, 1), (1, 0)])


def place_of(n, step, from_core, tensor):
    position = jnp.where(tensor % 2 == 0, tensor // 2, n - 1 - tensor // 2)
    k = position + jnp.where(from_core == position % 2, -step, step)
    k = jnp.where(k < 0, k + n, jnp.where(k >= n, k - n, k))
    return jnp.where(k < n // 2, 2 * k, 2 * n - 1 - 2 * k)


def column_starts(n, pieces, cols):
    core = lax.axis_index("rollout")
    tensor = lax.axis_index("tensor")
    blocks = []
    for step, own_ring, own_layer in pieces:
        place = place_of(n, step, core if own_ring else 1 - core, tensor)
        blocks.append((core if own_layer else 1 - core, pl.multiple_of(place * cols, LANES)))
    return blocks


def owned(owners, layer, proj, core, shape):
    return jnp.broadcast_to(owners[pl.ds(layer, 1), proj : proj + 1] == core, shape)


def choose_a_kernel(owners, own, other, first, second):
    core = lax.axis_index("rollout")
    for out, layer in ((first, core), (second, 1 - core)):
        for proj in range(own.shape[1]):
            mine = owned(owners, layer, proj, core, out.shape[1:])
            out[proj] = jnp.where(mine, own[layer, proj], other[layer, proj])


def choose_a(owners, own, other):
    piece = jax.ShapeDtypeStruct(own.shape[1:], own.dtype)
    return pl.pallas_call(
        choose_a_kernel,
        in_specs=[VMEM, VMEM, VMEM],
        out_specs=[VMEM, VMEM],
        out_shape=[piece, piece],
        compiler_params=pltpu.CompilerParams(vmem_limit_bytes=4 * MIB),
    )(in_vmem(owners), in_vmem(own), other)


def start_fetches(n, pieces, bases, blocks, sems):
    cols = blocks[0].shape[2]
    fetches = []
    for i, (layer, start) in enumerate(column_starts(n, pieces, cols)):
        for base, block in zip(bases, blocks):
            source = base.at[layer, :, pl.ds(start, cols)]
            fetches.append(pltpu.make_async_copy(source, block.at[i], sems.at[len(fetches)]))
            fetches[-1].start()
    return fetches


def block_shapes(bases, pieces, cols):
    return [jax.ShapeDtypeStruct((len(pieces), base.shape[1], cols), base.dtype) for base in bases]


def moved(shapes):
    size = sum(x.size * x.dtype.itemsize for x in shapes)
    return pl.CostEstimate(flops=0, bytes_accessed=2 * size, transcendentals=0)


def fetch_kernel(n, pieces, *refs):
    count = len(refs) // 2
    for fetch in start_fetches(n, pieces, refs[:count], refs[count:-1], refs[-1]):
        fetch.wait()


def fetch_blocks(n, cols, bases, pieces):
    blocks = block_shapes(bases, pieces, cols)
    return pl.pallas_call(
        functools.partial(fetch_kernel, n, pieces),
        in_specs=[HBM] * len(bases),
        out_specs=[VMEM] * len(bases),
        out_shape=blocks,
        scratch_shapes=[pltpu.SemaphoreType.DMA((len(bases) * len(pieces),))],
        compiler_params=pltpu.CompilerParams(vmem_limit_bytes=4 * MIB),
        cost_estimate=moved(blocks),
    )(*[in_hbm(base) for base in bases])


def merge_pieces(n, pieces, scale, b_refs, a_refs, base_of, outs, bufs, sem):
    cols = a_refs[0].shape[-1]
    for i, (layer, start) in enumerate(column_starts(n, pieces, cols)):
        for proj in (1, 2, 0):
            last_row = bufs[proj].shape[1]
            for row in range(0, last_row, TILE_ROWS):
                rows = pl.ds(row, min(TILE_ROWS, last_row - row))
                for col in range(0, cols, TILE_COLS):
                    width = min(TILE_COLS, cols - col)
                    delta = jnp.dot(
                        b_refs[proj][layer, rows],
                        a_refs[i][proj, :, col : col + width],
                        preferred_element_type=jnp.float32,
                    )
                    block = base_of(proj, i, layer, rows, start, col, width)
                    merged = block.astype(jnp.float32) + scale * delta
                    bufs[proj][i, rows, col : col + width] = merged.astype(jnp.bfloat16)
                end = min(row + TILE_ROWS, last_row)
                if end % STORE_ROWS == 0 or end == last_row:
                    begin = (end - 1) // STORE_ROWS * STORE_ROWS
                    done = pl.ds(begin, end - begin)
                    target = outs[proj].at[layer, done, pl.ds(start, cols)]
                    pltpu.make_async_copy(bufs[proj].at[i, done], target, sem.at[proj]).start()
    for proj in range(3):
        pltpu.make_async_copy(bufs[proj], bufs[proj], sem.at[proj]).wait()


def merge_own_kernel(n, pieces, scale, owners, *refs):
    own, other, blocks, a_refs = refs[0:3], refs[3:6], refs[6:9], refs[9:11]
    outs, b_refs, bufs, sem = refs[11:14], refs[14:17], refs[17:20], refs[20]
    core = lax.axis_index("rollout")
    for proj in range(3):
        for layer in range(own[proj].shape[0]):
            mine = owned(owners, layer, proj, core, own[proj].shape[1:])
            b_refs[proj][layer] = jnp.where(mine, own[proj][layer], other[proj][layer]).T

    def base_of(proj, i, layer, rows, start, col, width):
        return blocks[proj][i, rows, col : col + width]

    merge_pieces(n, pieces, scale, b_refs, a_refs, base_of, outs, bufs, sem)


def merge_kernel(n, pieces, scale, *refs):
    count = len(pieces)
    b_refs, a_refs, bases = refs[0:3], refs[3 : 3 + count], refs[3 + count : 6 + count]
    outs, bufs, sem = refs[9 + count : 12 + count], refs[12 + count : 15 + count], refs[15 + count]

    def base_of(proj, i, layer, rows, start, col, width):
        return bases[proj][layer, rows, pl.ds(pl.multiple_of(start + col, LANES), width)]

    merge_pieces(n, pieces, scale, b_refs, a_refs, base_of, outs, bufs, sem)


def merge_cost(bases, a_list):
    rank, cols = a_list[0].shape[-2:]
    cells = len(a_list) * sum(base.shape[1] for base in bases) * cols
    return pl.CostEstimate(flops=2 * cells * rank, bytes_accessed=4 * cells, transcendentals=0)


def buffers(bases, a_list):
    cols = a_list[0].shape[-1]
    return [pltpu.VMEM((len(a_list), base.shape[1], cols), base.dtype) for base in bases]


def merge_own(n, scale, owners, own, other, blocks, a_list, bases, pieces):
    chosen = [jax.ShapeDtypeStruct((x.shape[0], x.shape[2], x.shape[1]), x.dtype) for x in own]
    out = pl.pallas_call(
        functools.partial(merge_own_kernel, n, pieces, scale),
        in_specs=[VMEM] * (10 + len(a_list)),
        out_specs=[HBM] * 3 + [VMEM] * 3,
        out_shape=[jax.ShapeDtypeStruct(base.shape, base.dtype) for base in bases] + chosen,
        scratch_shapes=buffers(bases, a_list) + [pltpu.SemaphoreType.DMA((3,))],
        compiler_params=pltpu.CompilerParams(vmem_limit_bytes=16 * MIB),
        cost_estimate=merge_cost(bases, a_list),
    )(in_vmem(owners), *[in_vmem(x) for x in own], *other, *blocks, *a_list)
    return out[:3], out[3:]


def merge(n, scale, b, a_list, bases, outs, pieces):
    return pl.pallas_call(
        functools.partial(merge_kernel, n, pieces, scale),
        in_specs=[VMEM] * (3 + len(a_list) + 3) + [HBM] * 3,
        out_specs=[HBM] * 3,
        out_shape=[jax.ShapeDtypeStruct(base.shape, base.dtype) for base in bases],
        scratch_shapes=buffers(bases, a_list) + [pltpu.SemaphoreType.DMA((3,))],
        input_output_aliases={6 + len(a_list) + i: i for i in range(3)},
        compiler_params=pltpu.CompilerParams(vmem_limit_bytes=16 * MIB),
        cost_estimate=merge_cost(bases, a_list),
    )(*b, *a_list, *[in_vmem(base) for base in bases], *outs)


def per_device(
    n,
    owners,
    base_query,
    base_key,
    base_value,
    left_shared_matrix,
    right_queries_matrix,
    right_keys_matrix,
    right_values_matrix,
):
    layers, projs, rank, cols = left_shared_matrix.shape[1:]
    scale = numerator_gain / rank
    bases = (base_query, base_key, base_value)
    rights = (right_queries_matrix, right_keys_matrix, right_values_matrix)
    last = n // 2

    own_a = left_shared_matrix[0]
    own_b = [jnp.swapaxes(right[0], 1, 2) for right in rights]

    if cols % LANES == 0:
        tie = lax.optimization_barrier
        pieces = [(0, True, True), (0, True, False)]
        blocks = fetch_blocks(n, cols, bases, pieces)
        other_a, blocks = tie((swap_cores(own_a), blocks))
        first, second = choose_a(owners, own_a, other_a)
        other_b = [swap_cores(x) for x in own_b]
        held = [first, second]
        first = ring_pass(first, n)
        second = ring_pass(second, n)
        outs, b = merge_own(n, scale, owners, own_b, other_b, blocks, held, bases, pieces)
        first, outs = tie((first, outs))

        def go(outs, *named):
            pieces = [(step, not swapped, ((step % 2 == 0) == (ring == "a")) != swapped) for step, ring, swapped, _ in named]
            return merge(n, scale, b, [chunk for *_, chunk in named], bases, outs, pieces)

        swapped_a = swapped_b = ()
        for step in range(1, last):
            a_here = (step, "a", False, first)
            a_there = (step, "a", True, swap_cores(first))
            first = ring_pass(first, n)
            outs = go(outs, a_here, *swapped_a)
            second, outs = tie((second, outs))
            b_here = (step, "b", False, second)
            b_there = (step, "b", True, swap_cores(second))
            if step < last - 1:
                second = ring_pass(second, n)
            outs = go(outs, b_here, *swapped_b, *([a_there] if step == last - 1 else []))
            first, outs = tie((first, outs))
            swapped_a, swapped_b = (a_there,), (b_there,)
        a_there = (last, "a", True, swap_cores(first))
        outs = go(outs, *swapped_b, (last, "a", False, first))
        return tuple(go(outs, a_there))

    core = lax.axis_index("rollout")
    tensor = lax.axis_index("tensor")
    mine = owners == core
    a = jnp.where(mine[:, :, None, None], own_a, swap_cores(own_a))
    b = [jnp.where(mine[:, proj, None, None], x, swap_cores(x)) for proj, x in enumerate(own_b)]
    full = jnp.zeros((layers, projs, rank, n * cols), own_a.dtype)

    def put(full, piece, layer, step, from_core):
        start = place_of(n, step, from_core, tensor) * cols
        return lax.dynamic_update_slice(full, piece[None], (layer, 0, 0, start))

    first = jnp.where(core == 0, a[0], a[1])
    second = jnp.where(core == 0, a[1], a[0])
    full = put(full, first, core, 0, core)
    full = put(full, second, 1 - core, 0, core)
    for step in range(1, last + 1):
        layer = (core + step) % 2
        first = ring_pass(first, n)
        full = put(full, first, layer, step, core)
        full = put(full, swap_cores(first), 1 - layer, step, 1 - core)
        if step < last:
            second = ring_pass(second, n)
            full = put(full, second, 1 - layer, step, core)
            full = put(full, swap_cores(second), layer, step, 1 - core)
    merged = []
    for proj in range(projs):
        delta = jnp.einsum("lkr,lkc->lrc", b[proj], full[:, proj], preferred_element_type=jnp.float32)
        merged.append((bases[proj].astype(jnp.float32) + scale * delta).astype(jnp.bfloat16))
    return tuple(merged)


def solution(mesh):
    return jax.shard_map(
        functools.partial(per_device, mesh.shape["tensor"]),
        mesh=mesh,
        in_specs=(
            P("copies", None),
            P("copies", "tensor", None),
            P("copies", "tensor", None),
            P("copies", "tensor", None),
            P("rollout", "copies", None, None, "tensor"),
            P("rollout", "copies", "tensor", None),
            P("rollout", "copies", "tensor", None),
            P("rollout", "copies", "tensor", None),
        ),
        out_specs=(
            P("copies", "tensor", None),
            P("copies", "tensor", None),
            P("copies", "tensor", None),
        ),
        check_vma=False,
    )
```

```python
import functools

import jax
import jax.numpy as jnp
from jax import lax
from jax.experimental import pallas as pl
from jax.experimental.pallas import tpu as pltpu
from jax.sharding import PartitionSpec as P

numerator_gain = 16.0
LANES = 128
MIB = 1024 * 1024
TILE_ROWS = 160
TILE_COLS = 256
STORE_ROWS = 320
VMEM = pl.BlockSpec(memory_space=pltpu.VMEM)
HBM = pl.BlockSpec(memory_space=pltpu.HBM)
ANY = pl.BlockSpec(memory_space=pl.ANY)


def in_hbm(array):
    return pltpu.with_memory_space_constraint(array, pltpu.HBM)


def in_vmem(array):
    return pltpu.with_memory_space_constraint(array, pltpu.VMEM)


def ring_order(n):
    return list(range(0, n, 2)) + list(range(n - 1, 0, -2))


def ring_pass(array, n):
    order = ring_order(n)
    pairs = []
    for k in range(n):
        up, down = k % 2, 1 - k % 2
        pairs.append((up * n + order[k], (1 - up) * n + order[(k + 1) % n]))
        pairs.append((down * n + order[k], (1 - down) * n + order[(k - 1) % n]))
    return lax.ppermute(array, ("rollout", "tensor"), pairs)


def swap_cores(array):
    return lax.ppermute(array, "rollout", [(0, 1), (1, 0)])


def place_of(n, step, from_core, tensor):
    position = jnp.where(tensor % 2 == 0, tensor // 2, n - 1 - tensor // 2)
    k = position + jnp.where(from_core == position % 2, -step, step)
    k = jnp.where(k < 0, k + n, jnp.where(k >= n, k - n, k))
    return jnp.where(k < n // 2, 2 * k, 2 * n - 1 - 2 * k)


def column_starts(n, pieces, cols):
    core = lax.axis_index("rollout")
    tensor = lax.axis_index("tensor")
    blocks = []
    for step, own_ring, own_layer in pieces:
        place = place_of(n, step, core if own_ring else 1 - core, tensor)
        blocks.append((core if own_layer else 1 - core, pl.multiple_of(place * cols, LANES)))
    return blocks


def owned(owners, layer, proj, core, shape):
    return jnp.broadcast_to(owners[pl.ds(layer, 1), proj : proj + 1] == core, shape)


def choose_a_kernel(owners, own, other, first, second):
    core = lax.axis_index("rollout")
    for out, layer in ((first, core), (second, 1 - core)):
        for proj in range(own.shape[1]):
            mine = owned(owners, layer, proj, core, out.shape[1:])
            out[proj] = jnp.where(mine, own[layer, proj], other[layer, proj])


def choose_a(owners, own, other):
    piece = jax.ShapeDtypeStruct(own.shape[1:], own.dtype)
    return pl.pallas_call(
        choose_a_kernel,
        in_specs=[VMEM, VMEM, VMEM],
        out_specs=[VMEM, VMEM],
        out_shape=[piece, piece],
        compiler_params=pltpu.CompilerParams(vmem_limit_bytes=4 * MIB),
    )(in_vmem(owners), in_vmem(own), other)


def start_fetches(n, pieces, bases, blocks, sems):
    cols = blocks[0].shape[2]
    fetches = []
    for i, (layer, start) in enumerate(column_starts(n, pieces, cols)):
        for base, block in zip(bases, blocks):
            source = base.at[layer, :, pl.ds(start, cols)]
            fetches.append(pltpu.make_async_copy(source, block.at[i], sems.at[len(fetches)]))
            fetches[-1].start()
    return fetches


def block_shapes(bases, pieces, cols):
    return [jax.ShapeDtypeStruct((len(pieces), base.shape[1], cols), base.dtype) for base in bases]


def moved(shapes):
    size = sum(x.size * x.dtype.itemsize for x in shapes)
    return pl.CostEstimate(flops=0, bytes_accessed=2 * size, transcendentals=0)


def fetch_kernel(n, pieces, *refs):
    count = len(refs) // 2
    for fetch in start_fetches(n, pieces, refs[:count], refs[count:-1], refs[-1]):
        fetch.wait()


def fetch_blocks(n, cols, bases, pieces):
    blocks = block_shapes(bases, pieces, cols)
    return pl.pallas_call(
        functools.partial(fetch_kernel, n, pieces),
        in_specs=[HBM] * len(bases),
        out_specs=[VMEM] * len(bases),
        out_shape=blocks,
        scratch_shapes=[pltpu.SemaphoreType.DMA((len(bases) * len(pieces),))],
        compiler_params=pltpu.CompilerParams(vmem_limit_bytes=4 * MIB),
        cost_estimate=moved(blocks),
    )(*[in_hbm(base) for base in bases])


def merge_pieces(n, pieces, scale, b_refs, a_refs, base_of, outs, bufs, sem):
    cols = a_refs[0].shape[-1]
    for i, (layer, start) in enumerate(column_starts(n, pieces, cols)):
        for proj in (1, 2, 0):
            last_row = bufs[proj].shape[1]
            for row in range(0, last_row, TILE_ROWS):
                rows = pl.ds(row, min(TILE_ROWS, last_row - row))
                for col in range(0, cols, TILE_COLS):
                    width = min(TILE_COLS, cols - col)
                    delta = jnp.dot(
                        b_refs[proj][layer, rows],
                        a_refs[i][proj, :, col : col + width],
                        preferred_element_type=jnp.float32,
                    )
                    block = base_of(proj, i, layer, rows, start, col, width)
                    merged = block.astype(jnp.float32) + scale * delta
                    bufs[proj][i, rows, col : col + width] = merged.astype(jnp.bfloat16)
                end = min(row + TILE_ROWS, last_row)
                if end % STORE_ROWS == 0 or end == last_row:
                    begin = (end - 1) // STORE_ROWS * STORE_ROWS
                    done = pl.ds(begin, end - begin)
                    target = outs[proj].at[layer, done, pl.ds(start, cols)]
                    pltpu.make_async_copy(bufs[proj].at[i, done], target, sem.at[proj]).start()
    for proj in range(3):
        pltpu.make_async_copy(bufs[proj], bufs[proj], sem.at[proj]).wait()


def merge_own_kernel(n, pieces, scale, owners, *refs):
    own, other, blocks, a_refs = refs[0:3], refs[3:6], refs[6:9], refs[9:11]
    outs, b_refs, bufs, sem = refs[11:14], refs[14:17], refs[17:20], refs[20]
    core = lax.axis_index("rollout")
    for proj in range(3):
        for layer in range(own[proj].shape[0]):
            mine = owned(owners, layer, proj, core, own[proj].shape[1:])
            b_refs[proj][layer] = jnp.where(mine, own[proj][layer], other[proj][layer]).T

    def base_of(proj, i, layer, rows, start, col, width):
        return blocks[proj][i, rows, col : col + width]

    merge_pieces(n, pieces, scale, b_refs, a_refs, base_of, outs, bufs, sem)


def merge_kernel(n, pieces, scale, *refs):
    count = len(pieces)
    b_refs, a_refs, bases = refs[0:3], refs[3 : 3 + count], refs[3 + count : 6 + count]
    outs, bufs, sem = refs[9 + count : 12 + count], refs[12 + count : 15 + count], refs[15 + count]

    def base_of(proj, i, layer, rows, start, col, width):
        return bases[proj][layer, rows, pl.ds(pl.multiple_of(start + col, LANES), width)]

    merge_pieces(n, pieces, scale, b_refs, a_refs, base_of, outs, bufs, sem)


def merge_cost(bases, a_list):
    rank, cols = a_list[0].shape[-2:]
    cells = len(a_list) * sum(base.shape[1] for base in bases) * cols
    return pl.CostEstimate(flops=2 * cells * rank, bytes_accessed=4 * cells, transcendentals=0)


def buffers(bases, a_list):
    cols = a_list[0].shape[-1]
    return [pltpu.VMEM((len(a_list), base.shape[1], cols), base.dtype) for base in bases]


def merge_own(n, scale, owners, own, other, blocks, a_list, bases, pieces):
    chosen = [jax.ShapeDtypeStruct((x.shape[0], x.shape[2], x.shape[1]), x.dtype) for x in own]
    out = pl.pallas_call(
        functools.partial(merge_own_kernel, n, pieces, scale),
        in_specs=[VMEM] * (10 + len(a_list)),
        out_specs=[HBM] * 3 + [VMEM] * 3,
        out_shape=[jax.ShapeDtypeStruct(base.shape, base.dtype) for base in bases] + chosen,
        scratch_shapes=buffers(bases, a_list) + [pltpu.SemaphoreType.DMA((3,))],
        compiler_params=pltpu.CompilerParams(vmem_limit_bytes=16 * MIB),
        cost_estimate=merge_cost(bases, a_list),
    )(in_vmem(owners), *[in_vmem(x) for x in own], *other, *blocks, *a_list)
    return out[:3], out[3:]


def merge(n, scale, b, a_list, bases, outs, pieces):
    return pl.pallas_call(
        functools.partial(merge_kernel, n, pieces, scale),
        in_specs=[VMEM] * (3 + len(a_list) + 3) + [HBM] * 3,
        out_specs=[HBM] * 3,
        out_shape=[jax.ShapeDtypeStruct(base.shape, base.dtype) for base in bases],
        scratch_shapes=buffers(bases, a_list) + [pltpu.SemaphoreType.DMA((3,))],
        input_output_aliases={6 + len(a_list) + i: i for i in range(3)},
        compiler_params=pltpu.CompilerParams(vmem_limit_bytes=16 * MIB),
        cost_estimate=merge_cost(bases, a_list),
    )(*b, *a_list, *[in_vmem(base) for base in bases], *outs)


def per_device(
    n,
    owners,
    base_query,
    base_key,
    base_value,
    left_shared_matrix,
    right_queries_matrix,
    right_keys_matrix,
    right_values_matrix,
):
    layers, projs, rank, cols = left_shared_matrix.shape[1:]
    scale = numerator_gain / rank
    bases = (base_query, base_key, base_value)
    rights = (right_queries_matrix, right_keys_matrix, right_values_matrix)
    last = n // 2

    own_a = left_shared_matrix[0]
    own_b = [jnp.swapaxes(right[0], 1, 2) for right in rights]

    if cols % LANES == 0:
        tie = lax.optimization_barrier
        pieces = [(0, True, True), (0, True, False)]
        blocks = fetch_blocks(n, cols, bases, pieces)
        other_a, blocks = tie((swap_cores(own_a), blocks))
        first, second = choose_a(owners, own_a, other_a)
        other_b = [swap_cores(x) for x in own_b]
        held = [first, second]
        first = ring_pass(first, n)
        second = ring_pass(second, n)
        outs, b = merge_own(n, scale, owners, own_b, other_b, blocks, held, bases, pieces)
        first, outs = tie((first, outs))

        def go(outs, *named):
            pieces = [(step, not swapped, ((step % 2 == 0) == (ring == "a")) != swapped) for step, ring, swapped, _ in named]
            return merge(n, scale, b, [chunk for *_, chunk in named], bases, outs, pieces)

        swapped_a = swapped_b = late = ()
        for step in range(1, last):
            a_here = (step, "a", False, first)
            a_there = (step, "a", True, swap_cores(first))
            first = ring_pass(first, n)
            outs = go(outs, a_here, *swapped_a, *late)
            second, outs = tie((second, outs))
            b_here = (step, "b", False, second)
            b_there = (step, "b", True, swap_cores(second))
            if step < last - 1:
                second = ring_pass(second, n)
            outs = go(outs, b_here, *((*swapped_b, a_there) if step == last - 1 else ()))
            first, outs = tie((first, outs))
            swapped_a, swapped_b, late = (a_there,), (b_there,), swapped_b
        a_there = (last, "a", True, swap_cores(first))
        outs = go(outs, *swapped_b, (last, "a", False, first))
        return tuple(go(outs, a_there))

    core = lax.axis_index("rollout")
    tensor = lax.axis_index("tensor")
    mine = owners == core
    a = jnp.where(mine[:, :, None, None], own_a, swap_cores(own_a))
    b = [jnp.where(mine[:, proj, None, None], x, swap_cores(x)) for proj, x in enumerate(own_b)]
    full = jnp.zeros((layers, projs, rank, n * cols), own_a.dtype)

    def put(full, piece, layer, step, from_core):
        start = place_of(n, step, from_core, tensor) * cols
        return lax.dynamic_update_slice(full, piece[None], (layer, 0, 0, start))

    first = jnp.where(core == 0, a[0], a[1])
    second = jnp.where(core == 0, a[1], a[0])
    full = put(full, first, core, 0, core)
    full = put(full, second, 1 - core, 0, core)
    for step in range(1, last + 1):
        layer = (core + step) % 2
        first = ring_pass(first, n)
        full = put(full, first, layer, step, core)
        full = put(full, swap_cores(first), 1 - layer, step, 1 - core)
        if step < last:
            second = ring_pass(second, n)
            full = put(full, second, 1 - layer, step, core)
            full = put(full, swap_cores(second), layer, step, 1 - core)
    merged = []
    for proj in range(projs):
        delta = jnp.einsum("lkr,lkc->lrc", b[proj], full[:, proj], preferred_element_type=jnp.float32)
        merged.append((bases[proj].astype(jnp.float32) + scale * delta).astype(jnp.bfloat16))
    return tuple(merged)


def solution(mesh):
    return jax.shard_map(
        functools.partial(per_device, mesh.shape["tensor"]),
        mesh=mesh,
        in_specs=(
            P("copies", None),
            P("copies", "tensor", None),
            P("copies", "tensor", None),
            P("copies", "tensor", None),
            P("rollout", "copies", None, None, "tensor"),
            P("rollout", "copies", "tensor", None),
            P("rollout", "copies", "tensor", None),
            P("rollout", "copies", "tensor", None),
        ),
        out_specs=(
            P("copies", "tensor", None),
            P("copies", "tensor", None),
            P("copies", "tensor", None),
        ),
        check_vma=False,
    )
```

```python
import functools

import jax
import jax.numpy as jnp
from jax import lax
from jax.experimental import pallas as pl
from jax.experimental.pallas import tpu as pltpu
from jax.sharding import PartitionSpec as P

numerator_gain = 16.0
LANES = 128
MIB = 1024 * 1024
TILE_ROWS = 160
TILE_COLS = 256
STORE_ROWS = 320
VMEM = pl.BlockSpec(memory_space=pltpu.VMEM)
HBM = pl.BlockSpec(memory_space=pltpu.HBM)
ANY = pl.BlockSpec(memory_space=pl.ANY)


def in_hbm(array):
    return pltpu.with_memory_space_constraint(array, pltpu.HBM)


def in_vmem(array):
    return pltpu.with_memory_space_constraint(array, pltpu.VMEM)


def ring_order(n):
    return list(range(0, n, 2)) + list(range(n - 1, 0, -2))


def ring_pass(array, n):
    order = ring_order(n)
    pairs = []
    for k in range(n):
        up, down = k % 2, 1 - k % 2
        pairs.append((up * n + order[k], (1 - up) * n + order[(k + 1) % n]))
        pairs.append((down * n + order[k], (1 - down) * n + order[(k - 1) % n]))
    return lax.ppermute(array, ("rollout", "tensor"), pairs)


def swap_cores(array):
    return lax.ppermute(array, "rollout", [(0, 1), (1, 0)])


def place_of(n, step, from_core, tensor):
    position = jnp.where(tensor % 2 == 0, tensor // 2, n - 1 - tensor // 2)
    k = position + jnp.where(from_core == position % 2, -step, step)
    k = jnp.where(k < 0, k + n, jnp.where(k >= n, k - n, k))
    return jnp.where(k < n // 2, 2 * k, 2 * n - 1 - 2 * k)


def column_starts(n, pieces, cols):
    core = lax.axis_index("rollout")
    tensor = lax.axis_index("tensor")
    blocks = []
    for step, own_ring, own_layer in pieces:
        place = place_of(n, step, core if own_ring else 1 - core, tensor)
        blocks.append((core if own_layer else 1 - core, pl.multiple_of(place * cols, LANES)))
    return blocks


def owned(owners, layer, proj, core, shape):
    return jnp.broadcast_to(owners[pl.ds(layer, 1), proj : proj + 1] == core, shape)


def choose_a_kernel(owners, own, other, first, second):
    core = lax.axis_index("rollout")
    for out, layer in ((first, core), (second, 1 - core)):
        for proj in range(own.shape[1]):
            mine = owned(owners, layer, proj, core, out.shape[1:])
            out[proj] = jnp.where(mine, own[layer, proj], other[layer, proj])


def choose_a(owners, own, other):
    piece = jax.ShapeDtypeStruct(own.shape[1:], own.dtype)
    return pl.pallas_call(
        choose_a_kernel,
        in_specs=[VMEM, VMEM, VMEM],
        out_specs=[VMEM, VMEM],
        out_shape=[piece, piece],
        compiler_params=pltpu.CompilerParams(vmem_limit_bytes=4 * MIB),
    )(in_vmem(owners), in_vmem(own), other)


def start_fetches(n, pieces, bases, blocks, sems):
    cols = blocks[0].shape[2]
    fetches = []
    for i, (layer, start) in enumerate(column_starts(n, pieces, cols)):
        for base, block in zip(bases, blocks):
            source = base.at[layer, :, pl.ds(start, cols)]
            fetches.append(pltpu.make_async_copy(source, block.at[i], sems.at[len(fetches)]))
            fetches[-1].start()
    return fetches


def block_shapes(bases, pieces, cols):
    return [jax.ShapeDtypeStruct((len(pieces), base.shape[1], cols), base.dtype) for base in bases]


def moved(shapes):
    size = sum(x.size * x.dtype.itemsize for x in shapes)
    return pl.CostEstimate(flops=0, bytes_accessed=2 * size, transcendentals=0)


def fetch_kernel(n, pieces, *refs):
    count = len(refs) // 2
    for fetch in start_fetches(n, pieces, refs[:count], refs[count:-1], refs[-1]):
        fetch.wait()


def fetch_blocks(n, cols, bases, pieces):
    blocks = block_shapes(bases, pieces, cols)
    return pl.pallas_call(
        functools.partial(fetch_kernel, n, pieces),
        in_specs=[HBM] * len(bases),
        out_specs=[VMEM] * len(bases),
        out_shape=blocks,
        scratch_shapes=[pltpu.SemaphoreType.DMA((len(bases) * len(pieces),))],
        compiler_params=pltpu.CompilerParams(vmem_limit_bytes=4 * MIB),
        cost_estimate=moved(blocks),
    )(*[in_hbm(base) for base in bases])


def merge_pieces(n, pieces, scale, b_refs, a_refs, base_of, outs, bufs, sem):
    cols = a_refs[0].shape[-1]
    for i, (layer, start) in enumerate(column_starts(n, pieces, cols)):
        for proj in (1, 2, 0):
            last_row = bufs[proj].shape[1]
            for row in range(0, last_row, TILE_ROWS):
                rows = pl.ds(row, min(TILE_ROWS, last_row - row))
                for col in range(0, cols, TILE_COLS):
                    width = min(TILE_COLS, cols - col)
                    delta = jnp.dot(
                        b_refs[proj][layer, rows],
                        a_refs[i][proj, :, col : col + width],
                        preferred_element_type=jnp.float32,
                    )
                    block = base_of(proj, i, layer, rows, start, col, width)
                    merged = block.astype(jnp.float32) + scale * delta
                    bufs[proj][i, rows, col : col + width] = merged.astype(jnp.bfloat16)
                end = min(row + TILE_ROWS, last_row)
                if end % STORE_ROWS == 0 or end == last_row:
                    begin = (end - 1) // STORE_ROWS * STORE_ROWS
                    done = pl.ds(begin, end - begin)
                    target = outs[proj].at[layer, done, pl.ds(start, cols)]
                    pltpu.make_async_copy(bufs[proj].at[i, done], target, sem.at[proj]).start()
    for proj in range(3):
        pltpu.make_async_copy(bufs[proj], bufs[proj], sem.at[proj]).wait()


def merge_own_kernel(n, pieces, scale, owners, *refs):
    own, other, blocks, a_refs = refs[0:3], refs[3:6], refs[6:9], refs[9:11]
    outs, b_refs, bufs, sem = refs[11:14], refs[14:17], refs[17:20], refs[20]
    core = lax.axis_index("rollout")
    for proj in range(3):
        for layer in range(own[proj].shape[0]):
            mine = owned(owners, layer, proj, core, own[proj].shape[1:])
            b_refs[proj][layer] = jnp.where(mine, own[proj][layer], other[proj][layer]).T

    def base_of(proj, i, layer, rows, start, col, width):
        return blocks[proj][i, rows, col : col + width]

    merge_pieces(n, pieces, scale, b_refs, a_refs, base_of, outs, bufs, sem)


def merge_kernel(n, pieces, scale, *refs):
    count = len(pieces)
    b_refs, a_refs, bases = refs[0:3], refs[3 : 3 + count], refs[3 + count : 6 + count]
    outs, bufs, sem = refs[9 + count : 12 + count], refs[12 + count : 15 + count], refs[15 + count]

    def base_of(proj, i, layer, rows, start, col, width):
        return bases[proj][layer, rows, pl.ds(pl.multiple_of(start + col, LANES), width)]

    merge_pieces(n, pieces, scale, b_refs, a_refs, base_of, outs, bufs, sem)


def merge_cost(bases, a_list):
    rank, cols = a_list[0].shape[-2:]
    cells = len(a_list) * sum(base.shape[1] for base in bases) * cols
    return pl.CostEstimate(flops=2 * cells * rank, bytes_accessed=4 * cells, transcendentals=0)


def buffers(bases, a_list):
    cols = a_list[0].shape[-1]
    return [pltpu.VMEM((len(a_list), base.shape[1], cols), base.dtype) for base in bases]


def merge_own(n, scale, owners, own, other, blocks, a_list, bases, pieces):
    chosen = [jax.ShapeDtypeStruct((x.shape[0], x.shape[2], x.shape[1]), x.dtype) for x in own]
    out = pl.pallas_call(
        functools.partial(merge_own_kernel, n, pieces, scale),
        in_specs=[VMEM] * (10 + len(a_list)),
        out_specs=[HBM] * 3 + [VMEM] * 3,
        out_shape=[jax.ShapeDtypeStruct(base.shape, base.dtype) for base in bases] + chosen,
        scratch_shapes=buffers(bases, a_list) + [pltpu.SemaphoreType.DMA((3,))],
        compiler_params=pltpu.CompilerParams(vmem_limit_bytes=16 * MIB),
        cost_estimate=merge_cost(bases, a_list),
    )(in_vmem(owners), *[in_vmem(x) for x in own], *other, *blocks, *a_list)
    return out[:3], out[3:]


def merge(n, scale, b, a_list, bases, outs, pieces):
    return pl.pallas_call(
        functools.partial(merge_kernel, n, pieces, scale),
        in_specs=[VMEM] * (3 + len(a_list) + 3) + [HBM] * 3,
        out_specs=[HBM] * 3,
        out_shape=[jax.ShapeDtypeStruct(base.shape, base.dtype) for base in bases],
        scratch_shapes=buffers(bases, a_list) + [pltpu.SemaphoreType.DMA((3,))],
        input_output_aliases={6 + len(a_list) + i: i for i in range(3)},
        compiler_params=pltpu.CompilerParams(vmem_limit_bytes=16 * MIB),
        cost_estimate=merge_cost(bases, a_list),
    )(*b, *a_list, *[in_vmem(base) for base in bases], *outs)


def per_device(
    n,
    owners,
    base_query,
    base_key,
    base_value,
    left_shared_matrix,
    right_queries_matrix,
    right_keys_matrix,
    right_values_matrix,
):
    layers, projs, rank, cols = left_shared_matrix.shape[1:]
    scale = numerator_gain / rank
    bases = (base_query, base_key, base_value)
    rights = (right_queries_matrix, right_keys_matrix, right_values_matrix)
    last = n // 2

    own_a = left_shared_matrix[0]
    own_b = [jnp.swapaxes(right[0], 1, 2) for right in rights]

    if cols % LANES == 0:
        tie = lax.optimization_barrier
        pieces = [(0, True, True), (0, True, False)]
        blocks = fetch_blocks(n, cols, bases, pieces)
        other_a, blocks = tie((swap_cores(own_a), blocks))
        first, second = choose_a(owners, own_a, other_a)
        other_b = [swap_cores(x) for x in own_b]
        held = [first, second]
        first = ring_pass(first, n)
        second = ring_pass(second, n)
        outs, b = merge_own(n, scale, owners, own_b, other_b, blocks, held, bases, pieces)
        first, outs = tie((first, outs))

        def go(outs, *named):
            pieces = [(step, not swapped, ((step % 2 == 0) == (ring == "a")) != swapped) for step, ring, swapped, _ in named]
            return merge(n, scale, b, [chunk for *_, chunk in named], bases, outs, pieces)

        swapped = ()
        for step in range(1, last):
            a_here = (step, "a", False, first)
            a_there = (step, "a", True, swap_cores(first))
            first = ring_pass(first, n)
            if step == last - 1 and swapped:
                outs, swapped = go(outs, *swapped), ()
            second, outs = tie((second, outs))
            b_here = (step, "b", False, second)
            b_there = (step, "b", True, swap_cores(second))
            if step < last - 1:
                second = ring_pass(second, n)
            outs = go(outs, a_here, b_here, *swapped, *([a_there] if step == last - 1 else []))
            first, outs = tie((first, outs))
            swapped = (a_there, b_there)
        a_there = (last, "a", True, swap_cores(first))
        outs = go(outs, b_there, (last, "a", False, first))
        return tuple(go(outs, a_there))

    core = lax.axis_index("rollout")
    tensor = lax.axis_index("tensor")
    mine = owners == core
    a = jnp.where(mine[:, :, None, None], own_a, swap_cores(own_a))
    b = [jnp.where(mine[:, proj, None, None], x, swap_cores(x)) for proj, x in enumerate(own_b)]
    full = jnp.zeros((layers, projs, rank, n * cols), own_a.dtype)

    def put(full, piece, layer, step, from_core):
        start = place_of(n, step, from_core, tensor) * cols
        return lax.dynamic_update_slice(full, piece[None], (layer, 0, 0, start))

    first = jnp.where(core == 0, a[0], a[1])
    second = jnp.where(core == 0, a[1], a[0])
    full = put(full, first, core, 0, core)
    full = put(full, second, 1 - core, 0, core)
    for step in range(1, last + 1):
        layer = (core + step) % 2
        first = ring_pass(first, n)
        full = put(full, first, layer, step, core)
        full = put(full, swap_cores(first), 1 - layer, step, 1 - core)
        if step < last:
            second = ring_pass(second, n)
            full = put(full, second, 1 - layer, step, core)
            full = put(full, swap_cores(second), layer, step, 1 - core)
    merged = []
    for proj in range(projs):
        delta = jnp.einsum("lkr,lkc->lrc", b[proj], full[:, proj], preferred_element_type=jnp.float32)
        merged.append((bases[proj].astype(jnp.float32) + scale * delta).astype(jnp.bfloat16))
    return tuple(merged)


def solution(mesh):
    return jax.shard_map(
        functools.partial(per_device, mesh.shape["tensor"]),
        mesh=mesh,
        in_specs=(
            P("copies", None),
            P("copies", "tensor", None),
            P("copies", "tensor", None),
            P("copies", "tensor", None),
            P("rollout", "copies", None, None, "tensor"),
            P("rollout", "copies", "tensor", None),
            P("rollout", "copies", "tensor", None),
            P("rollout", "copies", "tensor", None),
        ),
        out_specs=(
            P("copies", "tensor", None),
            P("copies", "tensor", None),
            P("copies", "tensor", None),
        ),
        check_vma=False,
    )
```

```python
import functools

import jax
import jax.numpy as jnp
from jax import lax
from jax.experimental import pallas as pl
from jax.experimental.pallas import tpu as pltpu
from jax.sharding import PartitionSpec as P

numerator_gain = 16.0
LANES = 128
MIB = 1024 * 1024
TILE_ROWS = 160
TILE_COLS = 256
STORE_ROWS = 320
VMEM = pl.BlockSpec(memory_space=pltpu.VMEM)
HBM = pl.BlockSpec(memory_space=pltpu.HBM)
ANY = pl.BlockSpec(memory_space=pl.ANY)


def in_hbm(array):
    return pltpu.with_memory_space_constraint(array, pltpu.HBM)


def in_vmem(array):
    return pltpu.with_memory_space_constraint(array, pltpu.VMEM)


def ring_order(n):
    return list(range(0, n, 2)) + list(range(n - 1, 0, -2))


def ring_pass(array, n):
    order = ring_order(n)
    pairs = []
    for k in range(n):
        up, down = k % 2, 1 - k % 2
        pairs.append((up * n + order[k], (1 - up) * n + order[(k + 1) % n]))
        pairs.append((down * n + order[k], (1 - down) * n + order[(k - 1) % n]))
    return lax.ppermute(array, ("rollout", "tensor"), pairs)


def swap_cores(array):
    return lax.ppermute(array, "rollout", [(0, 1), (1, 0)])


def place_of(n, step, from_core, tensor):
    position = jnp.where(tensor % 2 == 0, tensor // 2, n - 1 - tensor // 2)
    k = position + jnp.where(from_core == position % 2, -step, step)
    k = jnp.where(k < 0, k + n, jnp.where(k >= n, k - n, k))
    return jnp.where(k < n // 2, 2 * k, 2 * n - 1 - 2 * k)


def column_starts(n, pieces, cols):
    core = lax.axis_index("rollout")
    tensor = lax.axis_index("tensor")
    blocks = []
    for step, own_ring, own_layer in pieces:
        place = place_of(n, step, core if own_ring else 1 - core, tensor)
        blocks.append((core if own_layer else 1 - core, pl.multiple_of(place * cols, LANES)))
    return blocks


def owned(owners, layer, proj, core, shape):
    return jnp.broadcast_to(owners[pl.ds(layer, 1), proj : proj + 1] == core, shape)


def choose_a_kernel(owners, own, other, first, second):
    core = lax.axis_index("rollout")
    for out, layer in ((first, core), (second, 1 - core)):
        for proj in range(own.shape[1]):
            mine = owned(owners, layer, proj, core, out.shape[1:])
            out[proj] = jnp.where(mine, own[layer, proj], other[layer, proj])


def choose_a(owners, own, other):
    piece = jax.ShapeDtypeStruct(own.shape[1:], own.dtype)
    return pl.pallas_call(
        choose_a_kernel,
        in_specs=[VMEM, VMEM, VMEM],
        out_specs=[VMEM, VMEM],
        out_shape=[piece, piece],
        compiler_params=pltpu.CompilerParams(vmem_limit_bytes=4 * MIB),
    )(in_vmem(owners), in_vmem(own), other)


def start_fetches(n, pieces, bases, blocks, sems):
    cols = blocks[0].shape[2]
    fetches = []
    for i, (layer, start) in enumerate(column_starts(n, pieces, cols)):
        for base, block in zip(bases, blocks):
            source = base.at[layer, :, pl.ds(start, cols)]
            fetches.append(pltpu.make_async_copy(source, block.at[i], sems.at[len(fetches)]))
            fetches[-1].start()
    return fetches


def block_shapes(bases, pieces, cols):
    return [jax.ShapeDtypeStruct((len(pieces), base.shape[1], cols), base.dtype) for base in bases]


def moved(shapes):
    size = sum(x.size * x.dtype.itemsize for x in shapes)
    return pl.CostEstimate(flops=0, bytes_accessed=2 * size, transcendentals=0)


def fetch_kernel(n, pieces, *refs):
    count = len(refs) // 2
    for fetch in start_fetches(n, pieces, refs[:count], refs[count:-1], refs[-1]):
        fetch.wait()


def fetch_blocks(n, cols, bases, pieces):
    blocks = block_shapes(bases, pieces, cols)
    return pl.pallas_call(
        functools.partial(fetch_kernel, n, pieces),
        in_specs=[HBM] * len(bases),
        out_specs=[VMEM] * len(bases),
        out_shape=blocks,
        scratch_shapes=[pltpu.SemaphoreType.DMA((len(bases) * len(pieces),))],
        compiler_params=pltpu.CompilerParams(vmem_limit_bytes=4 * MIB),
        cost_estimate=moved(blocks),
    )(*[in_hbm(base) for base in bases])


def merge_pieces(n, pieces, scale, b_refs, a_refs, base_of, outs, bufs, sem):
    cols = a_refs[0].shape[-1]
    for i, (layer, start) in enumerate(column_starts(n, pieces, cols)):
        for proj in (1, 2, 0):
            last_row = bufs[proj].shape[1]
            for row in range(0, last_row, TILE_ROWS):
                rows = pl.ds(row, min(TILE_ROWS, last_row - row))
                for col in range(0, cols, TILE_COLS):
                    width = min(TILE_COLS, cols - col)
                    delta = jnp.dot(
                        b_refs[proj][layer, rows],
                        a_refs[i][proj, :, col : col + width],
                        preferred_element_type=jnp.float32,
                    )
                    block = base_of(proj, i, layer, rows, start, col, width)
                    merged = block.astype(jnp.float32) + scale * delta
                    bufs[proj][i, rows, col : col + width] = merged.astype(jnp.bfloat16)
                end = min(row + TILE_ROWS, last_row)
                if end % STORE_ROWS == 0 or end == last_row:
                    begin = (end - 1) // STORE_ROWS * STORE_ROWS
                    done = pl.ds(begin, end - begin)
                    target = outs[proj].at[layer, done, pl.ds(start, cols)]
                    pltpu.make_async_copy(bufs[proj].at[i, done], target, sem.at[proj]).start()
    for proj in range(3):
        pltpu.make_async_copy(bufs[proj], bufs[proj], sem.at[proj]).wait()


def merge_own_kernel(n, pieces, scale, owners, *refs):
    own, other, blocks, a_refs = refs[0:3], refs[3:6], refs[6:9], refs[9:11]
    outs, b_refs, bufs, sem = refs[11:14], refs[14:17], refs[17:20], refs[20]
    core = lax.axis_index("rollout")
    for proj in range(3):
        for layer in range(own[proj].shape[0]):
            mine = owned(owners, layer, proj, core, own[proj].shape[1:])
            b_refs[proj][layer] = jnp.where(mine, own[proj][layer], other[proj][layer]).T

    def base_of(proj, i, layer, rows, start, col, width):
        return blocks[proj][i, rows, col : col + width]

    merge_pieces(n, pieces, scale, b_refs, a_refs, base_of, outs, bufs, sem)


def merge_kernel(n, pieces, scale, *refs):
    count = len(pieces)
    b_refs, a_refs, bases = refs[0:3], refs[3 : 3 + count], refs[3 + count : 6 + count]
    outs, bufs, sem = refs[9 + count : 12 + count], refs[12 + count : 15 + count], refs[15 + count]

    def base_of(proj, i, layer, rows, start, col, width):
        return bases[proj][layer, rows, pl.ds(pl.multiple_of(start + col, LANES), width)]

    merge_pieces(n, pieces, scale, b_refs, a_refs, base_of, outs, bufs, sem)


def merge_cost(bases, a_list):
    rank, cols = a_list[0].shape[-2:]
    cells = len(a_list) * sum(base.shape[1] for base in bases) * cols
    return pl.CostEstimate(flops=2 * cells * rank, bytes_accessed=4 * cells, transcendentals=0)


def buffers(bases, a_list):
    cols = a_list[0].shape[-1]
    return [pltpu.VMEM((len(a_list), base.shape[1], cols), base.dtype) for base in bases]


def merge_own(n, scale, owners, own, other, blocks, a_list, bases, pieces):
    chosen = [jax.ShapeDtypeStruct((x.shape[0], x.shape[2], x.shape[1]), x.dtype) for x in own]
    out = pl.pallas_call(
        functools.partial(merge_own_kernel, n, pieces, scale),
        in_specs=[VMEM] * (10 + len(a_list)),
        out_specs=[HBM] * 3 + [VMEM] * 3,
        out_shape=[jax.ShapeDtypeStruct(base.shape, base.dtype) for base in bases] + chosen,
        scratch_shapes=buffers(bases, a_list) + [pltpu.SemaphoreType.DMA((3,))],
        compiler_params=pltpu.CompilerParams(vmem_limit_bytes=16 * MIB),
        cost_estimate=merge_cost(bases, a_list),
    )(in_vmem(owners), *[in_vmem(x) for x in own], *other, *blocks, *a_list)
    return out[:3], out[3:]


def merge(n, scale, b, a_list, bases, outs, pieces):
    return pl.pallas_call(
        functools.partial(merge_kernel, n, pieces, scale),
        in_specs=[VMEM] * (3 + len(a_list) + 3) + [HBM] * 3,
        out_specs=[HBM] * 3,
        out_shape=[jax.ShapeDtypeStruct(base.shape, base.dtype) for base in bases],
        scratch_shapes=buffers(bases, a_list) + [pltpu.SemaphoreType.DMA((3,))],
        input_output_aliases={6 + len(a_list) + i: i for i in range(3)},
        compiler_params=pltpu.CompilerParams(vmem_limit_bytes=16 * MIB),
        cost_estimate=merge_cost(bases, a_list),
    )(*b, *a_list, *[in_vmem(base) for base in bases], *outs)


def per_device(
    n,
    owners,
    base_query,
    base_key,
    base_value,
    left_shared_matrix,
    right_queries_matrix,
    right_keys_matrix,
    right_values_matrix,
):
    layers, projs, rank, cols = left_shared_matrix.shape[1:]
    scale = numerator_gain / rank
    bases = (base_query, base_key, base_value)
    rights = (right_queries_matrix, right_keys_matrix, right_values_matrix)
    last = n // 2

    own_a = left_shared_matrix[0]
    own_b = [jnp.swapaxes(right[0], 1, 2) for right in rights]

    if cols % LANES == 0:
        tie = lax.optimization_barrier
        pieces = [(0, True, True), (0, True, False)]
        blocks = fetch_blocks(n, cols, bases, pieces)
        other_a, blocks = tie((swap_cores(own_a), blocks))
        first, second = choose_a(owners, own_a, other_a)
        other_b = [swap_cores(x) for x in own_b]
        held = [first, second]
        first = ring_pass(first, n)
        second = ring_pass(second, n)
        outs, b = merge_own(n, scale, owners, own_b, other_b, blocks, held, bases, pieces)
        first, outs = tie((first, outs))

        def go(outs, *named):
            pieces = [(step, not swapped, ((step % 2 == 0) == (ring == "a")) != swapped) for step, ring, swapped, _ in named]
            return merge(n, scale, b, [chunk for *_, chunk in named], bases, outs, pieces)

        swapped = ()
        for step in range(1, last):
            a_here = (step, "a", False, first)
            a_there = (step, "a", True, swap_cores(first))
            first = ring_pass(first, n)
            if step < last - 1:
                outs = go(outs, a_here)
            elif swapped:
                outs, swapped = go(outs, *swapped), ()
            second, outs = tie((second, outs))
            b_here = (step, "b", False, second)
            b_there = (step, "b", True, swap_cores(second))
            if step < last - 1:
                second = ring_pass(second, n)
            outs = go(outs, b_here, *swapped, *([a_here, a_there] if step == last - 1 else []))
            first, outs = tie((first, outs))
            swapped = (a_there, b_there)
        a_there = (last, "a", True, swap_cores(first))
        outs = go(outs, b_there, (last, "a", False, first))
        return tuple(go(outs, a_there))

    core = lax.axis_index("rollout")
    tensor = lax.axis_index("tensor")
    mine = owners == core
    a = jnp.where(mine[:, :, None, None], own_a, swap_cores(own_a))
    b = [jnp.where(mine[:, proj, None, None], x, swap_cores(x)) for proj, x in enumerate(own_b)]
    full = jnp.zeros((layers, projs, rank, n * cols), own_a.dtype)

    def put(full, piece, layer, step, from_core):
        start = place_of(n, step, from_core, tensor) * cols
        return lax.dynamic_update_slice(full, piece[None], (layer, 0, 0, start))

    first = jnp.where(core == 0, a[0], a[1])
    second = jnp.where(core == 0, a[1], a[0])
    full = put(full, first, core, 0, core)
    full = put(full, second, 1 - core, 0, core)
    for step in range(1, last + 1):
        layer = (core + step) % 2
        first = ring_pass(first, n)
        full = put(full, first, layer, step, core)
        full = put(full, swap_cores(first), 1 - layer, step, 1 - core)
        if step < last:
            second = ring_pass(second, n)
            full = put(full, second, 1 - layer, step, core)
            full = put(full, swap_cores(second), layer, step, 1 - core)
    merged = []
    for proj in range(projs):
        delta = jnp.einsum("lkr,lkc->lrc", b[proj], full[:, proj], preferred_element_type=jnp.float32)
        merged.append((bases[proj].astype(jnp.float32) + scale * delta).astype(jnp.bfloat16))
    return tuple(merged)


def solution(mesh):
    return jax.shard_map(
        functools.partial(per_device, mesh.shape["tensor"]),
        mesh=mesh,
        in_specs=(
            P("copies", None),
            P("copies", "tensor", None),
            P("copies", "tensor", None),
            P("copies", "tensor", None),
            P("rollout", "copies", None, None, "tensor"),
            P("rollout", "copies", "tensor", None),
            P("rollout", "copies", "tensor", None),
            P("rollout", "copies", "tensor", None),
        ),
        out_specs=(
            P("copies", "tensor", None),
            P("copies", "tensor", None),
            P("copies", "tensor", None),
        ),
        check_vma=False,
    )
```
